128 devices in a mesh: grp: 16 (over y, x_lo, core), tp: 8 (over x_hi, z).
Axes of the slice: x: 4 (x_hi: 2, x_lo: 2; x = x_hi * 2 + x_lo), y: 4, z: 4, core: 2. Of those that a mesh axis runs over, the one named last changes fastest.
Arguments:
- targets: int32 [256], replicated, may hold values from 0 to 31, as said below
- prompt_lens: int32 [256], replicated, may hold values from 1 to 512, 65536 in all
- prompt_kv: bfloat16 [256, 8, 512, 256], P('grp', 'tp'), may hold values from -14 to 14
- cache_pool: bfloat16 [16, 8, 224, 2, 64, 256], P('grp', 'tp'), may hold values from -14 to 14
- block_table: int32 [16, 2, 64, 6], P('grp'), may hold values from 0 to 223, as said below
- cache_lens: int32 [16, 2, 64], P('grp'), may hold values from 1 to 384
- queries: bfloat16 [16, 8, 80, 2048], P('grp', 'tp'), may hold values from -11 to 11
- new_kv: bfloat16 [16, 8, 80, 2, 256], P('grp', 'tp'), may hold values from -14 to 14
Outputs:
- context: bfloat16 [16, 8, 80, 2048], P('grp', 'tp')
- landed: bfloat16 [16, 8, 16, 2, 512, 256], P('grp', 'tp')
The draws below stay inside these ranges and needn't reach their ends.
Inputs may be any that keep to these rules, and one draw needn't show every extreme that they name: `targets`: value v sends the prompt to decode group v % 2 of serving group v // 2. Each prefill group sends exactly 2 or none of its prompts to each serving group, every serving group receives 16 prompts in all, and one decode group receives up to 16, some decode group exactly 16. `block_table`: for the rows of one decode group, the pages at entries c < ceil(cache_lens / 64) are all distinct; other entries name some page and are not read.
All inputs are finite; a program needn't handle non-finite values.
Results may differ from the reference program's by a relative error of at most 0.0019.
Values may be sent and summed in bfloat16 or wider, within the bound.
No kernel may reach another device: no remote copies, remote signals or barrier semaphores. Data moves between devices by JAX's collectives and lax.ppermute only.
A program may use at most 256 MiB of HBM per device.

```python
import math
import jax
import jax.numpy as jnp
import numpy as np
from jax import lax

KEY_VALUE_HEADS = 8
HEAD_SIZE = 128
PSRC = 16
PROMPT_TOKENS = 512
DEC = 64
PAGE = 64
MAXPG = 6
QPK = 8
KVD = 1
POOL = 224
CAPS = 2
RCAP = 16
ROWS = 80
PROMPT_TOTAL = 256
N_GRP = 16
N_TP = 8


def key_value_pairs(key, lead_shape):
    noise_part = jax.random.truncated_normal(key, -4.0, 4.0, lead_shape + (2 * HEAD_SIZE,), jnp.float32)
    shifted = noise_part[..., :HEAD_SIZE]
    return jnp.concatenate([shifted, noise_part[..., HEAD_SIZE:]], axis=-1).astype(jnp.bfloat16)


def draw_prompt_kv(key, part):
    key = jax.random.fold_in(key, 101)
    return key_value_pairs(key, (PROMPT_TOTAL, KEY_VALUE_HEADS, PROMPT_TOKENS))


def draw_cache_pool(key, part):
    key = jax.random.fold_in(key, 107)
    return key_value_pairs(key, (N_GRP, N_TP, POOL, 2 * KVD, PAGE))


def draw_new_kv(key, part):
    key = jax.random.fold_in(key, 109)
    return key_value_pairs(key, (N_GRP, N_TP, ROWS, 2 * KVD))


def draw_queries(key, part):
    lead_shape = (N_GRP, N_TP, ROWS, 2 * KVD, QPK)
    key = jax.random.fold_in(key, 103)
    aligned = jax.random.truncated_normal(key, -4.0, 4.0, lead_shape + (HEAD_SIZE,), jnp.float32)
    return aligned.reshape(N_GRP, N_TP, ROWS, 2 * KVD * QPK * HEAD_SIZE).astype(jnp.bfloat16)


def draw_targets(key, part):
    key = jax.random.fold_in(key, 113)
    offset_key, shuffle_key, count_key, full_key, priority_key = jax.random.split(key, 5)
    half_way = N_GRP // 2
    candidates = jnp.arange(N_GRP, dtype=jnp.int32)
    special = (candidates == 1) | (candidates == half_way) | (candidates == N_GRP - 1)
    scores = jnp.where(special, N_GRP + candidates, jax.random.permutation(offset_key, N_GRP).astype(jnp.int32))
    ordered = jnp.argsort(scores, stable=True).astype(jnp.int32)
    fixed_offsets = jnp.array([half_way, 1, N_GRP - 1], dtype=jnp.int32)
    offsets = jnp.concatenate([fixed_offsets, ordered[:PSRC // CAPS - 3]])
    source_keys = jax.random.split(shuffle_key, N_GRP)

    def shuffle_block(one_key):
        return jax.random.permutation(one_key, PSRC)
    shuffle = jax.vmap(shuffle_block)(source_keys)
    source_ids = jnp.arange(N_GRP, dtype=jnp.int32)[:, None]
    dest_grp = ((source_ids + offsets[shuffle // CAPS]) % N_GRP).reshape(PROMPT_TOTAL)
    counts = jax.random.randint(count_key, (N_GRP,), 0, PSRC + 1)
    full_grp = jax.random.randint(full_key, (), 0, N_GRP)
    counts = jnp.where(jnp.arange(N_GRP) == full_grp, PSRC, counts)
    priority = jax.random.permutation(priority_key, PROMPT_TOTAL)
    same_dest = dest_grp[:, None] == dest_grp[None, :]
    arrival_rank = jnp.sum(same_dest & (priority[None, :] < priority[:, None]), axis=1)
    half_id = (arrival_rank >= counts[dest_grp]).astype(jnp.int32)
    return (2 * dest_grp + half_id).astype(jnp.int32)


def page_plan(key):
    count_key, force_key, tail_key, shuffle_key = jax.random.split(key, 4)
    first_pages = jax.random.randint(count_key, (N_GRP, 2, DEC // 2), 1, MAXPG + 1)
    forced_pair = jax.random.randint(force_key, (N_GRP, 2, 1), 0, DEC // 2)
    pair_ids = jnp.arange(DEC // 2)[None, None, :]
    first_pages = jnp.where(pair_ids == forced_pair, MAXPG, first_pages)
    page_counts = jnp.stack([first_pages, MAXPG + 1 - first_pages], axis=-1).reshape(N_GRP, 2, DEC)
    tail_len = jax.random.randint(tail_key, (N_GRP, 2, DEC), 1, PAGE + 1)
    row_ids = jnp.arange(DEC)[None, None, :]
    tail_len = jnp.where(row_ids == 2 * forced_pair, PAGE, tail_len)
    lengths = (page_counts - 1) * PAGE + tail_len
    starts = jnp.cumsum(page_counts, axis=-1) - page_counts

    def shuffle_pool(one_key):
        return jax.random.permutation(one_key, POOL)
    shuffled = jax.vmap(shuffle_pool)(jax.random.split(shuffle_key, N_GRP * 2)).reshape(N_GRP, 2, POOL)
    columns = (starts[..., None] + jnp.arange(MAXPG)[None, None, None, :]) % POOL
    page_table = jnp.take_along_axis(shuffled, columns.reshape(N_GRP, 2, DEC * MAXPG), axis=2)
    return (lengths.astype(jnp.int32), page_table.reshape(N_GRP, 2, DEC, MAXPG).astype(jnp.int32))


def draw_cache_lens(key, part):
    lengths, page_table = page_plan(key)
    return lengths


def draw_block_table(key, part):
    lengths, page_table = page_plan(key)
    return page_table


def profile(number_of, total, limit, slope):
    weights = [(1 << 20) // math.isqrt(standing ** slope) + 1 for standing in range(2, number_of + 1)]
    spare, given = total - limit - (number_of - 1), [1] * (number_of - 1)
    while spare > 0:
        movable = [i for i in range(number_of - 1) if given[i] < limit]
        whole, budget = sum([weights[i] for i in movable]), spare
        for i in movable:
            more = min(limit - given[i], max(1, budget * weights[i] // whole), spare)
            given[i] = given[i] + more
            spare = spare - more
    return np.array([limit] + given)


def uneven(stream_key, count, total, reach, lean):
    if count == 2:
        one = jax.random.randint(stream_key, (), max(1, total - reach), min(reach, total - 1) + 1)
        return jnp.stack([one, total - one])
    tallies = jnp.asarray(profile(count, total, reach, lean), jnp.int32)
    couples = (count - 1) // 2
    source_of, receiver = tallies[1:1 + 2 * couples:2], tallies[2:2 + 2 * couples:2]
    slack = jnp.minimum(source_of - 1, reach - receiver)
    passed = jax.random.randint(jax.random.fold_in(stream_key, 1), (couples,), 0, 1 << 20) % (slack + 1)
    tallies = tallies.at[1:1 + 2 * couples:2].set(source_of - passed).at[2:2 + 2 * couples:2].set(receiver + passed)
    return tallies[jax.random.permutation(jax.random.fold_in(stream_key, 2), count)]


def setup_inputs(seed: int = 0) -> dict:
    splits = jax.random.split(jax.random.key(seed), 9)
    return {
        "targets": draw_targets(jax.random.fold_in(splits[8], 71), 0),
        "prompt_lens": uneven(splits[1], PROMPT_TOTAL, PROMPT_TOTAL * PROMPT_TOKENS // 2, PROMPT_TOKENS, 1).astype(jnp.int32),
        "prompt_kv": draw_prompt_kv(jax.random.fold_in(splits[8], 71), 0),
        "cache_pool": draw_cache_pool(jax.random.fold_in(splits[8], 71), 0),
        "block_table": draw_block_table(jax.random.fold_in(splits[8], 71), 0),
        "cache_lens": draw_cache_lens(jax.random.fold_in(splits[8], 71), 0),
        "queries": draw_queries(jax.random.fold_in(splits[8], 71), 0),
        "new_kv": draw_new_kv(jax.random.fold_in(splits[8], 71), 0),
    }


def earlier_matches(labels, block_len, kind_count):
    onehot = (labels[:, None] == jnp.arange(kind_count, dtype=jnp.int32)[None, :]).astype(jnp.int32)
    blocks = onehot.reshape(labels.shape[0] // block_len, block_len, kind_count)
    before = jnp.cumsum(blocks, axis=1) - blocks
    return lax.optimization_barrier(jnp.sum(before * blocks, axis=2)).reshape(labels.shape[0])

def attend(query_rows, cache_kv, lengths, own_kv):
    head_dim = query_rows.shape[-1]
    scaling = 1.0 / math.sqrt(head_dim)
    key_part = cache_kv[..., :head_dim].astype(jnp.float32)
    value_part = cache_kv[..., head_dim:].astype(jnp.float32)
    scores = jnp.einsum('rjqd,rcjmd->rjqcm', query_rows.astype(jnp.float32), key_part) * scaling
    row_count, head_count, query_count, page_count, page_span = scores.shape
    scores = scores.reshape(row_count, head_count, query_count, page_count * page_span)
    own_score = jnp.einsum('rjqd,rjd->rjq', query_rows.astype(jnp.float32), own_kv[..., :head_dim].astype(jnp.float32)) * scaling
    position = jnp.arange(page_count * page_span, dtype=jnp.int32)
    live_mask = (position[None, :] < lengths[:, None])[:, None, None, :]
    row_max = jnp.maximum(lax.optimization_barrier(jnp.max(jnp.where(live_mask, scores, -jnp.inf), axis=3)), own_score)
    weights = jnp.where(live_mask, jnp.exp(scores - row_max[..., None]), 0.0)
    own_weight = jnp.exp(own_score - row_max)
    denominator = lax.optimization_barrier(jnp.sum(weights, axis=3)) + own_weight
    rounded_length = weights.astype(jnp.bfloat16).reshape(row_count, head_count, query_count, page_count, page_span)
    mixture = jnp.einsum('rjqcm,rcjmd->rjqd', rounded_length.astype(jnp.float32), value_part)
    own_rounded = lax.optimization_barrier(own_weight.astype(jnp.bfloat16))
    mixture = mixture + own_rounded.astype(jnp.float32)[..., None] * own_kv[:, :, None, head_dim:].astype(jnp.float32)
    return (mixture / denominator[..., None]).astype(jnp.bfloat16)

def reference(targets, prompt_lens, prompt_kv, cache_pool, block_table, cache_lens, queries, new_kv):
    arrival = earlier_matches(targets, PROMPT_TOTAL, 2 * N_GRP)
    slot_ids = jnp.arange(RCAP, dtype=jnp.int32)
    prompt_ids = jnp.arange(PROMPT_TOTAL, dtype=jnp.int32)

    def one_device(device):
        group_id = device // N_TP
        member = device % N_TP
        half_id = member % 2
        pair_id = member // 2
        matches = (targets[None, :] == 2 * group_id + half_id) & (arrival[None, :] == slot_ids[:, None])
        picked = lax.optimization_barrier(jnp.sum(jnp.where(matches, prompt_ids[None, :], 0), axis=1)).astype(jnp.int32)
        length = lax.optimization_barrier(jnp.sum(jnp.where(matches, prompt_lens[None, :], 0), axis=1)).astype(jnp.int32)
        picked_rows = jnp.take(prompt_kv, picked, axis=0)
        head_rows = lax.dynamic_slice_in_dim(picked_rows, (2 * pair_id * KVD).astype(jnp.int32), 2 * KVD, 1)
        live_mask = jnp.arange(PROMPT_TOKENS, dtype=jnp.int32)[None, :] < length[:, None]
        landed_dev = jnp.where(live_mask[:, None, :, None], head_rows, jnp.zeros_like(head_rows))
        page_table = block_table[group_id, half_id]
        pool_dev = cache_pool[group_id, member]
        gathered = jnp.take(pool_dev, page_table.reshape(-1), axis=0).reshape((DEC, MAXPG) + pool_dev.shape[1:])
        queries_dev = queries[group_id, member].reshape(ROWS, 2 * KVD, QPK, HEAD_SIZE)
        own_kv = new_kv[group_id, member]
        decoded = attend(queries_dev[:DEC], gathered, cache_lens[group_id, half_id], own_kv[:DEC])
        handed = attend(queries_dev[DEC:], landed_dev[:, None], length, own_kv[DEC:])
        return (jnp.concatenate([decoded, handed], axis=0).reshape(ROWS, 2 * KVD * QPK * HEAD_SIZE), landed_dev)
    context, landed = lax.map(one_device, jnp.arange(N_GRP * N_TP, dtype=jnp.int32))
    return (context.reshape(N_GRP, N_TP, ROWS, 2 * KVD * QPK * HEAD_SIZE), landed.reshape(N_GRP, N_TP, RCAP, 2 * KVD, PROMPT_TOKENS, 2 * HEAD_SIZE))
```

```python
import functools
import math

import jax
import jax.numpy as jnp
import numpy as np
from jax import lax
from jax.experimental import pallas as pl
from jax.experimental.pallas import tpu as pltpu
from jax.sharding import PartitionSpec as P

CHUNK = 32
PROMPT_CHUNKS = 16
OWN_CHUNKS = 256
REGION = 192
BOX = 832
SPACE = 1408
C_REGION = 320
X, YA, YB, Z, CORE = 1, 2, 4, 8, 16
XY = (X, YA, X | YA)
YZ = (YB, Z, YB | Z)
KEYS_FIRST = 0
LISTS = (
    [(0, X | YA, m) for m in XY]
    + [(X | YA, YB | Z, m) for m in YZ]
    + [(0, YB | Z, m) for m in YZ]
    + [(YB | Z, X | YA, m) for m in XY]
    + [(15, CORE, CORE)]
)
LEVELS = (
    (64, 72, 64, 96, 96, 96, 80, 80, 80, 112, 112, 104, 208),
    (80, 80, 72, 104, 104, 104, 88, 96, 88, 128, 128, 120, 240),
    (104, 112, 96, 136, 144, 136, 112, 120, 112, 168, 176, 184, 304),
)
VMEM_LIMIT = 56 * 1024 * 1024


def flipped(group, mask):
    x, core, y = (group >> 1) & 1, group & 1, group >> 2
    if mask & X:
        x ^= 1
    if mask & YA:
        y ^= 1
    if mask & YB:
        y = 3 - y
    if mask & CORE:
        core ^= 1
    return (y << 2) | (x << 1) | core


def hop(value, mask):
    groups, members = lax.axis_size("grp"), lax.axis_size("tp")
    if not mask & Z:
        pairs = [(g, flipped(g, mask)) for g in range(groups)]
        return lax.ppermute(value, "grp", pairs)
    if mask == Z:
        return lax.ppermute(value, "tp", [(t, t ^ 1) for t in range(members)])
    pairs = [
        (g * members + t, flipped(g, mask) * members + (t ^ 1))
        for g in range(groups)
        for t in range(members)
    ]
    return lax.ppermute(value, ("grp", "tp"), pairs)


def node_of(group, parity):
    y = group >> 2
    return (
        ((group >> 1) & 1)
        | (((y ^ (y >> 1)) & 1) << 1)
        | (((y >> 1) & 1) << 2)
        | (parity << 3)
        | ((group & 1) << 4)
    )


def plan_kernel(where_ref, targets_ref, lens_ref, const_ref, slots_ref, core_ref, land_ref):
    me = where_ref[0]
    mine = where_ref[1]
    row_t = jnp.concatenate([targets_ref[...], targets_ref[...]], axis=1)
    row_l = jnp.concatenate([lens_ref[...], lens_ref[...]], axis=1)
    items = row_t.shape[1]
    prompts = items // 2

    def upright(row):
        down = lax.broadcasted_iota(jnp.int32, (prompts, prompts), 0)
        along = lax.broadcasted_iota(jnp.int32, (prompts, prompts), 1)
        column = jnp.sum(jnp.where(down == along, row[:, :prompts], 0), axis=1, keepdims=True)
        return jnp.concatenate([column, column], axis=0)

    def derive(targets, lens, item):
        prompt = item & (prompts - 1)
        parity = item >> 8
        start = node_of(prompt >> 4, parity)
        end = node_of(targets >> 1, targets & 1)
        chunks = (lens + (CHUNK - 1)) >> 5
        return prompt, parity, start, start ^ end, chunks

    col_t, col_l = upright(row_t), upright(row_l)
    item = lax.broadcasted_iota(jnp.int32, (items, 1), 0)
    prompt, parity, start, ways, chunks = derive(col_t, col_l, item)
    routed, phase, bits, sender = (const_ref[k : k + 1, :] for k in range(4))
    crosses = (ways & phase) == bits
    at = start ^ (ways & routed)
    lane = lax.broadcasted_iota(jnp.int32, (1, 32), 1)
    listed = crosses & (at == (me ^ sender)) & (lane < 29)
    landing = (col_t == mine) & (((lane == 30) & (parity == 0)) | ((lane == 31) & (parity == 1)))
    weight = jnp.where(listed, chunks, jnp.where(landing, 1, 0)).astype(jnp.float32)
    down = lax.broadcasted_iota(jnp.int32, (items, items), 0)
    along = lax.broadcasted_iota(jnp.int32, (items, items), 1)
    earlier = jnp.where(along < down, 1.0, 0.0).astype(jnp.bfloat16)
    place = jnp.dot(
        earlier, weight.astype(jnp.bfloat16), preferred_element_type=jnp.float32
    ).astype(jnp.int32)

    all_weight = jnp.where(crosses & (lane < 13), chunks, 0).astype(jnp.float32)
    row_item = lax.broadcasted_iota(jnp.int32, (1, items), 1)
    _, _, row_start, row_ways, _ = derive(row_t, row_l, row_item)
    nodes = lax.broadcasted_iota(jnp.int32, (32, 1), 0)
    need = jnp.zeros((1, 32), jnp.float32)
    for done in (0, X | YA, YB | Z, 15):
        present = jnp.where(nodes == (row_start ^ (row_ways & done)), 1.0, 0.0)
        held = jnp.dot(
            present.astype(jnp.bfloat16),
            all_weight.astype(jnp.bfloat16),
            preferred_element_type=jnp.float32,
        )
        need = jnp.maximum(need, jnp.max(jnp.where(routed == done, held, 0.0), axis=0, keepdims=True))
    level = jnp.zeros((1, 1), jnp.int32)
    for k in range(len(LEVELS)):
        over = (need.astype(jnp.int32) > const_ref[4 + k : 5 + k, :]) & (lane < 13)
        level += jnp.max(jnp.where(over, 1, 0), axis=1, keepdims=True)

    own = (prompt & 15) * PROMPT_CHUNKS

    def arrived(first, offset, before):
        total = jnp.zeros_like(own)
        for k in range(3):
            took = listed[:, first + k : first + k + 1]
            total += jnp.where(took, offset + REGION * k + place[:, first + k : first + k + 1], 0)
        return jnp.where((ways & before) == 0, 0, total)

    def moved(first, offset, mask, previous):
        return jnp.where((ways & mask) == 0, previous, arrived(first, offset, mask))

    keys_1 = moved(16, OWN_CHUNKS, X | YA, own)
    keys_2 = moved(19, BOX, YB | Z, keys_1)
    values_1 = moved(22, OWN_CHUNKS, YB | Z, own)
    values_2 = moved(25, BOX, X | YA, values_1)
    core = place[:, 28:29]

    def sources(k, base, count):
        slot = lax.broadcasted_iota(jnp.int32, (1, count), 1)
        first = jnp.where(listed[:, k : k + 1], place[:, k : k + 1], 1 << 20)
        offset = slot - first
        inside = (offset >= 0) & (offset < chunks)
        return jnp.sum(jnp.where(inside, offset + base, 0), axis=0, keepdims=True)

    bases = (own, keys_1, own, values_1)
    slots_ref[...] = jnp.concatenate(
        [sources(k, bases[k // 3], slots_ref.shape[1]) for k in range(12)]
        + [jnp.zeros((4, slots_ref.shape[1]), jnp.int32)],
        axis=0,
    )
    core_ref[...] = jnp.concatenate(
        [sources(12, keys_2, core_ref.shape[1]), sources(12, values_2, core_ref.shape[1])]
        + [jnp.zeros((6, core_ref.shape[1]), jnp.int32)],
        axis=0,
    )

    slot = lax.broadcasted_iota(jnp.int32, (1, 128), 1)
    rank = jnp.where(parity == 0, place[:, 30:31], place[:, 31:32])
    lands = (col_t == mine) & (rank == slot)

    def landed(value, which):
        return jnp.sum(jnp.where(lands & (parity == which), value, 0), axis=0, keepdims=True)

    crossed = (ways & CORE) >> 4
    land_ref[...] = jnp.concatenate(
        [
            landed(col_l, 0),
            landed(crossed, 0),
            landed(keys_2, 0),
            landed(keys_2, 1),
            landed(values_2, 0),
            landed(values_2, 1),
            landed(core, 0),
            landed(core, 1),
            jnp.broadcast_to(level, (1, 128)),
            jnp.zeros((7, 128), jnp.int32),
        ],
        axis=0,
    )


def plan(targets, prompt_lens, group, member):
    const = np.zeros((16, 32), np.int32)
    for k, (routed, phase, bits) in enumerate(LISTS):
        for first, sender in ((0, 0), (16, bits)):
            const[:4, first + k] = (routed, phase, bits, sender)
    const[0, 13:16] = const[0, 29:] = 64
    const[2, 13:16] = const[2, 29:] = 1
    for k, level in enumerate(LEVELS):
        const[4 + k, :13] = level
    where = jnp.stack([node_of(group, member % 2), 2 * group + member % 2]).astype(jnp.int32)
    vmem = pl.BlockSpec(memory_space=pltpu.VMEM)
    return pl.pallas_call(
        plan_kernel,
        out_shape=(
            jax.ShapeDtypeStruct((16, 256), jnp.int32),
            jax.ShapeDtypeStruct((8, 384), jnp.int32),
            jax.ShapeDtypeStruct((16, 128), jnp.int32),
        ),
        in_specs=[pl.BlockSpec(memory_space=pltpu.SMEM), vmem, vmem, vmem],
        out_specs=(vmem, vmem, vmem),
        compiler_params=pltpu.CompilerParams(vmem_limit_bytes=VMEM_LIMIT),
        name="plan",
    )(where, targets.reshape(1, -1), prompt_lens.reshape(1, -1), jnp.asarray(const))


def fetch(pairs, sems):
    copies = [
        pltpu.make_async_copy(source, target, sems.at[k]) for k, (source, target) in enumerate(pairs)
    ]
    for copy in copies:
        copy.start()
    return copies


def gather_chunks(table_ref, row, out_ref, pick):
    count = out_ref.shape[0]

    def body(s, carry):
        out_ref[s] = pick(table_ref[row, s])
        return carry

    lax.fori_loop(0, count, body, 0, unroll=8)


SMEM = pl.BlockSpec(memory_space=pltpu.SMEM)
ANY = pl.BlockSpec(memory_space=pl.ANY)
VMEM = pl.BlockSpec(memory_space=pltpu.VMEM)


def chunks_of(count, width=128):
    return jax.ShapeDtypeStruct((count, CHUNK, width), jnp.bfloat16)


def cost(bytes_accessed, flops=0):
    return pl.CostEstimate(flops=flops, bytes_accessed=bytes_accessed, transcendentals=0)


def first_kernel(table_ref, kv_ref, *rest):
    outs, space, sems = rest[:6], rest[6], rest[7]
    for copy in fetch([(kv_ref, space)], sems):
        copy.wait()
    for k in range(6):
        lanes = pl.ds(0, 128) if k < 3 else pl.ds(128, 128)
        gather_chunks(table_ref, k if k < 3 else k + 3, outs[k], lambda i: space[i, :, lanes])


def first_lists(table, kv, caps):
    sizes = caps[0:3] + caps[6:9]
    return pl.pallas_call(
        first_kernel,
        out_shape=tuple(chunks_of(c) for c in sizes),
        in_specs=[SMEM, ANY],
        out_specs=(VMEM,) * 6,
        scratch_shapes=[
            pltpu.VMEM((OWN_CHUNKS, CHUNK, 256), jnp.bfloat16),
            pltpu.SemaphoreType.DMA((1,)),
        ],
        compiler_params=pltpu.CompilerParams(vmem_limit_bytes=VMEM_LIMIT),
        cost_estimate=cost(8 << 20),
        name="first_lists",
    )(table, kv)


def second_kernel(first_row, lane, table_ref, kv_ref, *rest):
    boxes, outs, space, sems = rest[:3], rest[3:6], rest[6], rest[7]
    pairs = [(kv_ref.at[:, :, pl.ds(lane, 128)], space.at[pl.ds(0, OWN_CHUNKS)])]
    for k, box in enumerate(boxes):
        pairs.append((box, space.at[pl.ds(OWN_CHUNKS + REGION * k, box.shape[0])]))
    for copy in fetch(pairs, sems):
        copy.wait()
    for k in range(3):
        gather_chunks(table_ref, first_row + k, outs[k], lambda i: space[i])


def second_lists(table, kv, boxes, first_row, lane, caps):
    return pl.pallas_call(
        functools.partial(second_kernel, first_row, lane),
        out_shape=tuple(chunks_of(c) for c in caps[first_row : first_row + 3]),
        in_specs=[SMEM, ANY] + [ANY] * 3,
        out_specs=(VMEM,) * 3,
        scratch_shapes=[
            pltpu.VMEM((BOX, CHUNK, 128), jnp.bfloat16),
            pltpu.SemaphoreType.DMA((4,)),
        ],
        compiler_params=pltpu.CompilerParams(vmem_limit_bytes=VMEM_LIMIT),
        cost_estimate=cost(6 << 20),
        name="second_lists",
    )(table, kv, *boxes)


def gathered_space(kv_ref, boxes, spaces, sems):
    pairs = []
    for side in range(2):
        space = spaces[side]
        pairs.append((kv_ref.at[:, :, pl.ds(128 * side, 128)], space.at[pl.ds(0, OWN_CHUNKS)]))
        for k, box in enumerate(boxes[6 * side : 6 * side + 6]):
            pairs.append((box, space.at[pl.ds(OWN_CHUNKS + REGION * k, box.shape[0])]))
    return fetch(pairs, sems)


def core_kernel(table_ref, kv_ref, *rest):
    boxes, out_ref, spaces, sems = rest[:12], rest[12], rest[13:15], rest[15]
    for copy in gathered_space(kv_ref, boxes, spaces, sems):
        copy.wait()

    def body(s, carry):
        out_ref[s, :, 0:128] = spaces[0][table_ref[0, s]]
        out_ref[s, :, 128:256] = spaces[1][table_ref[1, s]]
        return carry

    lax.fori_loop(0, out_ref.shape[0], body, 0, unroll=8)


def core_list(table, kv, boxes, count):
    return pl.pallas_call(
        core_kernel,
        out_shape=chunks_of(count, 256),
        in_specs=[SMEM, ANY] + [ANY] * 12,
        out_specs=VMEM,
        scratch_shapes=[
            pltpu.VMEM((SPACE, CHUNK, 128), jnp.bfloat16),
            pltpu.VMEM((SPACE, CHUNK, 128), jnp.bfloat16),
            pltpu.SemaphoreType.DMA((14,)),
        ],
        compiler_params=pltpu.CompilerParams(vmem_limit_bytes=VMEM_LIMIT),
        cost_estimate=cost(16 << 20),
        name="core_list",
    )(table, kv, *boxes)


def attend_head(query, key, value, own, length):
    scaling = 1.0 / math.sqrt(query.shape[1])
    scores = (
        lax.dot_general(query, key, (((1,), (1,)), ((), ())), preferred_element_type=jnp.float32)
        * scaling
    )
    own_key = own[:, :128].astype(jnp.float32)
    own_value = own[:, 128:].astype(jnp.float32)
    own_score = jnp.sum(query.astype(jnp.float32) * own_key, axis=1, keepdims=True) * scaling
    live = lax.broadcasted_iota(jnp.int32, scores.shape, 1) < length
    scores = jnp.where(live, scores, -jnp.inf)
    row_max = jnp.maximum(jnp.max(scores, axis=1, keepdims=True), own_score)
    weights = jnp.where(live, jnp.exp(scores - row_max), 0.0)
    own_weight = jnp.exp(own_score - row_max)
    denominator = jnp.sum(weights, axis=1, keepdims=True) + own_weight
    mixture = jnp.dot(weights.astype(jnp.bfloat16), value, preferred_element_type=jnp.float32)
    mixture += own_weight.astype(jnp.bfloat16).astype(jnp.float32) * own_value
    return (mixture / denominator).astype(jnp.bfloat16)


DEPTH = 8


def running_kernel(half_ref, pages_ref, lens_ref, query_ref, own_ref, pool_ref, out_ref, held, sems):
    rows = query_ref.shape[0]
    max_pages = held.shape[1]
    half = half_ref[0]
    held[...] = jnp.zeros_like(held)

    def each_page(row, action):
        slot = row % DEPTH
        count = (lens_ref[half * rows + row] + 63) // 64
        for c in range(max_pages):

            @pl.when(c < count)
            def _():
                page = pages_ref[(half * rows + row) * max_pages + c]
                action(pltpu.make_async_copy(pool_ref.at[page], held.at[slot, c], sems.at[slot, c]))

    for row in range(DEPTH - 1):
        each_page(row, lambda copy: copy.start())

    def body(row, carry):
        @pl.when(row + DEPTH - 1 < rows)
        def _():
            each_page(row + DEPTH - 1, lambda copy: copy.start())

        each_page(row, lambda copy: copy.wait())
        slot = row % DEPTH
        length = lens_ref[half * rows + row]
        for pages in (2, 4, 6):

            @pl.when((length > 64 * (pages - 2)) & (length <= 64 * pages))
            def _():
                for j in range(2):
                    block = held[slot, 0:pages, j].reshape(pages * 64, 256)
                    out_ref[row, 8 * j : 8 * j + 8, :] = attend_head(
                        query_ref[row, 8 * j : 8 * j + 8, :],
                        block[:, :128],
                        block[:, 128:],
                        own_ref[row, j : j + 1, :],
                        length,
                    )

        return carry

    lax.fori_loop(0, rows, body, 0)


def running_rows(half, pages, lens, queries, own, pool):
    rows = queries.shape[0]
    max_pages = pages.shape[-1]
    return pl.pallas_call(
        running_kernel,
        out_shape=jax.ShapeDtypeStruct((rows, 16, 128), jnp.bfloat16),
        in_specs=[SMEM, SMEM, SMEM, VMEM, VMEM, ANY],
        out_specs=VMEM,
        scratch_shapes=[
            pltpu.VMEM((DEPTH, max_pages) + pool.shape[1:], jnp.bfloat16),
            pltpu.SemaphoreType.DMA((DEPTH, max_pages)),
        ],
        compiler_params=pltpu.CompilerParams(vmem_limit_bytes=VMEM_LIMIT),
        cost_estimate=cost(16 << 20, 1 << 30),
        name="running_rows",
    )(half, pages.reshape(-1), lens.reshape(-1), queries, own, pool)


def land_rows(land_ref, query_ref, own_ref, out_ref, landed_ref, block, sems, wanted, pick):
    slots = query_ref.shape[0]

    def write(slot, turn):
        return pltpu.make_async_copy(block.at[turn], landed_ref.at[slot], sems.at[turn])

    def body(slot, done):
        length = land_ref[0, slot]
        turn = done % 2
        takes = wanted(slot, length)

        @pl.when(takes & (done >= 2))
        def _():
            write(0, turn).wait()

        @pl.when(takes)
        def _():
            count = (length + (CHUNK - 1)) // CHUNK
            for j in range(2):

                def copy(k, carry):
                    key, value = pick(slot, j, k)
                    row = k * CHUNK + lax.broadcasted_iota(jnp.int32, (CHUNK, 128), 0)
                    zero = jnp.zeros((CHUNK, 128), jnp.bfloat16)
                    block[turn, j, k, :, 0:128] = jnp.where(row < length, key, zero)
                    block[turn, j, k, :, 128:256] = jnp.where(row < length, value, zero)
                    return carry

                def clear(k, carry):
                    block[turn, j, k] = jnp.zeros((CHUNK, 256), jnp.bfloat16)
                    return carry

                lax.fori_loop(0, count, copy, 0)
                lax.fori_loop(count, PROMPT_CHUNKS, clear, 0)
            write(slot, turn).start()

        for part in range(4):

            @pl.when(takes & (length > 128 * part) & (length <= 128 * (part + 1)))
            def _():
                span = 128 * (part + 1)
                for j in range(2):
                    held = block[turn, j, 0 : span // CHUNK].reshape(span, 256)
                    out_ref[slot, 8 * j : 8 * j + 8, :] = attend_head(
                        query_ref[slot, 8 * j : 8 * j + 8, :],
                        held[:, :128],
                        held[:, 128:],
                        own_ref[slot, j : j + 1, :],
                        length,
                    )

        @pl.when(takes & (length == 0))
        def _():
            for j in range(2):
                value = own_ref[slot, j : j + 1, 128:256]
                out_ref[slot, 8 * j : 8 * j + 8, :] = jnp.broadcast_to(value, (8, 128))

        return done + takes.astype(jnp.int32)

    done = lax.fori_loop(0, slots, body, 0)

    @pl.when(done >= 1)
    def _():
        write(0, (done - 1) % 2).wait()

    @pl.when(done >= 2)
    def _():
        write(0, done % 2).wait()


def near_kernel(land_ref, query_ref, own_ref, kv_ref, *rest):
    boxes, rest = rest[:12], rest[12:]
    out_ref, landed_ref, block, sems, keys, values, box_sems = rest
    out_ref[...] = jnp.zeros_like(out_ref)
    for copy in gathered_space(kv_ref, boxes, (keys, values), box_sems):
        copy.wait()

    def pick(slot, j, k):
        return keys[land_ref[2 + j, slot] + k], values[land_ref[4 + j, slot] + k]

    def wanted(slot, length):
        return land_ref[1, slot] == 0

    land_rows(land_ref, query_ref, own_ref, out_ref, landed_ref, block, sems, wanted, pick)


def near_rows(land, queries, own, kv, boxes):
    slots = queries.shape[0]
    return pl.pallas_call(
        near_kernel,
        out_shape=(
            jax.ShapeDtypeStruct((slots, 16, 128), jnp.bfloat16),
            jax.ShapeDtypeStruct((slots, 2, PROMPT_CHUNKS, CHUNK, 256), jnp.bfloat16),
        ),
        in_specs=[SMEM, VMEM, VMEM, ANY] + [ANY] * 12,
        out_specs=(VMEM, ANY),
        scratch_shapes=[
            pltpu.VMEM((2, 2, PROMPT_CHUNKS, CHUNK, 256), jnp.bfloat16),
            pltpu.SemaphoreType.DMA((2,)),
            pltpu.VMEM((SPACE, CHUNK, 128), jnp.bfloat16),
            pltpu.VMEM((SPACE, CHUNK, 128), jnp.bfloat16),
            pltpu.SemaphoreType.DMA((14,)),
        ],
        compiler_params=pltpu.CompilerParams(vmem_limit_bytes=VMEM_LIMIT),
        cost_estimate=cost(20 << 20, 1 << 28),
        name="near_rows",
    )(land, queries, own, kv, *boxes)


def far_kernel(land_ref, query_ref, own_ref, box_ref, near_ref, _, out_ref, landed_ref, block, sems, space, box_sems):
    out_ref[...] = near_ref[...]
    for copy in fetch([(box_ref, space)], box_sems):
        copy.wait()

    def pick(slot, j, k):
        chunk = space.at[land_ref[6 + j, slot] + k]
        return chunk[:, 0:128], chunk[:, 128:256]

    def wanted(slot, length):
        return land_ref[1, slot] != 0

    land_rows(land_ref, query_ref, own_ref, out_ref, landed_ref, block, sems, wanted, pick)


def far_rows(land, queries, own, box, near, landed):
    return pl.pallas_call(
        far_kernel,
        out_shape=(
            jax.ShapeDtypeStruct(near.shape, near.dtype),
            jax.ShapeDtypeStruct(landed.shape, landed.dtype),
        ),
        in_specs=[SMEM, VMEM, VMEM, ANY, VMEM, ANY],
        out_specs=(VMEM, ANY),
        input_output_aliases={5: 1},
        scratch_shapes=[
            pltpu.VMEM((2, 2, PROMPT_CHUNKS, CHUNK, 256), jnp.bfloat16),
            pltpu.SemaphoreType.DMA((2,)),
            pltpu.VMEM(box.shape, jnp.bfloat16),
            pltpu.SemaphoreType.DMA((1,)),
        ],
        compiler_params=pltpu.CompilerParams(vmem_limit_bytes=VMEM_LIMIT),
        cost_estimate=cost(12 << 20, 1 << 28),
        name="far_rows",
    )(land, queries, own, box, near, landed)


def routed(caps, slots, core, land, kv, half, pages, lens, queries, own, pool):
    running = pages.shape[1]
    lists = first_lists(slots, kv, caps)
    keys = [hop(v, m) for v, m in zip(lists[:3], XY)]
    values = [hop(v, m) for v, m in zip(lists[3:], YZ)]
    decoded = running_rows(half, pages, lens, queries[:running], own[:running], pool)
    keys += [hop(v, m) for v, m in zip(second_lists(slots, kv, keys, 3, 0, caps), YZ)]
    values += [hop(v, m) for v, m in zip(second_lists(slots, kv, values, 9, 128, caps), XY)]
    boxes = keys + values
    box = hop(core_list(core, kv, boxes, caps[12]), CORE)
    near, landed = near_rows(land, queries[running:], own[running:], kv, boxes)
    handed, landed = far_rows(land, queries[running:], own[running:], box, near, landed)
    return jnp.concatenate([decoded, handed], axis=0), landed


def earlier_matches(labels, block_len, kind_count):
    onehot = (labels[:, None] == jnp.arange(kind_count, dtype=jnp.int32)[None, :]).astype(jnp.int32)
    blocks = onehot.reshape(labels.shape[0] // block_len, block_len, kind_count)
    before = jnp.cumsum(blocks, axis=1) - blocks
    return jnp.sum(before * blocks, axis=2).reshape(labels.shape[0])


def lookup(matches):
    prompt_ids = jnp.arange(matches.shape[1], dtype=jnp.int32)
    row_index = jnp.sum(jnp.where(matches, prompt_ids[None, :], 0), axis=1)
    return (row_index, jnp.any(matches, axis=1))


def pick_rows(table_rows, row_index, is_valid):
    picked = jnp.take(table_rows, row_index, axis=0)
    mask_shape = (is_valid.shape[0],) + (1,) * (picked.ndim - 1)
    return jnp.where(is_valid.reshape(mask_shape), picked, jnp.zeros_like(picked))


def any_fill(targets, prompt_lens, land, kv, half, pages, lens, queries, own, pool):
    prompt_kv = kv.reshape(16, 1, 512, 256)
    groups = lax.axis_size("grp")
    group_id = lax.axis_index("grp")
    half_id = lax.axis_index("tp") % 2
    block_len = prompt_kv.shape[0]
    prompt_count = targets.shape[0]
    span_len = prompt_kv.shape[2]
    capacity = max(2, block_len // groups)
    source = jnp.arange(prompt_count, dtype=jnp.int32) // block_len
    arrival = earlier_matches(targets, prompt_count, 2 * groups)
    slot_ids = jnp.arange(block_len, dtype=jnp.int32)
    land_match = (targets[None, :] == 2 * group_id + half_id) & (
        arrival[None, :] == slot_ids[:, None]
    )
    land_len = jnp.sum(jnp.where(land_match, prompt_lens[None, :], 0), axis=1)
    land_live = jnp.arange(span_len, dtype=jnp.int32)[None, :] < land_len[:, None]
    land_index, land_valid = lookup(land_match)
    outgoing = source == group_id
    dest_ids = jnp.arange(groups, dtype=jnp.int32)
    cap_ids = jnp.arange(capacity, dtype=jnp.int32)
    partner = hop(prompt_kv, Z)
    pair_kv = jnp.where(
        half_id == 0,
        jnp.concatenate([prompt_kv, partner], axis=1),
        jnp.concatenate([partner, prompt_kv], axis=1),
    )
    within = earlier_matches(targets, block_len, 2 * groups)
    send_match = (
        outgoing[None, None, :]
        & (targets[None, None, :] == (2 * dest_ids + half_id)[:, None, None])
        & (within[None, None, :] == cap_ids[None, :, None])
    )
    send_index, send_valid = lookup(send_match.reshape(groups * capacity, prompt_count))
    send_index = jnp.where(send_valid, send_index - group_id * block_len, 0)
    outbox = pick_rows(pair_kv, send_index, send_valid)
    outbox = outbox.reshape((groups, capacity) + outbox.shape[1:])
    inbound = lax.all_to_all(outbox, "grp", split_axis=0, concat_axis=0, tiled=True)
    inbound = inbound.reshape((groups * capacity,) + inbound.shape[2:])
    entry_ids = source * capacity + within
    landed = pick_rows(inbound, jnp.take(entry_ids, land_index), land_valid)
    landed = jnp.where(land_live[:, None, :, None], landed, jnp.zeros_like(landed))
    running = pages.shape[1]
    decoded = running_rows(half, pages, lens, queries[:running], own[:running], pool)
    handed = jnp.stack(
        [
            jnp.concatenate(
                [
                    attend_head(
                        queries[running + s, 8 * j : 8 * j + 8],
                        landed[s, j, :, :128],
                        landed[s, j, :, 128:],
                        own[running + s, j : j + 1],
                        land_len[s],
                    )
                    for j in range(2)
                ],
                axis=0,
            )
            for s in range(block_len)
        ]
    )
    landed = landed.reshape(block_len, 2, PROMPT_CHUNKS, CHUNK, 256)
    return jnp.concatenate([decoded, handed], axis=0), landed


def local(targets, prompt_lens, prompt_kv, cache_pool, block_table, cache_lens, queries, new_kv):
    group = lax.axis_index("grp")
    member = lax.axis_index("tp")
    slots, core, land = plan(targets, prompt_lens, group, member)
    half = (member % 2).astype(jnp.int32).reshape(1)
    rows = queries.shape[2]
    shared = (
        prompt_kv.reshape(OWN_CHUNKS, CHUNK, 256),
        half,
        block_table[0],
        cache_lens[0],
        queries.reshape(rows, 16, 128),
        new_kv[0, 0],
        cache_pool[0, 0],
    )

    def at_level(caps):
        return lambda t, l, s, c, w, *rest: routed(caps, s, c, w, *rest)

    branches = [at_level(caps) for caps in LEVELS]
    branches.append(lambda t, l, s, c, w, *rest: any_fill(t, l, w, *rest))
    context, landed = lax.switch(
        land[8, 0], branches, targets, prompt_lens, slots, core, land, *shared
    )
    return (
        context.reshape(1, 1, rows, queries.shape[3]),
        landed.reshape(1, 1, 16, 2, 512, 256),
    )


def solution(mesh):
    placed = (
        P(),
        P(),
        P("grp", "tp", None, None),
        P("grp", "tp", None, None, None, None),
        P("grp", None, None, None),
        P("grp", None, None),
        P("grp", "tp", None, None),
        P("grp", "tp", None, None, None),
    )
    return jax.shard_map(
        local,
        mesh=mesh,
        in_specs=placed,
        out_specs=(P("grp", "tp", None, None), P("grp", "tp", None, None, None, None)),
        check_vma=False,
    )
```

```python
import functools
import math

import jax
import jax.numpy as jnp
import numpy as np
from jax import lax
from jax.experimental import pallas as pl
from jax.experimental.pallas import tpu as pltpu
from jax.sharding import PartitionSpec as P

CHUNK = 32
PROMPT_CHUNKS = 16
OWN_CHUNKS = 256
HOME = 512
REGION = 192
BOX = 1088
SPACE = 1664
X, YA, YB, Z, CORE = 1, 2, 4, 8, 16
XY = (X, YA, X | YA)
YZ = (YB, Z, YB | Z)
LISTS = (
    [(0, X | YA, m) for m in XY]
    + [(X | YA, YB | Z, m) for m in YZ]
    + [(0, YB | Z, m) for m in YZ]
    + [(YB | Z, X | YA, m) for m in XY]
)
LEVELS = (
    (76, 80, 72, 100, 100, 100, 88, 92, 88, 128, 132, 120),
    (84, 84, 76, 108, 108, 104, 96, 100, 96, 136, 144, 132),
    (84, 92, 84, 112, 124, 112, 100, 104, 100, 144, 152, 144),
    (104, 112, 100, 136, 144, 136, 112, 120, 112, 168, 176, 188),
)
MIB = 1024 * 1024


def flipped(group, mask):
    x, core, y = (group >> 1) & 1, group & 1, group >> 2
    if mask & X:
        x ^= 1
    if mask & YA:
        y ^= 1
    if mask & YB:
        y = 3 - y
    if mask & CORE:
        core ^= 1
    return (y << 2) | (x << 1) | core


def hop(value, mask):
    groups, members = lax.axis_size("grp"), lax.axis_size("tp")
    if not mask & Z:
        pairs = [(g, flipped(g, mask)) for g in range(groups)]
        return lax.ppermute(value, "grp", pairs)
    if mask == Z:
        return lax.ppermute(value, "tp", [(t, t ^ 1) for t in range(members)])
    pairs = [
        (g * members + t, flipped(g, mask) * members + (t ^ 1))
        for g in range(groups)
        for t in range(members)
    ]
    return lax.ppermute(value, ("grp", "tp"), pairs)


def node_of(group, parity):
    y = group >> 2
    return (
        ((group >> 1) & 1)
        | (((y ^ (y >> 1)) & 1) << 1)
        | (((y >> 1) & 1) << 2)
        | (parity << 3)
        | ((group & 1) << 4)
    )


def plan_kernel(where_ref, targets_ref, lens_ref, const_ref, slots_ref, land_ref):
    me = where_ref[0]
    mine = where_ref[1]
    row_t = jnp.concatenate([targets_ref[...], targets_ref[...]], axis=1)
    row_l = jnp.concatenate([lens_ref[...], lens_ref[...]], axis=1)
    items = row_t.shape[1]
    prompts = items // 2

    def upright(row):
        down = lax.broadcasted_iota(jnp.int32, (prompts, prompts), 0)
        along = lax.broadcasted_iota(jnp.int32, (prompts, prompts), 1)
        column = jnp.sum(jnp.where(down == along, row[:, :prompts], 0), axis=1, keepdims=True)
        return jnp.concatenate([column, column], axis=0)

    def derive(targets, lens, item):
        prompt = item & (prompts - 1)
        parity = item >> 8
        start = node_of(prompt >> 4, parity)
        end = node_of(targets >> 1, targets & 1)
        chunks = (lens + (CHUNK - 1)) >> 5
        start = (start & 15) | (end & CORE)
        return prompt, parity, start, start ^ end, chunks

    col_t, col_l = upright(row_t), upright(row_l)
    item = lax.broadcasted_iota(jnp.int32, (items, 1), 0)
    prompt, parity, start, ways, chunks = derive(col_t, col_l, item)
    routed, phase, bits, sender = (const_ref[k : k + 1, :] for k in range(4))
    crosses = (ways & phase) == bits
    at = start ^ (ways & routed)
    lane = lax.broadcasted_iota(jnp.int32, (1, 32), 1)
    listed = crosses & (at == (me ^ sender)) & (lane < 28)
    landing = (col_t == mine) & (((lane == 30) & (parity == 0)) | ((lane == 31) & (parity == 1)))
    weight = jnp.where(listed, chunks, jnp.where(landing, 1, 0)).astype(jnp.float32)
    down = lax.broadcasted_iota(jnp.int32, (items, items), 0)
    along = lax.broadcasted_iota(jnp.int32, (items, items), 1)
    earlier = jnp.where(along < down, 1.0, 0.0).astype(jnp.bfloat16)
    place = jnp.dot(
        earlier, weight.astype(jnp.bfloat16), preferred_element_type=jnp.float32
    ).astype(jnp.int32)

    all_weight = jnp.where(crosses & (lane < 12), chunks, 0).astype(jnp.float32)
    row_item = lax.broadcasted_iota(jnp.int32, (1, items), 1)
    _, _, row_start, row_ways, _ = derive(row_t, row_l, row_item)
    nodes = lax.broadcasted_iota(jnp.int32, (32, 1), 0)
    need = jnp.zeros((1, 32), jnp.float32)
    for done in (0, X | YA, YB | Z):
        present = jnp.where(nodes == (row_start ^ (row_ways & done)), 1.0, 0.0)
        held = jnp.dot(
            present.astype(jnp.bfloat16),
            all_weight.astype(jnp.bfloat16),
            preferred_element_type=jnp.float32,
        )
        need = jnp.maximum(need, jnp.max(jnp.where(routed == done, held, 0.0), axis=0, keepdims=True))
    level = jnp.zeros((1, 1), jnp.int32)
    for k in range(len(LEVELS)):
        over = (need.astype(jnp.int32) > const_ref[4 + k : 5 + k, :]) & (lane < 12)
        level += jnp.max(jnp.where(over, 1, 0), axis=1, keepdims=True)

    own = (prompt & 15) * PROMPT_CHUNKS
    own += jnp.where(((prompt >> 4) & 1) == (me >> 4), 0, OWN_CHUNKS)

    def arrived(first, offset, before):
        total = jnp.zeros_like(own)
        for k in range(3):
            took = listed[:, first + k : first + k + 1]
            total += jnp.where(took, offset + REGION * k + place[:, first + k : first + k + 1], 0)
        return jnp.where((ways & before) == 0, 0, total)

    def moved(first, offset, mask, previous):
        return jnp.where((ways & mask) == 0, previous, arrived(first, offset, mask))

    keys_1 = moved(16, HOME, X | YA, own)
    keys_2 = moved(19, BOX, YB | Z, keys_1)
    values_1 = moved(22, HOME, YB | Z, own)
    values_2 = moved(25, BOX, X | YA, values_1)

    def sources(k, base, count):
        slot = lax.broadcasted_iota(jnp.int32, (1, count), 1)
        first = jnp.where(listed[:, k : k + 1], place[:, k : k + 1], 1 << 20)
        offset = slot - first
        inside = (offset >= 0) & (offset < chunks)
        return jnp.sum(jnp.where(inside, offset + base, 0), axis=0, keepdims=True)

    bases = (own, keys_1, own, values_1)
    slots_ref[...] = jnp.concatenate(
        [sources(k, bases[k // 3], slots_ref.shape[1]) for k in range(12)]
        + [jnp.zeros((4, slots_ref.shape[1]), jnp.int32)],
        axis=0,
    )
    slot = lax.broadcasted_iota(jnp.int32, (1, 128), 1)
    rank = jnp.where(parity == 0, place[:, 30:31], place[:, 31:32])
    lands = (col_t == mine) & (rank == slot)

    def landed(value, which):
        return jnp.sum(jnp.where(lands & (parity == which), value, 0), axis=0, keepdims=True)

    land_ref[...] = jnp.concatenate(
        [
            landed(col_l, 0),
            jnp.broadcast_to(level, (1, 128)),
            landed(keys_2, 0),
            landed(keys_2, 1),
            landed(values_2, 0),
            landed(values_2, 1),
            jnp.zeros((10, 128), jnp.int32),
        ],
        axis=0,
    )


def plan(targets, prompt_lens, group, member):
    const = np.zeros((16, 32), np.int32)
    for k, (routed, phase, bits) in enumerate(LISTS):
        for first, sender in ((0, 0), (16, bits)):
            const[:4, first + k] = (routed, phase, bits, sender)
    const[0, 12:16] = const[0, 28:] = 64
    const[2, 12:16] = const[2, 28:] = 1
    for k, level in enumerate(LEVELS):
        const[4 + k, :12] = level
    where = jnp.stack([node_of(group, member % 2), 2 * group + member % 2]).astype(jnp.int32)
    vmem = pl.BlockSpec(memory_space=pltpu.VMEM)
    return pl.pallas_call(
        plan_kernel,
        out_shape=(
            jax.ShapeDtypeStruct((16, 256), jnp.int32),
            jax.ShapeDtypeStruct((16, 128), jnp.int32),
        ),
        in_specs=[pl.BlockSpec(memory_space=pltpu.SMEM), vmem, vmem, vmem],
        out_specs=(vmem, vmem),
        compiler_params=pltpu.CompilerParams(vmem_limit_bytes=24 * MIB),
        name="plan",
    )(where, targets.reshape(1, -1), prompt_lens.reshape(1, -1), jnp.asarray(const))


def fetch(pairs, sems):
    copies = [
        pltpu.make_async_copy(source, target, sems.at[k]) for k, (source, target) in enumerate(pairs)
    ]
    for copy in copies:
        copy.start()
    return copies


def gather_chunks(table_ref, row, out_ref, pick):
    batch = 4

    def body(s, carry):
        first = s * batch
        held = [pick(table_ref[row, first + b]) for b in range(batch)]
        for b in range(batch):
            out_ref[first + b] = held[b]
        return carry

    lax.fori_loop(0, out_ref.shape[0] // batch, body, 0, unroll=2)


SMEM = pl.BlockSpec(memory_space=pltpu.SMEM)
ANY = pl.BlockSpec(memory_space=pl.ANY)
VMEM = pl.BlockSpec(memory_space=pltpu.VMEM)


def chunks_of(count, width=128):
    return jax.ShapeDtypeStruct((count, CHUNK, width), jnp.bfloat16)


def cost(bytes_accessed, flops=0):
    return pl.CostEstimate(flops=flops, bytes_accessed=bytes_accessed, transcendentals=0)


def first_kernel(table_ref, kv_ref, other_ref, *rest):
    outs, space, sems = rest[:6], rest[6], rest[7]
    pairs = [
        (kv_ref, space.at[pl.ds(0, OWN_CHUNKS)]),
        (other_ref, space.at[pl.ds(OWN_CHUNKS, OWN_CHUNKS)]),
    ]
    for copy in fetch(pairs, sems):
        copy.wait()
    for k in range(6):
        lanes = pl.ds(0, 128) if k < 3 else pl.ds(128, 128)
        gather_chunks(table_ref, k if k < 3 else k + 3, outs[k], lambda i: space[i, :, lanes])


def first_lists(table, kv, other, caps):
    sizes = caps[0:3] + caps[6:9]
    return pl.pallas_call(
        first_kernel,
        out_shape=tuple(chunks_of(c) for c in sizes),
        in_specs=[SMEM, ANY, ANY],
        out_specs=(VMEM,) * 6,
        scratch_shapes=[
            pltpu.VMEM((HOME, CHUNK, 256), jnp.bfloat16),
            pltpu.SemaphoreType.DMA((2,)),
        ],
        compiler_params=pltpu.CompilerParams(vmem_limit_bytes=24 * MIB),
        cost_estimate=cost(12 << 20),
        name="first_lists",
    )(table, kv, other)


def side_pairs(side, homes, boxes, space):
    pairs = []
    for k, home in enumerate(homes):
        half = home.at[:, :, pl.ds(128 * side, 128)]
        pairs.append((half, space.at[pl.ds(OWN_CHUNKS * k, OWN_CHUNKS)]))
    for k, box in enumerate(boxes):
        pairs.append((box, space.at[pl.ds(HOME + REGION * k, box.shape[0])]))
    return pairs


def second_kernel(first_row, side, table_ref, kv_ref, other_ref, *rest):
    boxes, outs, space, sems = rest[:3], rest[3:6], rest[6], rest[7]
    for copy in fetch(side_pairs(side, (kv_ref, other_ref), boxes, space), sems):
        copy.wait()
    for k in range(3):
        gather_chunks(table_ref, first_row + k, outs[k], lambda i: space[i])


def second_lists(table, kv, other, boxes, first_row, side, caps):
    return pl.pallas_call(
        functools.partial(second_kernel, first_row, side),
        out_shape=tuple(chunks_of(c) for c in caps[first_row : first_row + 3]),
        in_specs=[SMEM, ANY, ANY] + [ANY] * 3,
        out_specs=(VMEM,) * 3,
        scratch_shapes=[
            pltpu.VMEM((BOX, CHUNK, 128), jnp.bfloat16),
            pltpu.SemaphoreType.DMA((5,)),
        ],
        compiler_params=pltpu.CompilerParams(vmem_limit_bytes=24 * MIB),
        cost_estimate=cost(10 << 20),
        name="second_lists",
    )(table, kv, other, *boxes)


def attend_row(query, first, second, own, length):
    scaling = 1.0 / math.sqrt(query.shape[1])
    upper = lax.broadcasted_iota(jnp.int32, query.shape, 0) < 8
    zero = jnp.zeros_like(query)
    wide = jnp.concatenate([jnp.where(upper, query, zero), jnp.where(upper, zero, query)], axis=1)
    keys = jnp.concatenate([first[:, :128], second[:, :128]], axis=1)
    values = jnp.concatenate([first[:, 128:], second[:, 128:]], axis=1)
    scores = (
        lax.dot_general(wide, keys, (((1,), (1,)), ((), ())), preferred_element_type=jnp.float32)
        * scaling
    )
    own = own.astype(jnp.float32)
    own_key = jnp.where(upper, own[0:1, :128], own[1:2, :128])
    own_value = jnp.where(upper, own[0:1, 128:], own[1:2, 128:])
    own_score = jnp.sum(query.astype(jnp.float32) * own_key, axis=1, keepdims=True) * scaling
    live = lax.broadcasted_iota(jnp.int32, scores.shape, 1) < length
    scores = jnp.where(live, scores, -jnp.inf)
    row_max = jnp.maximum(jnp.max(scores, axis=1, keepdims=True), own_score)
    weights = jnp.where(live, jnp.exp(scores - row_max), 0.0)
    own_weight = jnp.exp(own_score - row_max)
    denominator = jnp.sum(weights, axis=1, keepdims=True) + own_weight
    both = jnp.dot(weights.astype(jnp.bfloat16), values, preferred_element_type=jnp.float32)
    mixture = jnp.where(upper, both[:, :128], both[:, 128:])
    mixture += own_weight.astype(jnp.bfloat16).astype(jnp.float32) * own_value
    return (mixture / denominator).astype(jnp.bfloat16)


TOGETHER = 4
DEPTH = 4 * TOGETHER


def running_kernel(first, half_ref, pages_ref, lens_ref, query_ref, own_ref, pool_ref, out_ref, held, sems):
    rows = out_ref.shape[0]
    all_rows = lens_ref.shape[0] // 2
    max_pages = held.shape[1]
    start = half_ref[0] * all_rows + first
    held[...] = jnp.zeros_like(held)

    def each_page(row, action):
        slot = row % DEPTH
        count = (lens_ref[start + row] + 63) // 64
        for c in range(max_pages):

            @pl.when(c < count)
            def _():
                page = pages_ref[(start + row) * max_pages + c]
                action(pltpu.make_async_copy(pool_ref.at[page], held.at[slot, c], sems.at[slot, c]))

    def begin(group):
        for r in range(TOGETHER):
            each_page(group * TOGETHER + r, lambda copy: copy.start())

    ahead = DEPTH // TOGETHER - 1
    for group in range(ahead):
        begin(group)

    def body(group, carry):
        @pl.when(group + ahead < rows // TOGETHER)
        def _():
            begin(group + ahead)

        for r in range(TOGETHER):
            each_page(group * TOGETHER + r, lambda copy: copy.wait())
        results = []
        for r in range(TOGETHER):
            row = group * TOGETHER + r
            slot = row % DEPTH
            blocks = [held[slot, :, j].reshape(max_pages * 64, 256) for j in range(2)]
            results.append(
                attend_row(query_ref[first + row], *blocks, own_ref[first + row], lens_ref[start + row])
            )
        for r in range(TOGETHER):
            out_ref[group * TOGETHER + r] = results[r]
        return carry

    lax.fori_loop(0, rows // TOGETHER, body, 0)


def running_rows(first, count, half, pages, lens, queries, own, pool):
    max_pages = pages.shape[-1]
    return pl.pallas_call(
        functools.partial(running_kernel, first),
        out_shape=jax.ShapeDtypeStruct((count, 16, 128), jnp.bfloat16),
        in_specs=[SMEM, SMEM, SMEM, VMEM, VMEM, ANY],
        out_specs=VMEM,
        scratch_shapes=[
            pltpu.VMEM((DEPTH, max_pages) + pool.shape[1:], jnp.bfloat16),
            pltpu.SemaphoreType.DMA((DEPTH, max_pages)),
        ],
        compiler_params=pltpu.CompilerParams(vmem_limit_bytes=16 * MIB),
        cost_estimate=cost(count << 18, 1 << 28),
        name="running_rows",
    )(half, pages.reshape(-1), lens.reshape(-1), queries, own, pool)


RING = 4


def land_kernel(first, land_ref, query_ref, own_ref, kv_ref, other_ref, *rest):
    boxes, rest = rest[:12], rest[12:]
    out_ref, landed_ref, block, sems, keys, values, box_sems = rest
    slots = out_ref.shape[0]
    homes = (kv_ref, other_ref)
    pairs = side_pairs(0, homes, boxes[:6], keys) + side_pairs(1, homes, boxes[6:], values)
    for copy in fetch(pairs, box_sems):
        copy.wait()

    def write(slot):
        turn = slot % RING
        return pltpu.make_async_copy(block.at[turn], landed_ref.at[slot], sems.at[turn])

    def assemble(slot):
        turn = slot % RING
        length = land_ref[0, slot]
        count = (length + (CHUNK - 1)) // CHUNK
        for j in range(2):
            key_base, value_base = land_ref[2 + j, slot], land_ref[4 + j, slot]

            def copy(k, carry):
                held = []
                for b in range(4):
                    shift = jnp.minimum(4 * k + b, count - 1)
                    held.append((keys[key_base + shift], values[value_base + shift]))
                for b in range(4):
                    block[turn, j, 4 * k + b, :, 0:128] = held[b][0]
                    block[turn, j, 4 * k + b, :, 128:256] = held[b][1]
                return carry

            def clear(k, carry):
                block[turn, j, k] = jnp.zeros((CHUNK, 256), jnp.bfloat16)
                return carry

            lax.fori_loop(0, (count + 3) // 4, copy, 0)
            lax.fori_loop(count, PROMPT_CHUNKS, clear, 0)

            @pl.when(count > 0)
            def _():
                last = count - 1
                row = last * CHUNK + lax.broadcasted_iota(jnp.int32, (CHUNK, 256), 0)
                zero = jnp.zeros((CHUNK, 256), jnp.bfloat16)
                block[turn, j, last] = jnp.where(row < length, block[turn, j, last], zero)

    def body(pair, carry):
        both = (2 * pair, 2 * pair + 1)
        for slot in both:

            @pl.when(slot >= RING)
            def _():
                write(slot).wait()

            assemble(slot)
            write(slot).start()
        results = []
        for slot in both:
            blocks = [block[slot % RING, j].reshape(PROMPT_CHUNKS * CHUNK, 256) for j in range(2)]
            results.append(
                attend_row(query_ref[first + slot], *blocks, own_ref[first + slot], land_ref[0, slot])
            )
        for slot, result in zip(both, results):
            out_ref[slot] = result
        return carry

    lax.fori_loop(0, slots // 2, body, 0)
    for slot in range(slots - RING, slots):
        write(slot).wait()


def land_rows(first, slots, land, queries, own, kv, other, boxes):
    return pl.pallas_call(
        functools.partial(land_kernel, first),
        out_shape=(
            jax.ShapeDtypeStruct((slots, 16, 128), jnp.bfloat16),
            jax.ShapeDtypeStruct((slots, 2, PROMPT_CHUNKS, CHUNK, 256), jnp.bfloat16),
        ),
        in_specs=[SMEM, VMEM, VMEM, ANY, ANY] + [ANY] * 12,
        out_specs=(VMEM, ANY),
        scratch_shapes=[
            pltpu.VMEM((RING, 2, PROMPT_CHUNKS, CHUNK, 256), jnp.bfloat16),
            pltpu.SemaphoreType.DMA((RING,)),
            pltpu.VMEM((SPACE, CHUNK, 128), jnp.bfloat16),
            pltpu.VMEM((SPACE, CHUNK, 128), jnp.bfloat16),
            pltpu.SemaphoreType.DMA((16,)),
        ],
        compiler_params=pltpu.CompilerParams(vmem_limit_bytes=36 * MIB),
        cost_estimate=cost(20 << 20, 1 << 28),
        name="land_rows",
    )(land, queries, own, kv, other, *boxes)


def routed(caps, slots, land, kv, other, half, pages, lens, queries, own, pool):
    running = pages.shape[1]
    rows = queries.shape[0]
    queries = queries.reshape(rows, 16, 128)

    def decode(first):
        return running_rows(first, running // 2, half, pages, lens, queries, own, pool)

    kx, ka, kxa, vb, vz, vbz = first_lists(slots, kv, other, caps)
    kx, ka, kxa, vb, vz = hop(kx, X), hop(ka, YA), hop(kxa, X | YA), hop(vb, YB), hop(vz, Z)
    vbz, vb, early = lax.optimization_barrier((vbz, vb, decode(0)))
    vbz = hop(vbz, YB | Z)
    keys = [kx, ka, kxa]
    values = [vb, vz, vbz]
    kb, kz, kbz = second_lists(slots, kv, other, keys, 3, 0, caps)
    kb, kz, kbz = hop(kb, YB), hop(kz, Z), hop(kbz, YB | Z)
    vx, va, vxa = second_lists(slots, kv, other, values, 9, 1, caps)
    vx, va = hop(vx, X), hop(va, YA)
    vxa, kb, late = lax.optimization_barrier((vxa, kb, decode(running // 2)))
    vxa = hop(vxa, X | YA)
    boxes = keys + [kb, kz, kbz] + values + [vx, va, vxa]
    handed, landed = land_rows(running, rows - running, land, queries, own, kv, other, boxes)
    return join(early, late, handed), landed


def join(*contexts):
    return jnp.concatenate([c.reshape(c.shape[0], -1) for c in contexts], axis=0)


def earlier_matches(labels, block_len, kind_count):
    onehot = (labels[:, None] == jnp.arange(kind_count, dtype=jnp.int32)[None, :]).astype(jnp.int32)
    blocks = onehot.reshape(labels.shape[0] // block_len, block_len, kind_count)
    before = jnp.cumsum(blocks, axis=1) - blocks
    return jnp.sum(before * blocks, axis=2).reshape(labels.shape[0])


def lookup(matches):
    prompt_ids = jnp.arange(matches.shape[1], dtype=jnp.int32)
    row_index = jnp.sum(jnp.where(matches, prompt_ids[None, :], 0), axis=1)
    return (row_index, jnp.any(matches, axis=1))


def pick_rows(table_rows, row_index, is_valid):
    picked = jnp.take(table_rows, row_index, axis=0)
    mask_shape = (is_valid.shape[0],) + (1,) * (picked.ndim - 1)
    return jnp.where(is_valid.reshape(mask_shape), picked, jnp.zeros_like(picked))


def any_fill(targets, prompt_lens, kv, half, pages, lens, queries, own, pool):
    prompt_kv = kv.reshape(16, 1, 512, 256)
    groups = lax.axis_size("grp")
    group_id = lax.axis_index("grp")
    half_id = lax.axis_index("tp") % 2
    block_len = prompt_kv.shape[0]
    prompt_count = targets.shape[0]
    span_len = prompt_kv.shape[2]
    capacity = max(2, block_len // groups)
    source = jnp.arange(prompt_count, dtype=jnp.int32) // block_len
    arrival = earlier_matches(targets, prompt_count, 2 * groups)
    slot_ids = jnp.arange(block_len, dtype=jnp.int32)
    land_match = (targets[None, :] == 2 * group_id + half_id) & (
        arrival[None, :] == slot_ids[:, None]
    )
    land_len = jnp.sum(jnp.where(land_match, prompt_lens[None, :], 0), axis=1)
    land_live = jnp.arange(span_len, dtype=jnp.int32)[None, :] < land_len[:, None]
    land_index, land_valid = lookup(land_match)
    outgoing = source == group_id
    dest_ids = jnp.arange(groups, dtype=jnp.int32)
    cap_ids = jnp.arange(capacity, dtype=jnp.int32)
    partner = hop(prompt_kv, Z)
    pair_kv = jnp.where(
        half_id == 0,
        jnp.concatenate([prompt_kv, partner], axis=1),
        jnp.concatenate([partner, prompt_kv], axis=1),
    )
    within = earlier_matches(targets, block_len, 2 * groups)
    send_match = (
        outgoing[None, None, :]
        & (targets[None, None, :] == (2 * dest_ids + half_id)[:, None, None])
        & (within[None, None, :] == cap_ids[None, :, None])
    )
    send_index, send_valid = lookup(send_match.reshape(groups * capacity, prompt_count))
    send_index = jnp.where(send_valid, send_index - group_id * block_len, 0)
    outbox = pick_rows(pair_kv, send_index, send_valid)
    outbox = outbox.reshape((groups, capacity) + outbox.shape[1:])
    inbound = lax.all_to_all(outbox, "grp", split_axis=0, concat_axis=0, tiled=True)
    inbound = inbound.reshape((groups * capacity,) + inbound.shape[2:])
    entry_ids = source * capacity + within
    landed = pick_rows(inbound, jnp.take(entry_ids, land_index), land_valid)
    landed = jnp.where(land_live[:, None, :, None], landed, jnp.zeros_like(landed))
    running = pages.shape[1]
    queries = queries.reshape(queries.shape[0], 16, 128)
    decoded = running_rows(0, running, half, pages, lens, queries, own, pool)
    handed = jnp.stack(
        [
            attend_row(queries[running + s], landed[s, 0], landed[s, 1], own[running + s], land_len[s])
            for s in range(block_len)
        ]
    )
    landed = landed.reshape(block_len, 2, PROMPT_CHUNKS, CHUNK, 256)
    return join(decoded, handed), landed


def local(targets, prompt_lens, prompt_kv, cache_pool, block_table, cache_lens, queries, new_kv):
    group = lax.axis_index("grp")
    member = lax.axis_index("tp")
    kv = prompt_kv.reshape(OWN_CHUNKS, CHUNK, 256)
    other = hop(kv, CORE)
    slots, land = plan(targets, prompt_lens, group, member)
    half = (member % 2).astype(jnp.int32).reshape(1)
    rows = queries.shape[2]
    shared = (
        half,
        block_table[0],
        cache_lens[0],
        queries.reshape(rows, -1),
        new_kv[0, 0],
        cache_pool[0, 0],
    )

    def at_level(caps):
        return lambda t, l, s, w, k, o, *rest: routed(caps, s, w, k, o, *rest)

    branches = [at_level(caps) for caps in LEVELS]
    branches.append(lambda t, l, s, w, k, o, *rest: any_fill(t, l, k, *rest))
    context, landed = lax.switch(
        land[1, 0], branches, targets, prompt_lens, slots, land, kv, other, *shared
    )
    return (
        context.reshape(1, 1, rows, queries.shape[3]),
        landed.reshape(1, 1, 16, 2, 512, 256),
    )


def solution(mesh):
    placed = (
        P(),
        P(),
        P("grp", "tp", None, None),
        P("grp", "tp", None, None, None, None),
        P("grp", None, None, None),
        P("grp", None, None),
        P("grp", "tp", None, None),
        P("grp", "tp", None, None, None),
    )
    return jax.shard_map(
        local,
        mesh=mesh,
        in_specs=placed,
        out_specs=(P("grp", "tp", None, None), P("grp", "tp", None, None, None, None)),
        check_vma=False,
    )
```

```python
import functools
import math

import jax
import jax.numpy as jnp
import numpy as np
from jax import lax
from jax.experimental import pallas as pl
from jax.experimental.pallas import tpu as pltpu
from jax.sharding import PartitionSpec as P

CHUNK = 32
PROMPT_CHUNKS = 16
OWN_CHUNKS = 256
HOME = 512
REGION = 192
BOX = 1088
SPACE = 1664
X, YA, YB, Z, CORE = 1, 2, 4, 8, 16
XY = (X, YA, X | YA)
YZ = (YB, Z, YB | Z)
LISTS = (
    [(0, X | YA, m) for m in XY]
    + [(X | YA, YB | Z, m) for m in YZ]
    + [(0, YB | Z, m) for m in YZ]
    + [(YB | Z, X | YA, m) for m in XY]
)
LEVELS = (
    (76, 80, 72, 100, 100, 100, 88, 92, 88, 128, 132, 120),
    (84, 84, 76, 108, 108, 104, 96, 100, 96, 136, 144, 132),
    (84, 92, 84, 112, 124, 112, 100, 104, 100, 144, 152, 144),
    (104, 112, 100, 136, 144, 136, 112, 120, 112, 168, 176, 188),
)
MIB = 1024 * 1024
SMALL = 4096


def flipped(group, mask):
    x, core, y = (group >> 1) & 1, group & 1, group >> 2
    if mask & X:
        x ^= 1
    if mask & YA:
        y ^= 1
    if mask & YB:
        y = 3 - y
    if mask & CORE:
        core ^= 1
    return (y << 2) | (x << 1) | core


def hop(value, mask):
    groups, members = lax.axis_size("grp"), lax.axis_size("tp")
    if not mask & Z:
        pairs = [(g, flipped(g, mask)) for g in range(groups)]
        return lax.ppermute(value, "grp", pairs)
    if mask == Z:
        return lax.ppermute(value, "tp", [(t, t ^ 1) for t in range(members)])
    pairs = [
        (g * members + t, flipped(g, mask) * members + (t ^ 1))
        for g in range(groups)
        for t in range(members)
    ]
    return lax.ppermute(value, ("grp", "tp"), pairs)


def node_of(group, parity):
    y = group >> 2
    return (
        ((group >> 1) & 1)
        | (((y ^ (y >> 1)) & 1) << 1)
        | (((y >> 1) & 1) << 2)
        | (parity << 3)
        | ((group & 1) << 4)
    )


def plan_kernel(where_ref, targets_ref, lens_ref, const_ref, slots_ref, land_ref):
    me = where_ref[0]
    mine = where_ref[1]
    row_t = jnp.concatenate([targets_ref[...], targets_ref[...]], axis=1)
    row_l = jnp.concatenate([lens_ref[...], lens_ref[...]], axis=1)
    items = row_t.shape[1]
    prompts = items // 2

    def upright(row):
        down = lax.broadcasted_iota(jnp.int32, (prompts, prompts), 0)
        along = lax.broadcasted_iota(jnp.int32, (prompts, prompts), 1)
        column = jnp.sum(jnp.where(down == along, row[:, :prompts], 0), axis=1, keepdims=True)
        return jnp.concatenate([column, column], axis=0)

    def derive(targets, lens, item):
        prompt = item & (prompts - 1)
        parity = item >> 8
        start = node_of(prompt >> 4, parity)
        end = node_of(targets >> 1, targets & 1)
        chunks = (lens + (CHUNK - 1)) >> 5
        start = (start & 15) | (end & CORE)
        return prompt, parity, start, start ^ end, chunks

    col_t, col_l = upright(row_t), upright(row_l)
    item = lax.broadcasted_iota(jnp.int32, (items, 1), 0)
    prompt, parity, start, ways, chunks = derive(col_t, col_l, item)
    routed, phase, bits, sender = (const_ref[k : k + 1, :] for k in range(4))
    crosses = (ways & phase) == bits
    at = start ^ (ways & routed)
    lane = lax.broadcasted_iota(jnp.int32, (1, 32), 1)
    listed = crosses & (at == (me ^ sender)) & (lane < 28)
    landing = (col_t == mine) & (((lane == 30) & (parity == 0)) | ((lane == 31) & (parity == 1)))
    weight = jnp.where(listed, chunks, jnp.where(landing, 1, 0)).astype(jnp.float32)
    down = lax.broadcasted_iota(jnp.int32, (items, items), 0)
    along = lax.broadcasted_iota(jnp.int32, (items, items), 1)
    earlier = jnp.where(along < down, 1.0, 0.0).astype(jnp.bfloat16)
    place = jnp.dot(
        earlier, weight.astype(jnp.bfloat16), preferred_element_type=jnp.float32
    ).astype(jnp.int32)

    all_weight = jnp.where(crosses & (lane < 12), chunks, 0).astype(jnp.float32)
    row_item = lax.broadcasted_iota(jnp.int32, (1, items), 1)
    _, _, row_start, row_ways, _ = derive(row_t, row_l, row_item)
    nodes = lax.broadcasted_iota(jnp.int32, (32, 1), 0)
    need = jnp.zeros((1, 32), jnp.float32)
    for done in (0, X | YA, YB | Z):
        present = jnp.where(nodes == (row_start ^ (row_ways & done)), 1.0, 0.0)
        held = jnp.dot(
            present.astype(jnp.bfloat16),
            all_weight.astype(jnp.bfloat16),
            preferred_element_type=jnp.float32,
        )
        need = jnp.maximum(need, jnp.max(jnp.where(routed == done, held, 0.0), axis=0, keepdims=True))
    level = jnp.zeros((1, 1), jnp.int32)
    for k in range(len(LEVELS)):
        over = (need.astype(jnp.int32) > const_ref[4 + k : 5 + k, :]) & (lane < 12)
        level += jnp.max(jnp.where(over, 1, 0), axis=1, keepdims=True)

    own = (prompt & 15) * PROMPT_CHUNKS
    own += jnp.where(((prompt >> 4) & 1) == (me >> 4), 0, OWN_CHUNKS)

    def arrived(first, offset, before):
        total = jnp.zeros_like(own)
        for k in range(3):
            took = listed[:, first + k : first + k + 1]
            total += jnp.where(took, offset + REGION * k + place[:, first + k : first + k + 1], 0)
        return jnp.where((ways & before) == 0, 0, total)

    def moved(first, offset, mask, previous):
        return jnp.where((ways & mask) == 0, previous, arrived(first, offset, mask))

    keys_1 = moved(16, HOME, X | YA, own)
    keys_2 = moved(19, BOX, YB | Z, keys_1)
    values_1 = moved(22, HOME, YB | Z, own)
    values_2 = moved(25, BOX, X | YA, values_1)

    def sources(k, base, count):
        slot = lax.broadcasted_iota(jnp.int32, (1, count), 1)
        first = jnp.where(listed[:, k : k + 1], place[:, k : k + 1], 1 << 20)
        offset = slot - first
        inside = (offset >= 0) & (offset < chunks)
        return jnp.sum(jnp.where(inside, offset + base, 0), axis=0, keepdims=True)

    bases = (own, keys_1, own, values_1)
    slots_ref[...] = jnp.concatenate(
        [sources(k, bases[k // 3], slots_ref.shape[1]) for k in range(12)]
        + [jnp.zeros((4, slots_ref.shape[1]), jnp.int32)],
        axis=0,
    )
    slot = lax.broadcasted_iota(jnp.int32, (1, 128), 1)
    rank = jnp.where(parity == 0, place[:, 30:31], place[:, 31:32])
    lands = (col_t == mine) & (rank == slot)

    def landed(value, which):
        return jnp.sum(jnp.where(lands & (parity == which), value, 0), axis=0, keepdims=True)

    land_ref[...] = jnp.concatenate(
        [
            landed(col_l, 0),
            jnp.broadcast_to(level, (1, 128)),
            landed(keys_2, 0),
            landed(keys_2, 1),
            landed(values_2, 0),
            landed(values_2, 1),
            jnp.zeros((10, 128), jnp.int32),
        ],
        axis=0,
    )


def plan(targets, prompt_lens, group, member):
    const = np.zeros((16, 32), np.int32)
    for k, (routed, phase, bits) in enumerate(LISTS):
        for first, sender in ((0, 0), (16, bits)):
            const[:4, first + k] = (routed, phase, bits, sender)
    const[0, 12:16] = const[0, 28:] = 64
    const[2, 12:16] = const[2, 28:] = 1
    for k, level in enumerate(LEVELS):
        const[4 + k, :12] = level
    where = jnp.stack([node_of(group, member % 2), 2 * group + member % 2]).astype(jnp.int32)
    vmem = pl.BlockSpec(memory_space=pltpu.VMEM)
    return pl.pallas_call(
        plan_kernel,
        out_shape=(
            jax.ShapeDtypeStruct((16, 256), jnp.int32),
            jax.ShapeDtypeStruct((16, 128), jnp.int32),
        ),
        in_specs=[pl.BlockSpec(memory_space=pltpu.SMEM), vmem, vmem, vmem],
        out_specs=(vmem, vmem),
        compiler_params=pltpu.CompilerParams(vmem_limit_bytes=24 * MIB),
        name="plan",
    )(where, targets.reshape(1, -1), prompt_lens.reshape(1, -1), jnp.asarray(const))


def fetch(pairs, sems):
    copies = [
        pltpu.make_async_copy(source, target, sems.at[k]) for k, (source, target) in enumerate(pairs)
    ]
    for copy in copies:
        copy.start()
    return copies


def gather_chunks(table_ref, row, out_ref, pick):
    batch = 4

    def body(s, carry):
        first = s * batch
        held = [pick(table_ref[row, first + b]) for b in range(batch)]
        for b in range(batch):
            out_ref[first + b] = held[b]
        return carry

    lax.fori_loop(0, out_ref.shape[0] // batch, body, 0, unroll=2)


SMEM = pl.BlockSpec(memory_space=pltpu.SMEM)
ANY = pl.BlockSpec(memory_space=pl.ANY)
VMEM = pl.BlockSpec(memory_space=pltpu.VMEM)


def chunks_of(count, width=128):
    return jax.ShapeDtypeStruct((count, CHUNK, width), jnp.bfloat16)


def cost(bytes_accessed, flops=0):
    return pl.CostEstimate(flops=flops, bytes_accessed=bytes_accessed, transcendentals=0)


def side_pairs(side, homes, boxes, space):
    pairs = []
    for k, home in enumerate(homes):
        half = home.at[:, :, pl.ds(128 * side, 128)]
        pairs.append((half, space.at[pl.ds(OWN_CHUNKS * k, OWN_CHUNKS)]))
    for k, box in enumerate(boxes):
        pairs.append((box, space.at[pl.ds(HOME + REGION * k, box.shape[0])]))
    return pairs


def pack_kernel(first_row, side, given, table_ref, kv_ref, other_ref, *rest):
    boxes, outs, space, sems = rest[:given], rest[given : given + 3], rest[given + 3], rest[given + 4]
    for copy in fetch(side_pairs(side, (kv_ref, other_ref), boxes, space), sems):
        copy.wait()
    for k in range(3):
        gather_chunks(table_ref, first_row + k, outs[k], lambda i: space[i])


def pack_lists(table, kv, other, boxes, first_row, side, caps):
    given = len(boxes)
    return pl.pallas_call(
        functools.partial(pack_kernel, first_row, side, given),
        out_shape=tuple(chunks_of(c) for c in caps[first_row : first_row + 3]),
        in_specs=[SMEM, ANY, ANY] + [ANY] * given,
        out_specs=(VMEM,) * 3,
        scratch_shapes=[
            pltpu.VMEM((BOX if given else HOME, CHUNK, 128), jnp.bfloat16),
            pltpu.SemaphoreType.DMA((2 + given,)),
        ],
        compiler_params=pltpu.CompilerParams(vmem_limit_bytes=24 * MIB),
        cost_estimate=cost(SMALL),
        name="pack_lists",
    )(table, kv, other, *boxes)


def attend_row(query, first, second, own, length):
    scaling = 1.0 / math.sqrt(query.shape[1])
    upper = lax.broadcasted_iota(jnp.int32, query.shape, 0) < 8
    zero = jnp.zeros_like(query)
    wide = jnp.concatenate([jnp.where(upper, query, zero), jnp.where(upper, zero, query)], axis=1)
    keys = jnp.concatenate([first[:, :128], second[:, :128]], axis=1)
    values = jnp.concatenate([first[:, 128:], second[:, 128:]], axis=1)
    scores = (
        lax.dot_general(wide, keys, (((1,), (1,)), ((), ())), preferred_element_type=jnp.float32)
        * scaling
    )
    own = own.astype(jnp.float32)
    own_key = jnp.where(upper, own[0:1, :128], own[1:2, :128])
    own_value = jnp.where(upper, own[0:1, 128:], own[1:2, 128:])
    own_score = jnp.sum(query.astype(jnp.float32) * own_key, axis=1, keepdims=True) * scaling
    live = lax.broadcasted_iota(jnp.int32, scores.shape, 1) < length
    scores = jnp.where(live, scores, -jnp.inf)
    row_max = jnp.maximum(jnp.max(scores, axis=1, keepdims=True), own_score)
    weights = jnp.where(live, jnp.exp(scores - row_max), 0.0)
    own_weight = jnp.exp(own_score - row_max)
    denominator = jnp.sum(weights, axis=1, keepdims=True) + own_weight
    both = jnp.dot(weights.astype(jnp.bfloat16), values, preferred_element_type=jnp.float32)
    mixture = jnp.where(upper, both[:, :128], both[:, 128:])
    mixture += own_weight.astype(jnp.bfloat16).astype(jnp.float32) * own_value
    return (mixture / denominator).astype(jnp.bfloat16)


TOGETHER = 4
DEPTH = 4 * TOGETHER


def running_kernel(first, half_ref, pages_ref, lens_ref, query_ref, own_ref, pool_ref, out_ref, held, sems):
    rows = out_ref.shape[0]
    all_rows = lens_ref.shape[0] // 2
    max_pages = held.shape[1]
    start = half_ref[0] * all_rows + first
    held[...] = jnp.zeros_like(held)

    def each_page(row, action):
        slot = row % DEPTH
        count = (lens_ref[start + row] + 63) // 64
        for c in range(max_pages):

            @pl.when(c < count)
            def _():
                page = pages_ref[(start + row) * max_pages + c]
                action(pltpu.make_async_copy(pool_ref.at[page], held.at[slot, c], sems.at[slot, c]))

    def begin(group):
        for r in range(TOGETHER):
            each_page(group * TOGETHER + r, lambda copy: copy.start())

    ahead = DEPTH // TOGETHER - 1
    for group in range(ahead):
        begin(group)

    def body(group, carry):
        @pl.when(group + ahead < rows // TOGETHER)
        def _():
            begin(group + ahead)

        for r in range(TOGETHER):
            each_page(group * TOGETHER + r, lambda copy: copy.wait())
        results = []
        for r in range(TOGETHER):
            row = group * TOGETHER + r
            slot = row % DEPTH
            blocks = [held[slot, :, j].reshape(max_pages * 64, 256) for j in range(2)]
            results.append(
                attend_row(query_ref[first + row], *blocks, own_ref[first + row], lens_ref[start + row])
            )
        for r in range(TOGETHER):
            out_ref[group * TOGETHER + r] = results[r]
        return carry

    lax.fori_loop(0, rows // TOGETHER, body, 0)


def running_rows(first, count, half, pages, lens, queries, own, pool):
    max_pages = pages.shape[-1]
    return pl.pallas_call(
        functools.partial(running_kernel, first),
        out_shape=jax.ShapeDtypeStruct((count, 16, 128), jnp.bfloat16),
        in_specs=[SMEM, SMEM, SMEM, VMEM, VMEM, pl.BlockSpec(memory_space=pltpu.HBM)],
        out_specs=VMEM,
        scratch_shapes=[
            pltpu.VMEM((DEPTH, max_pages) + pool.shape[1:], jnp.bfloat16),
            pltpu.SemaphoreType.DMA((DEPTH, max_pages)),
        ],
        compiler_params=pltpu.CompilerParams(vmem_limit_bytes=16 * MIB),
        cost_estimate=cost(SMALL),
        name="running_rows",
    )(half, pages.reshape(-1), lens.reshape(-1), queries, own, pool)


RING = 4


def land_kernel(first, land_ref, query_ref, own_ref, kv_ref, other_ref, *rest):
    boxes, rest = rest[:12], rest[12:]
    out_ref, landed_ref, block, sems, keys, values, box_sems = rest
    slots = out_ref.shape[0]
    homes = (kv_ref, other_ref)
    pairs = side_pairs(0, homes, boxes[:6], keys) + side_pairs(1, homes, boxes[6:], values)
    for copy in fetch(pairs, box_sems):
        copy.wait()

    def write(slot):
        turn = slot % RING
        return pltpu.make_async_copy(block.at[turn], landed_ref.at[slot], sems.at[turn])

    def assemble(slot):
        turn = slot % RING
        length = land_ref[0, slot]
        count = (length + (CHUNK - 1)) // CHUNK
        for j in range(2):
            key_base, value_base = land_ref[2 + j, slot], land_ref[4 + j, slot]

            def copy(k, carry):
                held = []
                for b in range(4):
                    shift = jnp.minimum(4 * k + b, count - 1)
                    held.append((keys[key_base + shift], values[value_base + shift]))
                for b in range(4):
                    block[turn, j, 4 * k + b, :, 0:128] = held[b][0]
                    block[turn, j, 4 * k + b, :, 128:256] = held[b][1]
                return carry

            def clear(k, carry):
                block[turn, j, k] = jnp.zeros((CHUNK, 256), jnp.bfloat16)
                return carry

            lax.fori_loop(0, (count + 3) // 4, copy, 0)
            lax.fori_loop(count, PROMPT_CHUNKS, clear, 0)

            @pl.when(count > 0)
            def _():
                last = count - 1
                row = last * CHUNK + lax.broadcasted_iota(jnp.int32, (CHUNK, 256), 0)
                zero = jnp.zeros((CHUNK, 256), jnp.bfloat16)
                block[turn, j, last] = jnp.where(row < length, block[turn, j, last], zero)

    def body(pair, carry):
        both = (2 * pair, 2 * pair + 1)
        for slot in both:

            @pl.when(slot >= RING)
            def _():
                write(slot).wait()

            assemble(slot)
            write(slot).start()
        results = []
        for slot in both:
            blocks = [block[slot % RING, j].reshape(PROMPT_CHUNKS * CHUNK, 256) for j in range(2)]
            results.append(
                attend_row(query_ref[first + slot], *blocks, own_ref[first + slot], land_ref[0, slot])
            )
        for slot, result in zip(both, results):
            out_ref[slot] = result
        return carry

    lax.fori_loop(0, slots // 2, body, 0)
    for slot in range(slots - RING, slots):
        write(slot).wait()


def land_rows(first, slots, land, queries, own, kv, other, boxes):
    return pl.pallas_call(
        functools.partial(land_kernel, first),
        out_shape=(
            jax.ShapeDtypeStruct((slots, 16, 128), jnp.bfloat16),
            jax.ShapeDtypeStruct((slots, 2, PROMPT_CHUNKS, CHUNK, 256), jnp.bfloat16),
        ),
        in_specs=[SMEM, VMEM, VMEM, ANY, ANY] + [ANY] * 12,
        out_specs=(VMEM, ANY),
        scratch_shapes=[
            pltpu.VMEM((RING, 2, PROMPT_CHUNKS, CHUNK, 256), jnp.bfloat16),
            pltpu.SemaphoreType.DMA((RING,)),
            pltpu.VMEM((SPACE, CHUNK, 128), jnp.bfloat16),
            pltpu.VMEM((SPACE, CHUNK, 128), jnp.bfloat16),
            pltpu.SemaphoreType.DMA((16,)),
        ],
        compiler_params=pltpu.CompilerParams(vmem_limit_bytes=36 * MIB),
        cost_estimate=cost(SMALL),
        name="land_rows",
    )(land, queries, own, kv, other, *boxes)


def routed(caps, slots, land, kv, other, half, pages, lens, queries, own, pool):
    running = pages.shape[1]
    rows = queries.shape[0]
    queries = queries.reshape(rows, 16, 128)

    quarter = running // 4
    table = slots

    def decode(part, after):
        ready, _ = lax.optimization_barrier((half, after))
        return running_rows(part * quarter, quarter, ready, pages, lens, queries, own, pool)

    def phase(part, table, lists):
        (kx, ka, kxa, kmasks), (vx, va, vxa, vmasks) = lists
        first = decode(part, (kx, vx))
        sent = [hop(kx, kmasks[0]), hop(ka, kmasks[1]), hop(vx, vmasks[0]), hop(va, vmasks[1])]
        kxa, vxa, sent, first = lax.optimization_barrier((kxa, vxa, sent, first))
        second = decode(part + 1, first)
        kxa, vxa = hop(kxa, kmasks[2]), hop(vxa, vmasks[2])
        table, kxa, vxa, second = lax.optimization_barrier((table, kxa, vxa, second))
        return table, sent[:2] + [kxa], sent[2:] + [vxa], [first, second]

    lists = (
        (*pack_lists(table, kv, other, [], 0, 0, caps), XY),
        (*pack_lists(table, kv, other, [], 6, 1, caps), YZ),
    )
    table, keys, values, early = phase(0, table, lists)
    lists = (
        (*pack_lists(table, kv, other, keys, 3, 0, caps), YZ),
        (*pack_lists(table, kv, other, values, 9, 1, caps), XY),
    )
    table, more_keys, more_values, late = phase(2, table, lists)
    boxes = keys + more_keys + values + more_values
    handed, landed = land_rows(running, rows - running, land, queries, own, kv, other, boxes)
    return join(*early, *late, handed), landed


def join(*contexts):
    return jnp.concatenate([c.reshape(c.shape[0], -1) for c in contexts], axis=0)


def earlier_matches(labels, block_len, kind_count):
    onehot = (labels[:, None] == jnp.arange(kind_count, dtype=jnp.int32)[None, :]).astype(jnp.int32)
    blocks = onehot.reshape(labels.shape[0] // block_len, block_len, kind_count)
    before = jnp.cumsum(blocks, axis=1) - blocks
    return jnp.sum(before * blocks, axis=2).reshape(labels.shape[0])


def lookup(matches):
    prompt_ids = jnp.arange(matches.shape[1], dtype=jnp.int32)
    row_index = jnp.sum(jnp.where(matches, prompt_ids[None, :], 0), axis=1)
    return (row_index, jnp.any(matches, axis=1))


def pick_rows(table_rows, row_index, is_valid):
    picked = jnp.take(table_rows, row_index, axis=0)
    mask_shape = (is_valid.shape[0],) + (1,) * (picked.ndim - 1)
    return jnp.where(is_valid.reshape(mask_shape), picked, jnp.zeros_like(picked))


def any_fill(targets, prompt_lens, kv, half, pages, lens, queries, own, pool):
    prompt_kv = kv.reshape(16, 1, 512, 256)
    groups = lax.axis_size("grp")
    group_id = lax.axis_index("grp")
    half_id = lax.axis_index("tp") % 2
    block_len = prompt_kv.shape[0]
    prompt_count = targets.shape[0]
    span_len = prompt_kv.shape[2]
    capacity = max(2, block_len // groups)
    source = jnp.arange(prompt_count, dtype=jnp.int32) // block_len
    arrival = earlier_matches(targets, prompt_count, 2 * groups)
    slot_ids = jnp.arange(block_len, dtype=jnp.int32)
    land_match = (targets[None, :] == 2 * group_id + half_id) & (
        arrival[None, :] == slot_ids[:, None]
    )
    land_len = jnp.sum(jnp.where(land_match, prompt_lens[None, :], 0), axis=1)
    land_live = jnp.arange(span_len, dtype=jnp.int32)[None, :] < land_len[:, None]
    land_index, land_valid = lookup(land_match)
    outgoing = source == group_id
    dest_ids = jnp.arange(groups, dtype=jnp.int32)
    cap_ids = jnp.arange(capacity, dtype=jnp.int32)
    partner = hop(prompt_kv, Z)
    pair_kv = jnp.where(
        half_id == 0,
        jnp.concatenate([prompt_kv, partner], axis=1),
        jnp.concatenate([partner, prompt_kv], axis=1),
    )
    within = earlier_matches(targets, block_len, 2 * groups)
    send_match = (
        outgoing[None, None, :]
        & (targets[None, None, :] == (2 * dest_ids + half_id)[:, None, None])
        & (within[None, None, :] == cap_ids[None, :, None])
    )
    send_index, send_valid = lookup(send_match.reshape(groups * capacity, prompt_count))
    send_index = jnp.where(send_valid, send_index - group_id * block_len, 0)
    outbox = pick_rows(pair_kv, send_index, send_valid)
    outbox = outbox.reshape((groups, capacity) + outbox.shape[1:])
    inbound = lax.all_to_all(outbox, "grp", split_axis=0, concat_axis=0, tiled=True)
    inbound = inbound.reshape((groups * capacity,) + inbound.shape[2:])
    entry_ids = source * capacity + within
    landed = pick_rows(inbound, jnp.take(entry_ids, land_index), land_valid)
    landed = jnp.where(land_live[:, None, :, None], landed, jnp.zeros_like(landed))
    running = pages.shape[1]
    queries = queries.reshape(queries.shape[0], 16, 128)
    decoded = running_rows(0, running, half, pages, lens, queries, own, pool)
    handed = jnp.stack(
        [
            attend_row(queries[running + s], landed[s, 0], landed[s, 1], own[running + s], land_len[s])
            for s in range(block_len)
        ]
    )
    landed = landed.reshape(block_len, 2, PROMPT_CHUNKS, CHUNK, 256)
    return join(decoded, handed), landed


def local(targets, prompt_lens, prompt_kv, cache_pool, block_table, cache_lens, queries, new_kv):
    group = lax.axis_index("grp")
    member = lax.axis_index("tp")
    kv = prompt_kv.reshape(OWN_CHUNKS, CHUNK, 256)
    other = hop(kv, CORE)
    slots, land = plan(targets, prompt_lens, group, member)
    half = (member % 2).astype(jnp.int32).reshape(1)
    rows = queries.shape[2]
    shared = (
        half,
        block_table[0],
        cache_lens[0],
        queries.reshape(rows, -1),
        new_kv[0, 0],
        cache_pool[0, 0],
    )

    def at_level(caps):
        return lambda t, l, s, w, k, o, *rest: routed(caps, s, w, k, o, *rest)

    branches = [at_level(caps) for caps in LEVELS]
    branches.append(lambda t, l, s, w, k, o, *rest: any_fill(t, l, k, *rest))
    context, landed = lax.switch(
        land[1, 0], branches, targets, prompt_lens, slots, land, kv, other, *shared
    )
    return (
        context.reshape(1, 1, rows, queries.shape[3]),
        landed.reshape(1, 1, 16, 2, 512, 256),
    )


def solution(mesh):
    placed = (
        P(),
        P(),
        P("grp", "tp", None, None),
        P("grp", "tp", None, None, None, None),
        P("grp", None, None, None),
        P("grp", None, None),
        P("grp", "tp", None, None),
        P("grp", "tp", None, None, None),
    )
    return jax.shard_map(
        local,
        mesh=mesh,
        in_specs=placed,
        out_specs=(P("grp", "tp", None, None), P("grp", "tp", None, None, None, None)),
        check_vma=False,
    )
```

```python
import functools
import math

import jax
import jax.numpy as jnp
import numpy as np
from jax import lax
from jax.experimental import pallas as pl
from jax.experimental.pallas import tpu as pltpu
from jax.sharding import PartitionSpec as P

CHUNK = 32
PROMPT_CHUNKS = 16
OWN_CHUNKS = 256
HOME = 512
X, YA, YB, Z, CORE = 1, 2, 4, 8, 16
ORDERS = ((X, Z, YB, YA), (YA, YB, Z, X), (YB, YA, X, Z), (Z, X, YA, YB))
DEAL = (2, 0, 1, 3, 2, 0, 1, 2, 3, 0, 1, 2, 0, 1, 3, 2)
SHARES = tuple(sum(1 << k for k, part in enumerate(DEAL) if part == q) for q in range(4))
ROOM = ((40, 40, 48, 36), (48, 44, 48, 48), (64, 52, 48, 52), (72, 72, 68, 60))
MIB = 1024 * 1024
SMALL = 4096


def region(phase, part):
    before = [room for rooms in ROOM[:phase] for room in rooms] + list(ROOM[phase][:part])
    return HOME + sum(before)


def space_of(phases):
    return HOME + sum(room for rooms in ROOM[:phases] for room in rooms)


def flipped(group, mask):
    x, core, y = (group >> 1) & 1, group & 1, group >> 2
    if mask & X:
        x ^= 1
    if mask & YA:
        y ^= 1
    if mask & YB:
        y = 3 - y
    if mask & CORE:
        core ^= 1
    return (y << 2) | (x << 1) | core


def hop(value, axis):
    if axis == Z:
        return lax.ppermute(value, "tp", [(t, t ^ 1) for t in range(lax.axis_size("tp"))])
    return lax.ppermute(value, "grp", [(g, flipped(g, axis)) for g in range(lax.axis_size("grp"))])


def node_of(group, parity):
    y = group >> 2
    return (
        ((group >> 1) & 1)
        | (((y ^ (y >> 1)) & 1) << 1)
        | (((y >> 1) & 1) << 2)
        | (parity << 3)
        | ((group & 1) << 4)
    )


def bits_set(word):
    word = word - ((word >> 1) & 0x5555)
    word = (word & 0x3333) + ((word >> 2) & 0x3333)
    word = (word + (word >> 4)) & 0x0F0F
    return (word + (word >> 8)) & 0x1F


def turned(share, by):
    return ((share | (share << 16)) >> by) & 0xFFFF


def below(k):
    return (1 << k) - 1


def plan_kernel(where_ref, targets_ref, lens_ref, const_ref, slots_ref, land_ref):
    me, mine, group = where_ref[0], where_ref[1], where_ref[2]
    row_t = jnp.concatenate([targets_ref[...], targets_ref[...]], axis=1)
    row_l = jnp.concatenate([lens_ref[...], lens_ref[...]], axis=1)
    items = row_t.shape[1]
    prompts = items // 2

    def upright(row):
        down = lax.broadcasted_iota(jnp.int32, (prompts, prompts), 0)
        along = lax.broadcasted_iota(jnp.int32, (prompts, prompts), 1)
        column = jnp.sum(jnp.where(down == along, row[:, :prompts], 0), axis=1, keepdims=True)
        return jnp.concatenate([column, column], axis=0)

    def derive(targets, item):
        prompt = item & (prompts - 1)
        parity = item >> 8
        start = node_of(prompt >> 4, parity)
        end = node_of(targets >> 1, targets & 1)
        start = (start & 15) | (end & CORE)
        return prompt, parity, start, start ^ end

    col_t, col_l = upright(row_t), upright(row_l)
    item = lax.broadcasted_iota(jnp.int32, (items, 1), 0)
    prompt, parity, start, ways = derive(col_t, item)
    chunks = (col_l + (CHUNK - 1)) >> 5
    turn = (prompt * 5) & 15
    routed, bit, sender, share, room = (const_ref[k : k + 1, :] for k in range(5))
    lane = lax.broadcasted_iota(jnp.int32, (1, 64), 1)
    weight = bits_set(turned(share, turn) & below(chunks))
    crosses = (ways & bit) != 0
    at_home = (ways & routed) == 0
    listed = crosses & ((start ^ (ways & routed)) == (me ^ sender)) & (lane < 32)
    landing = (col_t == mine) & (((lane == 32) & (parity == 0)) | ((lane == 33) & (parity == 1)))

    def exact(values):
        return values.astype(jnp.float32).astype(jnp.bfloat16)

    def dot(left, right):
        return jnp.dot(left, right, preferred_element_type=jnp.float32)

    down = lax.broadcasted_iota(jnp.int32, (items, items), 0)
    along = lax.broadcasted_iota(jnp.int32, (items, items), 1)
    amount = jnp.where(listed, weight, jnp.where(landing, 1, 0))
    place = dot(exact(jnp.where(along < down, 1, 0)), exact(amount)).astype(jnp.int32)

    everyone = exact(jnp.where(crosses & (lane < 16), weight, 0))
    row_item = lax.broadcasted_iota(jnp.int32, (1, items), 1)
    _, _, row_start, row_ways = derive(row_t, row_item)
    nodes = lax.broadcasted_iota(jnp.int32, (32, 1), 0)
    need = jnp.zeros((1, 64), jnp.float32)
    for done in sorted({sum(order[:p]) for order in ORDERS for p in range(4)}):
        present = exact(jnp.where(nodes == (row_start ^ (row_ways & done)), 1, 0))
        held = jnp.max(dot(present, everyone), axis=0, keepdims=True)
        need = jnp.where(routed == done, held, need)
    over = (need.astype(jnp.int32) > room) & (lane < 16)
    over = jnp.max(jnp.where(over, 1, 0), axis=1, keepdims=True)

    bases = [[jnp.zeros_like(ways)] * 4]
    for p in range(4):
        came = []
        for q in range(4):
            k = 16 + 4 * p + q
            moved = (ways & ORDERS[q][p]) != 0
            came.append(jnp.where(moved, region(p, q) + place[:, k : k + 1], bases[p][q]))
        bases.append(came)

    unit = lax.broadcasted_iota(jnp.int32, (HOME, 1), 0)
    local, k = unit >> 4, unit & 15
    unit_prompt = jnp.where(local < 16, 16 * group + local, 16 * (group ^ 1) + local - 16)
    unit_item = unit_prompt + prompts * ((me >> 3) & 1)
    told = jnp.where(listed & at_home, jnp.minimum(place, 250), 255)
    told = jnp.where(lane == 63, chunks, told)
    told = dot(exact(jnp.where(row_item == unit_item, 1, 0)), exact(told)).astype(jnp.int32)
    mine_of = turned(share, (unit_prompt * 5) & 15)
    dealt = (((mine_of >> k) & 1) != 0) & (k < told[:, 63:64]) & (told < 255)
    unit_place = jnp.where(dealt, told + bits_set(mine_of & below(k)), -1)

    slot = lax.broadcasted_iota(jnp.int32, (1, 128), 1)

    def sources(p, q):
        c = 4 * p + q
        found = jnp.where(unit_place[:, c : c + 1] == slot, unit, 0)
        if p:
            first = jnp.where(listed[:, c : c + 1] & jnp.logical_not(at_home[:, c : c + 1]), place[:, c : c + 1], 1 << 20)
            offset = slot - first
            inside = (offset >= 0) & (offset < weight[:, c : c + 1])
            found += jnp.where(inside, jnp.minimum(offset + bases[p][q], space_of(p) - 1), 0)
        return jnp.sum(found, axis=0, keepdims=True)

    slots_ref[...] = jnp.concatenate([sources(p, q) for p in range(4) for q in range(4)], axis=0)

    rank = jnp.where(parity == 0, place[:, 32:33], place[:, 33:34])
    lands = (col_t == mine) & (rank == slot)

    def landed(value, which):
        return jnp.sum(jnp.where(lands & (parity == which), value, 0), axis=0, keepdims=True)

    own = (prompt & 15) * PROMPT_CHUNKS
    own += jnp.where(((prompt >> 4) & 1) == (me >> 4), 0, OWN_CHUNKS)
    length = landed(col_l, 0)
    live = (length + (CHUNK - 1)) >> 5
    by = landed(turn, 0)
    rows = []
    for j in range(2):
        stays = landed(jnp.where((ways & 15) == 0, 1, 0), j)
        home = landed(own, j)
        held = [landed(bases[4][q], j) for q in range(4)]
        parts = [turned(jnp.full_like(by, SHARES[q]), by) for q in range(4)]
        for k in range(PROMPT_CHUNKS):
            source = jnp.zeros_like(by)
            for q in range(4):
                source += ((parts[q] >> k) & 1) * (held[q] + bits_set(parts[q] & ((1 << k) - 1)))
            source = jnp.where(stays != 0, home + k, jnp.minimum(source, space_of(4) - 1))
            rows.append(jnp.where(k < live, source, 0))
    rows += [length, jnp.broadcast_to(over, (1, 128)), jnp.zeros((6, 128), jnp.int32)]
    land_ref[...] = jnp.concatenate(rows, axis=0)


LENGTH, OVER = 32, 33


def plan(targets, prompt_lens, group, member):
    const = np.zeros((8, 64), np.int32)
    for p in range(4):
        for q, order in enumerate(ORDERS):
            for first, sender in ((0, 0), (16, order[p])):
                const[:5, first + 4 * p + q] = (sum(order[:p]), order[p], sender, SHARES[q], ROOM[p][q])
    where = jnp.stack([node_of(group, member % 2), 2 * group + member % 2, group]).astype(jnp.int32)
    vmem = pl.BlockSpec(memory_space=pltpu.VMEM)
    return pl.pallas_call(
        plan_kernel,
        out_shape=(
            jax.ShapeDtypeStruct((16, 128), jnp.int32),
            jax.ShapeDtypeStruct((40, 128), jnp.int32),
        ),
        in_specs=[pl.BlockSpec(memory_space=pltpu.SMEM), vmem, vmem, vmem],
        out_specs=(vmem, vmem),
        compiler_params=pltpu.CompilerParams(vmem_limit_bytes=24 * MIB),
        cost_estimate=cost(SMALL),
        name="plan",
    )(where, targets.reshape(1, -1), prompt_lens.reshape(1, -1), jnp.asarray(const))


def fetch(pairs, sems):
    copies = [
        pltpu.make_async_copy(source, target, sems.at[k]) for k, (source, target) in enumerate(pairs)
    ]
    for copy in copies:
        copy.start()
    return copies


def gather_chunks(table_ref, row, out_ref, pick):
    batch = 4

    def body(s, carry):
        first = s * batch
        held = [pick(table_ref[row, first + b]) for b in range(batch)]
        for b in range(batch):
            out_ref[first + b] = held[b]
        return carry

    lax.fori_loop(0, out_ref.shape[0] // batch, body, 0, unroll=2)


SMEM = pl.BlockSpec(memory_space=pltpu.SMEM)
ANY = pl.BlockSpec(memory_space=pl.ANY)
VMEM = pl.BlockSpec(memory_space=pltpu.VMEM)


def chunks_of(count):
    return jax.ShapeDtypeStruct((count, CHUNK, 256), jnp.bfloat16)


def cost(bytes_accessed, flops=0):
    return pl.CostEstimate(flops=flops, bytes_accessed=bytes_accessed, transcendentals=0)


def space_pairs(homes, boxes, space):
    pairs = [(home, space.at[pl.ds(OWN_CHUNKS * k, OWN_CHUNKS)]) for k, home in enumerate(homes)]
    for k, box in enumerate(boxes):
        pairs.append((box, space.at[pl.ds(region(k // 4, k % 4), box.shape[0])]))
    return pairs


def pack_kernel(phase, table_ref, kv_ref, other_ref, *rest):
    given = 4 * phase
    boxes, outs, space, sems = rest[:given], rest[given : given + 4], rest[given + 4], rest[given + 5]
    for copy in fetch(space_pairs((kv_ref, other_ref), boxes, space), sems):
        copy.wait()
    for q in range(4):
        gather_chunks(table_ref, given + q, outs[q], lambda i: space[i])


def pack_lists(phase, table, kv, other, boxes):
    return pl.pallas_call(
        functools.partial(pack_kernel, phase),
        out_shape=tuple(chunks_of(room) for room in ROOM[phase]),
        in_specs=[SMEM, ANY, ANY] + [ANY] * len(boxes),
        out_specs=(VMEM,) * 4,
        scratch_shapes=[
            pltpu.VMEM((space_of(phase), CHUNK, 256), jnp.bfloat16),
            pltpu.SemaphoreType.DMA((2 + len(boxes),)),
        ],
        compiler_params=pltpu.CompilerParams(vmem_limit_bytes=32 * MIB),
        cost_estimate=cost(SMALL),
        name="pack_lists",
    )(table, kv, other, *boxes)


def attend_row(query, first, second, own, length):
    scaling = 1.0 / math.sqrt(query.shape[1])
    upper = lax.broadcasted_iota(jnp.int32, query.shape, 0) < 8
    zero = jnp.zeros_like(query)
    wide = jnp.concatenate([jnp.where(upper, query, zero), jnp.where(upper, zero, query)], axis=1)
    keys = jnp.concatenate([first[:, :128], second[:, :128]], axis=1)
    values = jnp.concatenate([first[:, 128:], second[:, 128:]], axis=1)
    scores = (
        lax.dot_general(wide, keys, (((1,), (1,)), ((), ())), preferred_element_type=jnp.float32)
        * scaling
    )
    own = own.astype(jnp.float32)
    own_key = jnp.where(upper, own[0:1, :128], own[1:2, :128])
    own_value = jnp.where(upper, own[0:1, 128:], own[1:2, 128:])
    own_score = jnp.sum(query.astype(jnp.float32) * own_key, axis=1, keepdims=True) * scaling
    live = lax.broadcasted_iota(jnp.int32, scores.shape, 1) < length
    scores = jnp.where(live, scores, -jnp.inf)
    row_max = jnp.maximum(jnp.max(scores, axis=1, keepdims=True), own_score)
    weights = jnp.where(live, jnp.exp(scores - row_max), 0.0)
    own_weight = jnp.exp(own_score - row_max)
    denominator = jnp.sum(weights, axis=1, keepdims=True) + own_weight
    both = jnp.dot(weights.astype(jnp.bfloat16), values, preferred_element_type=jnp.float32)
    mixture = jnp.where(upper, both[:, :128], both[:, 128:])
    mixture += own_weight.astype(jnp.bfloat16).astype(jnp.float32) * own_value
    return (mixture / denominator).astype(jnp.bfloat16)


TOGETHER = 4
DEPTH = 4 * TOGETHER


def running_kernel(first, half_ref, pages_ref, lens_ref, query_ref, own_ref, pool_ref, out_ref, held, sems):
    rows = out_ref.shape[0]
    all_rows = lens_ref.shape[0] // 2
    max_pages = held.shape[1]
    start = half_ref[0] * all_rows + first
    held[...] = jnp.zeros_like(held)

    def each_page(row, action):
        slot = row % DEPTH
        count = (lens_ref[start + row] + 63) // 64
        for c in range(max_pages):

            @pl.when(c < count)
            def _():
                page = pages_ref[(start + row) * max_pages + c]
                action(pltpu.make_async_copy(pool_ref.at[page], held.at[slot, c], sems.at[slot, c]))

    def begin(group):
        for r in range(TOGETHER):
            each_page(group * TOGETHER + r, lambda copy: copy.start())

    ahead = DEPTH // TOGETHER - 1
    for group in range(ahead):
        begin(group)

    def body(group, carry):
        @pl.when(group + ahead < rows // TOGETHER)
        def _():
            begin(group + ahead)

        for r in range(TOGETHER):
            each_page(group * TOGETHER + r, lambda copy: copy.wait())
        results = []
        for r in range(TOGETHER):
            row = group * TOGETHER + r
            slot = row % DEPTH
            blocks = [held[slot, :, j].reshape(max_pages * 64, 256) for j in range(2)]
            results.append(
                attend_row(query_ref[first + row], *blocks, own_ref[first + row], lens_ref[start + row])
            )
        for r in range(TOGETHER):
            out_ref[group * TOGETHER + r] = results[r]
        return carry

    lax.fori_loop(0, rows // TOGETHER, body, 0)


def running_rows(first, count, half, pages, lens, queries, own, pool):
    max_pages = pages.shape[-1]
    return pl.pallas_call(
        functools.partial(running_kernel, first),
        out_shape=jax.ShapeDtypeStruct((count, 16, 128), jnp.bfloat16),
        in_specs=[SMEM, SMEM, SMEM, VMEM, VMEM, pl.BlockSpec(memory_space=pltpu.HBM)],
        out_specs=VMEM,
        scratch_shapes=[
            pltpu.VMEM((DEPTH, max_pages) + pool.shape[1:], jnp.bfloat16),
            pltpu.SemaphoreType.DMA((DEPTH, max_pages)),
        ],
        compiler_params=pltpu.CompilerParams(vmem_limit_bytes=48 * MIB),
        cost_estimate=cost(SMALL),
        name="running_rows",
    )(half, pages.reshape(-1), lens.reshape(-1), queries, own, pool)


RING = 4


def land_kernel(first, land_ref, query_ref, own_ref, kv_ref, other_ref, *rest):
    boxes, rest = rest[:16], rest[16:]
    out_ref, landed_ref, block, sems, space, box_sems = rest
    slots = out_ref.shape[0]
    for copy in fetch(space_pairs((kv_ref, other_ref), boxes, space), box_sems):
        copy.wait()

    def write(slot):
        turn = slot % RING
        return pltpu.make_async_copy(block.at[turn], landed_ref.at[slot], sems.at[turn])

    def assemble(slot):
        turn = slot % RING
        length = land_ref[LENGTH, slot]
        count = (length + (CHUNK - 1)) // CHUNK
        for j in range(2):

            def copy(k, carry):
                held = [space[land_ref[PROMPT_CHUNKS * j + 4 * k + b, slot]] for b in range(4)]
                for b in range(4):
                    block[turn, j, 4 * k + b] = held[b]
                return carry

            def clear(k, carry):
                block[turn, j, k] = jnp.zeros((CHUNK, 256), jnp.bfloat16)
                return carry

            lax.fori_loop(0, (count + 3) // 4, copy, 0)
            lax.fori_loop(count, PROMPT_CHUNKS, clear, 0)

            @pl.when(count > 0)
            def _():
                last = count - 1
                row = last * CHUNK + lax.broadcasted_iota(jnp.int32, (CHUNK, 256), 0)
                zero = jnp.zeros((CHUNK, 256), jnp.bfloat16)
                block[turn, j, last] = jnp.where(row < length, block[turn, j, last], zero)

    def body(pair, carry):
        both = (2 * pair, 2 * pair + 1)
        for slot in both:

            @pl.when(slot >= RING)
            def _():
                write(slot).wait()

            assemble(slot)
            write(slot).start()
        results = []
        for slot in both:
            blocks = [block[slot % RING, j].reshape(PROMPT_CHUNKS * CHUNK, 256) for j in range(2)]
            results.append(
                attend_row(query_ref[first + slot], *blocks, own_ref[first + slot], land_ref[LENGTH, slot])
            )
        for slot, result in zip(both, results):
            out_ref[slot] = result
        return carry

    lax.fori_loop(0, slots // 2, body, 0)
    for slot in range(slots - RING, slots):
        write(slot).wait()


def land_rows(first, slots, land, queries, own, kv, other, boxes):
    return pl.pallas_call(
        functools.partial(land_kernel, first),
        out_shape=(
            jax.ShapeDtypeStruct((slots, 16, 128), jnp.bfloat16),
            jax.ShapeDtypeStruct((slots, 2, PROMPT_CHUNKS, CHUNK, 256), jnp.bfloat16),
        ),
        in_specs=[SMEM, VMEM, VMEM, ANY, ANY] + [ANY] * 16,
        out_specs=(VMEM, ANY),
        scratch_shapes=[
            pltpu.VMEM((RING, 2, PROMPT_CHUNKS, CHUNK, 256), jnp.bfloat16),
            pltpu.SemaphoreType.DMA((RING,)),
            pltpu.VMEM((space_of(4), CHUNK, 256), jnp.bfloat16),
            pltpu.SemaphoreType.DMA((18,)),
        ],
        compiler_params=pltpu.CompilerParams(vmem_limit_bytes=40 * MIB),
        cost_estimate=cost(SMALL),
        name="land_rows",
    )(land, queries, own, kv, other, *boxes)


def routed(table, land, kv, other, half, pages, lens, queries, own, pool):
    running = pages.shape[1]
    rows = queries.shape[0]
    quarter = running // 4
    boxes, contexts = [], []
    for phase in range(4):
        lists = pack_lists(phase, table, kv, other, boxes)
        ready, _ = lax.optimization_barrier((half, lists))
        context = running_rows(phase * quarter, quarter, ready, pages, lens, queries, own, pool)
        sent = [hop(value, order[phase]) for value, order in zip(lists, ORDERS)]
        table, land, sent, context = lax.optimization_barrier((table, land, sent, context))
        boxes, contexts = boxes + sent, contexts + [context]
    handed, landed = land_rows(running, rows - running, land, queries, own, kv, other, boxes)
    return join(*contexts), join(handed), landed


def join(*contexts):
    return jnp.concatenate([c.reshape(c.shape[0], -1) for c in contexts], axis=0)


def earlier_matches(labels, block_len, kind_count):
    onehot = (labels[:, None] == jnp.arange(kind_count, dtype=jnp.int32)[None, :]).astype(jnp.int32)
    blocks = onehot.reshape(labels.shape[0] // block_len, block_len, kind_count)
    before = jnp.cumsum(blocks, axis=1) - blocks
    return jnp.sum(before * blocks, axis=2).reshape(labels.shape[0])


def lookup(matches):
    prompt_ids = jnp.arange(matches.shape[1], dtype=jnp.int32)
    row_index = jnp.sum(jnp.where(matches, prompt_ids[None, :], 0), axis=1)
    return (row_index, jnp.any(matches, axis=1))


def pick_rows(table_rows, row_index, is_valid):
    picked = jnp.take(table_rows, row_index, axis=0)
    mask_shape = (is_valid.shape[0],) + (1,) * (picked.ndim - 1)
    return jnp.where(is_valid.reshape(mask_shape), picked, jnp.zeros_like(picked))


def any_fill(targets, prompt_lens, kv, queries, own):
    prompt_kv = kv.reshape(16, 1, 512, 256)
    groups = lax.axis_size("grp")
    group_id = lax.axis_index("grp")
    half_id = lax.axis_index("tp") % 2
    block_len = prompt_kv.shape[0]
    prompt_count = targets.shape[0]
    span_len = prompt_kv.shape[2]
    capacity = max(2, block_len // groups)
    source = jnp.arange(prompt_count, dtype=jnp.int32) // block_len
    arrival = earlier_matches(targets, prompt_count, 2 * groups)
    slot_ids = jnp.arange(block_len, dtype=jnp.int32)
    land_match = (targets[None, :] == 2 * group_id + half_id) & (
        arrival[None, :] == slot_ids[:, None]
    )
    land_len = jnp.sum(jnp.where(land_match, prompt_lens[None, :], 0), axis=1)
    land_live = jnp.arange(span_len, dtype=jnp.int32)[None, :] < land_len[:, None]
    land_index, land_valid = lookup(land_match)
    outgoing = source == group_id
    dest_ids = jnp.arange(groups, dtype=jnp.int32)
    cap_ids = jnp.arange(capacity, dtype=jnp.int32)
    partner = hop(prompt_kv, Z)
    pair_kv = jnp.where(
        half_id == 0,
        jnp.concatenate([prompt_kv, partner], axis=1),
        jnp.concatenate([partner, prompt_kv], axis=1),
    )
    within = earlier_matches(targets, block_len, 2 * groups)
    send_match = (
        outgoing[None, None, :]
        & (targets[None, None, :] == (2 * dest_ids + half_id)[:, None, None])
        & (within[None, None, :] == cap_ids[None, :, None])
    )
    send_index, send_valid = lookup(send_match.reshape(groups * capacity, prompt_count))
    send_index = jnp.where(send_valid, send_index - group_id * block_len, 0)
    outbox = pick_rows(pair_kv, send_index, send_valid)
    outbox = outbox.reshape((groups, capacity) + outbox.shape[1:])
    inbound = lax.all_to_all(outbox, "grp", split_axis=0, concat_axis=0, tiled=True)
    inbound = inbound.reshape((groups * capacity,) + inbound.shape[2:])
    entry_ids = source * capacity + within
    landed = pick_rows(inbound, jnp.take(entry_ids, land_index), land_valid)
    landed = jnp.where(land_live[:, None, :, None], landed, jnp.zeros_like(landed))
    handed = jnp.stack(
        [
            attend_row(queries[s], landed[s, 0], landed[s, 1], own[s], land_len[s])
            for s in range(block_len)
        ]
    )
    return join(handed), landed.reshape(block_len, 2, PROMPT_CHUNKS, CHUNK, 256)


def local(targets, prompt_lens, prompt_kv, cache_pool, block_table, cache_lens, queries, new_kv):
    group = lax.axis_index("grp")
    member = lax.axis_index("tp")
    kv = prompt_kv.reshape(OWN_CHUNKS, CHUNK, 256)
    other = hop(kv, CORE)
    table, land = plan(targets, prompt_lens, group, member)
    half = (member % 2).astype(jnp.int32).reshape(1)
    rows = queries.shape[2]
    running = block_table.shape[2]
    by_head = queries.reshape(rows, 16, 128)
    own = new_kv[0, 0]
    decoded, handed, landed = routed(
        table, land, kv, other, half, block_table[0], cache_lens[0], by_head, own, cache_pool[0, 0]
    )

    def again(carry):
        return (*any_fill(targets, prompt_lens, kv, by_head[running:], own[running:]), jnp.zeros((), jnp.int32))

    handed, landed, _ = lax.while_loop(lambda carry: carry[2] > 0, again, (handed, landed, land[OVER, 0]))
    return (
        jnp.concatenate([decoded, handed], axis=0).reshape(1, 1, rows, queries.shape[3]),
        landed.reshape(1, 1, 16, 2, 512, 256),
    )


def solution(mesh):
    placed = (
        P(),
        P(),
        P("grp", "tp", None, None),
        P("grp", "tp", None, None, None, None),
        P("grp", None, None, None),
        P("grp", None, None),
        P("grp", "tp", None, None),
        P("grp", "tp", None, None, None),
    )
    return jax.shard_map(
        local,
        mesh=mesh,
        in_specs=placed,
        out_specs=(P("grp", "tp", None, None), P("grp", "tp", None, None, None, None)),
        check_vma=False,
    )
```

```python
import functools
import math

import jax
import jax.numpy as jnp
import numpy as np
from jax import lax
from jax.experimental import pallas as pl
from jax.experimental.pallas import tpu as pltpu
from jax.sharding import PartitionSpec as P

CHUNK = 32
PROMPT_CHUNKS = 16
OWN_CHUNKS = 256
HOME = 512
X, YA, YB, Z, CORE = 1, 2, 4, 8, 16
ORDERS = ((X, Z, YB, YA), (YA, YB, Z, X), (YB, YA, X, Z), (Z, X, YA, YB))
DEAL = (2, 0, 1, 3, 2, 0, 1, 2, 3, 0, 1, 2, 0, 1, 3, 2)
SHARES = tuple(sum(1 << k for k, part in enumerate(DEAL) if part == q) for q in range(4))
ROOM = ((40, 40, 48, 36), (48, 44, 48, 48), (64, 52, 48, 52), (72, 72, 68, 60))
MIB = 1024 * 1024
SMALL = 4096


KEPT = (52, 52, 64, 40)


def region(phase, part):
    return KEPT[part] + sum(rooms[part] for rooms in ROOM[:phase])


def begin_of(part):
    return sum(region(4, q) for q in range(part))


def flipped(group, mask):
    x, core, y = (group >> 1) & 1, group & 1, group >> 2
    if mask & X:
        x ^= 1
    if mask & YA:
        y ^= 1
    if mask & YB:
        y = 3 - y
    if mask & CORE:
        core ^= 1
    return (y << 2) | (x << 1) | core


def hop(value, axis):
    if axis == Z:
        return lax.ppermute(value, "tp", [(t, t ^ 1) for t in range(lax.axis_size("tp"))])
    return lax.ppermute(value, "grp", [(g, flipped(g, axis)) for g in range(lax.axis_size("grp"))])


def node_of(group, parity):
    y = group >> 2
    return (
        ((group >> 1) & 1)
        | (((y ^ (y >> 1)) & 1) << 1)
        | (((y >> 1) & 1) << 2)
        | (parity << 3)
        | ((group & 1) << 4)
    )


def bits_set(word):
    word = word - ((word >> 1) & 0x5555)
    word = (word & 0x3333) + ((word >> 2) & 0x3333)
    word = (word + (word >> 4)) & 0x0F0F
    return (word + (word >> 8)) & 0x1F


def turned(share, by):
    return ((share | (share << 16)) >> by) & 0xFFFF


def below(k):
    return (1 << k) - 1


def exact(values):
    return values.astype(jnp.float32).astype(jnp.bfloat16)


def dot(left, right):
    return jnp.dot(left, right, preferred_element_type=jnp.float32)


def standing(row):
    size = row.shape[1]
    down = lax.broadcasted_iota(jnp.int32, (size, size), 0)
    along = lax.broadcasted_iota(jnp.int32, (size, size), 1)
    return jnp.sum(jnp.where(down == along, row, 0), axis=1, keepdims=True)


def ends_of(targets, prompt, parity):
    start = node_of(prompt >> 4, parity)
    end = node_of(targets >> 1, targets & 1)
    start = (start & 15) | (end & CORE)
    return start, start ^ end


def earlier_rows(size):
    down = lax.broadcasted_iota(jnp.int32, (size, size), 0)
    along = lax.broadcasted_iota(jnp.int32, (size, size), 1)
    return exact(jnp.where(along < down, 1, 0))


SENT, RECEIVED, SLOTS, HELD = 0, 16, 32, 36


def first_plan_kernel(where_ref, targets_ref, lens_ref, const_ref, table_ref):
    me, group = where_ref[0], where_ref[2]
    local = lax.broadcasted_iota(jnp.int32, (32, 1), 0)
    prompt = 16 * (group & ~1) + local
    match = lax.broadcasted_iota(jnp.int32, (32, targets_ref.shape[1]), 1) == prompt
    targets = jnp.sum(jnp.where(match, targets_ref[...], 0), axis=1, keepdims=True)
    lens = jnp.sum(jnp.where(match, lens_ref[...], 0), axis=1, keepdims=True)
    start, ways = ends_of(targets, prompt, (me >> 3) & 1)
    bit, share = const_ref[1:2, :], const_ref[3:4, :]
    lane = lax.broadcasted_iota(jnp.int32, (1, 64), 1)
    word = turned(share, (prompt * 5) & 15) & below((lens + (CHUNK - 1)) >> 5)
    goes = (lane < 4) & ((ways & bit) != 0) | (lane >= HELD) & (lane < HELD + 4)
    goes = goes & (start == me)
    place = dot(earlier_rows(32), exact(jnp.where(goes, bits_set(word), 0))).astype(jnp.int32)
    place = jnp.where(goes, place, -256)

    def each_chunk(values):
        wide = jnp.broadcast_to(values[:, None, :], (32, PROMPT_CHUNKS, values.shape[1]))
        return wide.reshape(32 * PROMPT_CHUNKS, values.shape[1])

    unit = lax.broadcasted_iota(jnp.int32, (HOME, 1), 0)
    k = unit & 15
    home = jnp.where(((unit >> 8) & 1) == (group & 1), 0, OWN_CHUNKS) + (unit & (OWN_CHUNKS - 1))
    words = each_chunk(word)
    spot = jnp.where(((words >> k) & 1) != 0, each_chunk(place) + bits_set(words & below(k)), -1)
    slot = lax.broadcasted_iota(jnp.int32, (1, 128), 1)
    rows = []
    for c in (0, 1, 2, 3, HELD, HELD + 1, HELD + 2, HELD + 3):
        rows.append(jnp.sum(jnp.where(spot[:, c : c + 1] == slot, home, 0), axis=0, keepdims=True))
    table_ref[...] = jnp.concatenate(rows, axis=0)


LENGTH, OVER = 32, 33


def plan_kernel(where_ref, targets_ref, lens_ref, const_ref, slots_ref, land_ref):
    me, mine = where_ref[0], where_ref[1]
    row_t = jnp.concatenate([targets_ref[...], targets_ref[...]], axis=1)
    items = row_t.shape[1]
    prompts = items // 2
    col_t, col_l = standing(targets_ref[...]), standing(lens_ref[...])
    col_t, col_l = (jnp.concatenate([c, c], axis=0) for c in (col_t, col_l))
    item = lax.broadcasted_iota(jnp.int32, (items, 1), 0)
    prompt, parity = item & (prompts - 1), item >> 8
    start, ways = ends_of(col_t, prompt, parity)
    turn = (prompt * 5) & 15
    routed, bit, sender, share, room = (const_ref[k : k + 1, :] for k in range(5))
    lane = lax.broadcasted_iota(jnp.int32, (1, 64), 1)
    keeps = (lane >= HELD) & (lane < HELD + 4)
    weight = bits_set(turned(share, turn) & below((col_l + (CHUNK - 1)) >> 5))
    crosses = ((ways & bit) != 0) & (lane < SLOTS) | keeps
    listed = crosses & ((start ^ (ways & routed)) == (me ^ sender))
    landing = (col_t == mine) & (lane == SLOTS + parity)
    amount = jnp.where(listed, weight, jnp.where(landing, 1, 0))
    place = dot(earlier_rows(items), exact(amount)).astype(jnp.int32)

    everyone = exact(jnp.where(crosses, weight, 0))
    row_item = lax.broadcasted_iota(jnp.int32, (1, items), 1)
    row_start, row_ways = ends_of(row_t, row_item & (prompts - 1), row_item >> 8)
    nodes = lax.broadcasted_iota(jnp.int32, (32, 1), 0)
    need = jnp.zeros((1, 64), jnp.float32)
    for done in sorted({sum(order[:p]) for order in ORDERS for p in range(4)}):
        present = exact(jnp.where(nodes == (row_start ^ (row_ways & done)), 1, 0))
        held = jnp.max(dot(present, everyone), axis=0, keepdims=True)
        need = jnp.where(routed == done, held, need)
    over = (need.astype(jnp.int32) > room) & ((lane < RECEIVED) | keeps)
    over = jnp.max(jnp.where(over, 1, 0), axis=1, keepdims=True)

    bases = [[place[:, HELD + q : HELD + q + 1] for q in range(4)]]
    for p in range(4):
        came = []
        for q in range(4):
            c = RECEIVED + 4 * p + q
            moved = (ways & ORDERS[q][p]) != 0
            came.append(jnp.where(moved, region(p, q) + place[:, c : c + 1], bases[p][q]))
        bases.append(came)

    slot = lax.broadcasted_iota(jnp.int32, (1, 128), 1)

    def sources(p, q):
        c = 4 * p + q
        first = jnp.where(listed[:, c : c + 1], place[:, c : c + 1], 1 << 20)
        offset = slot - first
        inside = (offset >= 0) & (offset < weight[:, c : c + 1])
        found = jnp.where(inside, offset + bases[p][q], 0)
        return jnp.minimum(jnp.sum(found, axis=0, keepdims=True), region(p, q) - 1)

    slots_ref[...] = jnp.concatenate(
        [jnp.zeros((4, 128), jnp.int32)] + [sources(p, q) for p in range(1, 4) for q in range(4)], axis=0
    )

    rank = jnp.where(parity == 0, place[:, SLOTS : SLOTS + 1], place[:, SLOTS + 1 : SLOTS + 2])
    rank = jnp.where(col_t == mine, rank, -1)
    lands = [rank[:prompts] == slot, rank[prompts:] == slot]

    def landed(value, j):
        return jnp.sum(jnp.where(lands[j], value[j * prompts : (j + 1) * prompts], 0), axis=0, keepdims=True)

    length = landed(col_l, 0)
    live = (length + (CHUNK - 1)) >> 5
    by = landed(turn, 0)
    parts = [turned(jnp.full_like(by, SHARES[q]), by) for q in range(4)]
    rows = []
    for j in range(2):
        held = [landed(bases[4][q], j) for q in range(4)]
        for k in range(PROMPT_CHUNKS):
            source = jnp.zeros_like(by)
            for q in range(4):
                spot = jnp.minimum(held[q] + bits_set(parts[q] & ((1 << k) - 1)), region(4, q) - 1)
                source += ((parts[q] >> k) & 1) * (begin_of(q) + spot)
            rows.append(jnp.where(k < live, source, begin_of(4)))
    rows += [length, jnp.broadcast_to(over, (1, 128)), jnp.zeros((6, 128), jnp.int32)]
    land_ref[...] = jnp.concatenate(rows, axis=0)


def plan_const():
    const = np.zeros((8, 64), np.int32)
    for p in range(4):
        for q, order in enumerate(ORDERS):
            for first, sender in ((SENT, 0), (RECEIVED, order[p])):
                const[:5, first + 4 * p + q] = (sum(order[:p]), order[p], sender, SHARES[q], ROOM[p][q])
    for q in range(4):
        const[3:5, HELD + q] = (SHARES[q], KEPT[q])
    return jnp.asarray(const)


def plan_call(kernel, name, rows, *operands):
    vmem = pl.BlockSpec(memory_space=pltpu.VMEM)
    return pl.pallas_call(
        kernel,
        out_shape=tuple(jax.ShapeDtypeStruct((r, 128), jnp.int32) for r in rows),
        in_specs=[pl.BlockSpec(memory_space=pltpu.SMEM), vmem, vmem, vmem],
        out_specs=(vmem,) * len(rows),
        compiler_params=pltpu.CompilerParams(vmem_limit_bytes=24 * MIB),
        cost_estimate=cost(SMALL),
        name=name,
    )(*operands)


def plan_operands(targets, prompt_lens, group, member):
    where = jnp.stack([node_of(group, member % 2), 2 * group + member % 2, group]).astype(jnp.int32)
    return where, targets.reshape(1, -1), prompt_lens.reshape(1, -1), plan_const()


def fetch(pairs, sems):
    copies = [
        pltpu.make_async_copy(source, target, sems.at[k]) for k, (source, target) in enumerate(pairs)
    ]
    for copy in copies:
        copy.start()
    return copies


def gather_chunks(table_ref, row, out_ref, pick):
    batch = 4

    def body(s, carry):
        first = s * batch
        held = [pick(table_ref[row, first + b]) for b in range(batch)]
        for b in range(batch):
            out_ref[first + b] = held[b]
        return carry

    lax.fori_loop(0, out_ref.shape[0] // batch, body, 0, unroll=2)


SMEM = pl.BlockSpec(memory_space=pltpu.SMEM)
ANY = pl.BlockSpec(memory_space=pl.ANY)
VMEM = pl.BlockSpec(memory_space=pltpu.VMEM)


def chunks_of(count):
    return jax.ShapeDtypeStruct((count, CHUNK, 256), jnp.bfloat16)


def cost(bytes_accessed, flops=0):
    return pl.CostEstimate(flops=flops, bytes_accessed=bytes_accessed, transcendentals=0)


def home_kernel(rows, table_ref, kv_ref, other_ref, *rest):
    outs, space, sems = rest[:4], rest[4], rest[5]
    pairs = [(ref, space.at[pl.ds(OWN_CHUNKS * k, OWN_CHUNKS)]) for k, ref in enumerate((kv_ref, other_ref))]
    for copy in fetch(pairs, sems):
        copy.wait()
    for q in range(4):
        gather_chunks(table_ref, rows + q, outs[q], lambda i: space[i])


def home_lists(rows, rooms, table, kv, other):
    return pl.pallas_call(
        functools.partial(home_kernel, rows),
        out_shape=tuple(chunks_of(room) for room in rooms),
        in_specs=[SMEM, ANY, ANY],
        out_specs=(VMEM,) * 4,
        scratch_shapes=[
            pltpu.VMEM((HOME, CHUNK, 256), jnp.bfloat16),
            pltpu.SemaphoreType.DMA((2,)),
        ],
        compiler_params=pltpu.CompilerParams(vmem_limit_bytes=24 * MIB),
        cost_estimate=cost(SMALL),
        name="home_lists",
    )(table, kv, other)


def part_pairs(part, boxes, space, begin=0):
    pairs = []
    for k, box in enumerate(boxes):
        at = begin + (region(k - 1, part) if k else 0)
        pairs.append((box, space.at[pl.ds(at, box.shape[0])]))
    return pairs


def next_kernel(phase, part, table_ref, *rest):
    boxes, out_ref, space, sems = rest[: phase + 1], rest[phase + 1], rest[phase + 2], rest[phase + 3]
    for copy in fetch(part_pairs(part, boxes, space), sems):
        copy.wait()
    gather_chunks(table_ref, 4 * phase + part, out_ref, lambda i: space[i])


def next_list(phase, part, table, boxes):
    return pl.pallas_call(
        functools.partial(next_kernel, phase, part),
        out_shape=chunks_of(ROOM[phase][part]),
        in_specs=[SMEM] + [ANY] * len(boxes),
        out_specs=VMEM,
        scratch_shapes=[
            pltpu.VMEM((region(phase, part), CHUNK, 256), jnp.bfloat16),
            pltpu.SemaphoreType.DMA((len(boxes),)),
        ],
        compiler_params=pltpu.CompilerParams(vmem_limit_bytes=16 * MIB),
        cost_estimate=cost(SMALL),
        name="next_list",
    )(table, *boxes)


def attend_row(query, first, second, own, length):
    scaling = 1.0 / math.sqrt(query.shape[1])
    upper = lax.broadcasted_iota(jnp.int32, query.shape, 0) < 8
    zero = jnp.zeros_like(query)
    wide = jnp.concatenate([jnp.where(upper, query, zero), jnp.where(upper, zero, query)], axis=1)
    keys = jnp.concatenate([first[:, :128], second[:, :128]], axis=1)
    values = jnp.concatenate([first[:, 128:], second[:, 128:]], axis=1)
    scores = (
        lax.dot_general(wide, keys, (((1,), (1,)), ((), ())), preferred_element_type=jnp.float32)
        * scaling
    )
    own = own.astype(jnp.float32)
    own_key = jnp.where(upper, own[0:1, :128], own[1:2, :128])
    own_value = jnp.where(upper, own[0:1, 128:], own[1:2, 128:])
    own_score = jnp.sum(query.astype(jnp.float32) * own_key, axis=1, keepdims=True) * scaling
    live = lax.broadcasted_iota(jnp.int32, scores.shape, 1) < length
    scores = jnp.where(live, scores, -jnp.inf)
    row_max = jnp.maximum(jnp.max(scores, axis=1, keepdims=True), own_score)
    weights = jnp.where(live, jnp.exp(scores - row_max), 0.0)
    own_weight = jnp.exp(own_score - row_max)
    denominator = jnp.sum(weights, axis=1, keepdims=True) + own_weight
    both = jnp.dot(weights.astype(jnp.bfloat16), values, preferred_element_type=jnp.float32)
    mixture = jnp.where(upper, both[:, :128], both[:, 128:])
    mixture += own_weight.astype(jnp.bfloat16).astype(jnp.float32) * own_value
    return (mixture / denominator).astype(jnp.bfloat16)


TOGETHER = 4
DEPTH = 4 * TOGETHER


def running_kernel(first, half_ref, pages_ref, lens_ref, query_ref, own_ref, pool_ref, out_ref, held, sems):
    rows = out_ref.shape[0]
    all_rows = lens_ref.shape[0] // 2
    max_pages = held.shape[1]
    start = half_ref[0] * all_rows + first

    def each_page(row, action):
        slot = row % DEPTH
        for c in range(max_pages):
            page = pages_ref[(start + row) * max_pages + c]
            action(pltpu.make_async_copy(pool_ref.at[page], held.at[slot, c], sems.at[slot, c]))

    def begin(group):
        for r in range(TOGETHER):
            each_page(group * TOGETHER + r, lambda copy: copy.start())

    ahead = DEPTH // TOGETHER - 1
    for group in range(ahead):
        begin(group)

    def body(group, carry):
        @pl.when(group + ahead < rows // TOGETHER)
        def _():
            begin(group + ahead)

        for r in range(TOGETHER):
            each_page(group * TOGETHER + r, lambda copy: copy.wait())
        results = []
        for r in range(TOGETHER):
            row = group * TOGETHER + r
            slot = row % DEPTH
            blocks = [held[slot, :, j].reshape(max_pages * 64, 256) for j in range(2)]
            results.append(
                attend_row(query_ref[first + row], *blocks, own_ref[first + row], lens_ref[start + row])
            )
        for r in range(TOGETHER):
            out_ref[group * TOGETHER + r] = results[r]
        return carry

    lax.fori_loop(0, rows // TOGETHER, body, 0)


def running_rows(first, count, half, pages, lens, queries, own, pool):
    max_pages = pages.shape[-1]
    return pl.pallas_call(
        functools.partial(running_kernel, first),
        out_shape=jax.ShapeDtypeStruct((count, 16, 128), jnp.bfloat16),
        in_specs=[SMEM, SMEM, SMEM, VMEM, VMEM, pl.BlockSpec(memory_space=pltpu.HBM)],
        out_specs=VMEM,
        scratch_shapes=[
            pltpu.VMEM((DEPTH, max_pages) + pool.shape[1:], jnp.bfloat16),
            pltpu.SemaphoreType.DMA((DEPTH, max_pages)),
        ],
        compiler_params=pltpu.CompilerParams(vmem_limit_bytes=48 * MIB),
        cost_estimate=cost(SMALL),
        name="running_rows",
    )(half, pages.reshape(-1), lens.reshape(-1), queries, own, pool)


RING = 4


def land_kernel(given, land_ref, query_ref, own_ref, *rest):
    contexts, rest = rest[:given], rest[given:]
    boxes, (out_ref, landed_ref, block, sems, space, box_sems) = rest[:20], rest[20:]
    slots = landed_ref.shape[0]
    first = out_ref.shape[0] - slots
    pairs = []
    for q in range(4):
        pairs += part_pairs(q, boxes[5 * q : 5 * q + 5], space, begin_of(q))
    copies = fetch(pairs, box_sems)
    done = 0
    for context in contexts:
        out_ref[done : done + context.shape[0]] = context[...]
        done += context.shape[0]
    space[begin_of(4)] = jnp.zeros((CHUNK, 256), jnp.bfloat16)
    for copy in copies:
        copy.wait()

    def write(slot):
        turn = slot % RING
        return pltpu.make_async_copy(block.at[turn], landed_ref.at[slot], sems.at[turn])

    def assemble(slot):
        turn = slot % RING
        length = land_ref[LENGTH, slot]
        for j in range(2):
            for k in range(0, PROMPT_CHUNKS, 4):
                held = [space[land_ref[PROMPT_CHUNKS * j + k + b, slot]] for b in range(4)]
                for b in range(4):
                    block[turn, j, k + b] = held[b]
        last = jnp.maximum(length - 1, 0) // CHUNK
        row = last * CHUNK + lax.broadcasted_iota(jnp.int32, (CHUNK, 256), 0)
        zero = jnp.zeros((CHUNK, 256), jnp.bfloat16)
        for j in range(2):
            block[turn, j, last] = jnp.where(row < length, block[turn, j, last], zero)

    def body(pair, carry):
        both = (2 * pair, 2 * pair + 1)

        @pl.when(2 * pair >= RING)
        def _():
            for slot in both:
                write(slot).wait()

        for slot in both:
            assemble(slot)
        for slot in both:
            write(slot).start()
        results = []
        for slot in both:
            blocks = [block[slot % RING, j].reshape(PROMPT_CHUNKS * CHUNK, 256) for j in range(2)]
            results.append(
                attend_row(query_ref[first + slot], *blocks, own_ref[first + slot], land_ref[LENGTH, slot])
            )
        for slot, result in zip(both, results):
            out_ref[first + slot] = result
        return carry

    lax.fori_loop(0, slots // 2, body, 0)
    for slot in range(slots - RING, slots):
        write(slot).wait()


def land_rows(slots, land, queries, own, contexts, boxes):
    return pl.pallas_call(
        functools.partial(land_kernel, len(contexts)),
        out_shape=(
            jax.ShapeDtypeStruct(queries.shape, jnp.bfloat16),
            jax.ShapeDtypeStruct((slots, 2, PROMPT_CHUNKS, CHUNK, 256), jnp.bfloat16),
        ),
        in_specs=[SMEM, VMEM, VMEM] + [VMEM] * len(contexts) + [ANY] * 20,
        out_specs=(VMEM, ANY),
        scratch_shapes=[
            pltpu.VMEM((RING, 2, PROMPT_CHUNKS, CHUNK, 256), jnp.bfloat16),
            pltpu.SemaphoreType.DMA((RING,)),
            pltpu.VMEM((begin_of(4) + 1, CHUNK, 256), jnp.bfloat16),
            pltpu.SemaphoreType.DMA((20,)),
        ],
        compiler_params=pltpu.CompilerParams(vmem_limit_bytes=32 * MIB),
        cost_estimate=cost(SMALL),
        name="land_rows",
    )(land, queries, own, *contexts, *boxes)


def routed(operands, kv, other, half, pages, lens, queries, own, pool):
    running = pages.shape[1]
    rows = queries.shape[0]
    (table,) = plan_call(first_plan_kernel, "first_plan", (8,), *operands)
    lists = home_lists(0, ROOM[0], table, kv, other)
    sent = [hop(value, order[0]) for value, order in zip(lists, ORDERS)]
    (where, table), _ = lax.optimization_barrier(((operands[0], table), lists))
    kept = home_lists(4, KEPT, table, kv, other)
    table, land = plan_call(plan_kernel, "plan", (16, 40), where, *operands[1:])
    boxes = [[k] for k in kept]
    contexts = []
    count = running // 2
    for phase in range(1, 4):
        turns = sorted(range(4), key=lambda q: region(phase, q) - KEPT[q])
        lists = [None] * 4
        for q in turns:
            boxes[q] = boxes[q] + [sent[q]]
            lists[q] = next_list(phase, q, table, boxes[q])
            table, _ = lax.optimization_barrier((table, lists[q]))
        if phase > 1:
            ready, _ = lax.optimization_barrier((half, lists))
            context = running_rows(len(contexts) * count, count, ready, pages, lens, queries, own, pool)
            contexts.append(context)
            table, land, _ = lax.optimization_barrier((table, land, context))
        sent = [hop(value, order[phase]) for value, order in zip(lists, ORDERS)]
    boxes = [box for q in range(4) for box in boxes[q] + [sent[q]]]
    context, landed = land_rows(rows - running, land, queries, own, contexts, boxes)
    return context, landed, land[OVER, 0]


def earlier_matches(labels, block_len, kind_count):
    onehot = (labels[:, None] == jnp.arange(kind_count, dtype=jnp.int32)[None, :]).astype(jnp.int32)
    blocks = onehot.reshape(labels.shape[0] // block_len, block_len, kind_count)
    before = jnp.cumsum(blocks, axis=1) - blocks
    return jnp.sum(before * blocks, axis=2).reshape(labels.shape[0])


def lookup(matches):
    prompt_ids = jnp.arange(matches.shape[1], dtype=jnp.int32)
    row_index = jnp.sum(jnp.where(matches, prompt_ids[None, :], 0), axis=1)
    return (row_index, jnp.any(matches, axis=1))


def pick_rows(table_rows, row_index, is_valid):
    picked = jnp.take(table_rows, row_index, axis=0)
    mask_shape = (is_valid.shape[0],) + (1,) * (picked.ndim - 1)
    return jnp.where(is_valid.reshape(mask_shape), picked, jnp.zeros_like(picked))


def any_fill(targets, prompt_lens, kv, queries, own):
    prompt_kv = kv.reshape(16, 1, 512, 256)
    groups = lax.axis_size("grp")
    group_id = lax.axis_index("grp")
    half_id = lax.axis_index("tp") % 2
    block_len = prompt_kv.shape[0]
    prompt_count = targets.shape[0]
    span_len = prompt_kv.shape[2]
    capacity = max(2, block_len // groups)
    source = jnp.arange(prompt_count, dtype=jnp.int32) // block_len
    arrival = earlier_matches(targets, prompt_count, 2 * groups)
    slot_ids = jnp.arange(block_len, dtype=jnp.int32)
    land_match = (targets[None, :] == 2 * group_id + half_id) & (
        arrival[None, :] == slot_ids[:, None]
    )
    land_len = jnp.sum(jnp.where(land_match, prompt_lens[None, :], 0), axis=1)
    land_live = jnp.arange(span_len, dtype=jnp.int32)[None, :] < land_len[:, None]
    land_index, land_valid = lookup(land_match)
    outgoing = source == group_id
    dest_ids = jnp.arange(groups, dtype=jnp.int32)
    cap_ids = jnp.arange(capacity, dtype=jnp.int32)
    partner = hop(prompt_kv, Z)
    pair_kv = jnp.where(
        half_id == 0,
        jnp.concatenate([prompt_kv, partner], axis=1),
        jnp.concatenate([partner, prompt_kv], axis=1),
    )
    within = earlier_matches(targets, block_len, 2 * groups)
    send_match = (
        outgoing[None, None, :]
        & (targets[None, None, :] == (2 * dest_ids + half_id)[:, None, None])
        & (within[None, None, :] == cap_ids[None, :, None])
    )
    send_index, send_valid = lookup(send_match.reshape(groups * capacity, prompt_count))
    send_index = jnp.where(send_valid, send_index - group_id * block_len, 0)
    outbox = pick_rows(pair_kv, send_index, send_valid)
    outbox = outbox.reshape((groups, capacity) + outbox.shape[1:])
    inbound = lax.all_to_all(outbox, "grp", split_axis=0, concat_axis=0, tiled=True)
    inbound = inbound.reshape((groups * capacity,) + inbound.shape[2:])
    entry_ids = source * capacity + within
    landed = pick_rows(inbound, jnp.take(entry_ids, land_index), land_valid)
    landed = jnp.where(land_live[:, None, :, None], landed, jnp.zeros_like(landed))
    handed = jnp.stack(
        [
            attend_row(queries[s], landed[s, 0], landed[s, 1], own[s], land_len[s])
            for s in range(block_len)
        ]
    )
    return handed, landed.reshape(block_len, 2, PROMPT_CHUNKS, CHUNK, 256)


def local(targets, prompt_lens, prompt_kv, cache_pool, block_table, cache_lens, queries, new_kv):
    group = lax.axis_index("grp")
    member = lax.axis_index("tp")
    kv = prompt_kv.reshape(OWN_CHUNKS, CHUNK, 256)
    other = hop(kv, CORE)
    operands = plan_operands(targets, prompt_lens, group, member)
    half = (member % 2).astype(jnp.int32).reshape(1)
    rows = queries.shape[2]
    running = block_table.shape[2]
    by_head = queries.reshape(rows, 16, 128)
    own = new_kv[0, 0]
    context, landed, over = routed(
        operands, kv, other, half, block_table[0], cache_lens[0], by_head, own, cache_pool[0, 0]
    )

    def again(carry):
        handed, landed = any_fill(targets, prompt_lens, kv, by_head[running:], own[running:])
        return carry[0].at[running:].set(handed), landed, jnp.zeros((), jnp.int32)

    context, landed, _ = lax.while_loop(lambda carry: carry[2] > 0, again, (context, landed, over))
    return (
        context.reshape(1, 1, rows, queries.shape[3]),
        landed.reshape(1, 1, 16, 2, 512, 256),
    )


def solution(mesh):
    placed = (
        P(),
        P(),
        P("grp", "tp", None, None),
        P("grp", "tp", None, None, None, None),
        P("grp", None, None, None),
        P("grp", None, None),
        P("grp", "tp", None, None),
        P("grp", "tp", None, None, None),
    )
    return jax.shard_map(
        local,
        mesh=mesh,
        in_specs=placed,
        out_specs=(P("grp", "tp", None, None), P("grp", "tp", None, None, None, None)),
        check_vma=False,
    )
```

```python
import functools
import math

import jax
import jax.numpy as jnp
import numpy as np
from jax import lax
from jax.experimental import pallas as pl
from jax.experimental.pallas import tpu as pltpu
from jax.sharding import PartitionSpec as P

CHUNK = 32
PROMPT_CHUNKS = 16
OWN_CHUNKS = 256
HOME = 512
X, YA, YB, Z, CORE = 1, 2, 4, 8, 16
ORDERS = ((X, Z, YB, YA), (YA, YB, Z, X), (YB, YA, X, Z), (Z, X, YA, YB))
DEAL = (2, 0, 1, 3, 2, 0, 1, 2, 3, 0, 1, 2, 0, 1, 3, 2)
SHARES = tuple(sum(1 << k for k, part in enumerate(DEAL) if part == q) for q in range(4))
ROOM = ((40, 40, 48, 36), (48, 44, 48, 48), (64, 52, 48, 52), (72, 72, 68, 60))
MIB = 1024 * 1024
SMALL = 4096


KEPT = (52, 52, 64, 40)


def region(phase, part):
    return KEPT[part] + sum(rooms[part] for rooms in ROOM[:phase])


def begin_of(part, phase):
    return sum(region(phase, q) for q in range(part))


LATE_BEGIN = tuple(sum(ROOM[3][:q]) for q in range(5))


def flipped(group, mask):
    x, core, y = (group >> 1) & 1, group & 1, group >> 2
    if mask & X:
        x ^= 1
    if mask & YA:
        y ^= 1
    if mask & YB:
        y = 3 - y
    if mask & CORE:
        core ^= 1
    return (y << 2) | (x << 1) | core


def hop(value, axis):
    if axis == Z:
        return lax.ppermute(value, "tp", [(t, t ^ 1) for t in range(lax.axis_size("tp"))])
    return lax.ppermute(value, "grp", [(g, flipped(g, axis)) for g in range(lax.axis_size("grp"))])


def node_of(group, parity):
    y = group >> 2
    return (
        ((group >> 1) & 1)
        | (((y ^ (y >> 1)) & 1) << 1)
        | (((y >> 1) & 1) << 2)
        | (parity << 3)
        | ((group & 1) << 4)
    )


def bits_set(word):
    word = word - ((word >> 1) & 0x5555)
    word = (word & 0x3333) + ((word >> 2) & 0x3333)
    word = (word + (word >> 4)) & 0x0F0F
    return (word + (word >> 8)) & 0x1F


def turned(share, by):
    return ((share | (share << 16)) >> by) & 0xFFFF


def below(k):
    return (1 << k) - 1


def exact(values):
    return values.astype(jnp.float32).astype(jnp.bfloat16)


def dot(left, right):
    return jnp.dot(left, right, preferred_element_type=jnp.float32)


def standing(row):
    size = row.shape[1]
    down = lax.broadcasted_iota(jnp.int32, (size, size), 0)
    along = lax.broadcasted_iota(jnp.int32, (size, size), 1)
    return jnp.sum(jnp.where(down == along, row, 0), axis=1, keepdims=True)


def ends_of(targets, prompt, parity):
    start = node_of(prompt >> 4, parity)
    end = node_of(targets >> 1, targets & 1)
    start = (start & 15) | (end & CORE)
    return start, start ^ end


def earlier_rows(size):
    down = lax.broadcasted_iota(jnp.int32, (size, size), 0)
    along = lax.broadcasted_iota(jnp.int32, (size, size), 1)
    return exact(jnp.where(along < down, 1, 0))


SENT, RECEIVED, SLOTS, HELD = 0, 16, 32, 36


def first_plan_kernel(where_ref, targets_ref, lens_ref, const_ref, table_ref):
    me, group = where_ref[0], where_ref[2]
    local = lax.broadcasted_iota(jnp.int32, (32, 1), 0)
    prompt = 16 * (group & ~1) + local
    match = lax.broadcasted_iota(jnp.int32, (32, targets_ref.shape[1]), 1) == prompt
    targets = jnp.sum(jnp.where(match, targets_ref[...], 0), axis=1, keepdims=True)
    lens = jnp.sum(jnp.where(match, lens_ref[...], 0), axis=1, keepdims=True)
    start, ways = ends_of(targets, prompt, (me >> 3) & 1)
    bit, share = const_ref[1:2, :], const_ref[3:4, :]
    lane = lax.broadcasted_iota(jnp.int32, (1, 64), 1)
    word = turned(share, (prompt * 5) & 15) & below((lens + (CHUNK - 1)) >> 5)
    goes = (lane < 4) & ((ways & bit) != 0) | (lane >= HELD) & (lane < HELD + 4)
    goes = goes & (start == me)
    place = dot(earlier_rows(32), exact(jnp.where(goes, bits_set(word), 0))).astype(jnp.int32)
    place = jnp.where(goes, place, -256)

    def each_chunk(values):
        wide = jnp.broadcast_to(values[:, None, :], (32, PROMPT_CHUNKS, values.shape[1]))
        return wide.reshape(32 * PROMPT_CHUNKS, values.shape[1])

    unit = lax.broadcasted_iota(jnp.int32, (HOME, 1), 0)
    k = unit & 15
    home = jnp.where(((unit >> 8) & 1) == (group & 1), 0, OWN_CHUNKS) + (unit & (OWN_CHUNKS - 1))
    words = each_chunk(word)
    spot = jnp.where(((words >> k) & 1) != 0, each_chunk(place) + bits_set(words & below(k)), -1)
    slot = lax.broadcasted_iota(jnp.int32, (1, 128), 1)
    rows = []
    for c in (0, 1, 2, 3, HELD, HELD + 1, HELD + 2, HELD + 3):
        rows.append(jnp.sum(jnp.where(spot[:, c : c + 1] == slot, home, 0), axis=0, keepdims=True))
    table_ref[...] = jnp.concatenate(rows, axis=0)


LATE, LENGTH, OVER = 32, 64, 65


def plan_kernel(where_ref, targets_ref, lens_ref, const_ref, slots_ref, land_ref):
    me, mine = where_ref[0], where_ref[1]
    row_t = jnp.concatenate([targets_ref[...], targets_ref[...]], axis=1)
    items = row_t.shape[1]
    prompts = items // 2
    col_t, col_l = standing(targets_ref[...]), standing(lens_ref[...])
    col_t, col_l = (jnp.concatenate([c, c], axis=0) for c in (col_t, col_l))
    item = lax.broadcasted_iota(jnp.int32, (items, 1), 0)
    prompt, parity = item & (prompts - 1), item >> 8
    start, ways = ends_of(col_t, prompt, parity)
    turn = (prompt * 5) & 15
    routed, bit, sender, share, room = (const_ref[k : k + 1, :] for k in range(5))
    lane = lax.broadcasted_iota(jnp.int32, (1, 64), 1)
    keeps = (lane >= HELD) & (lane < HELD + 4)
    weight = bits_set(turned(share, turn) & below((col_l + (CHUNK - 1)) >> 5))
    crosses = ((ways & bit) != 0) & (lane < SLOTS) | keeps
    listed = crosses & ((start ^ (ways & routed)) == (me ^ sender))
    landing = (col_t == mine) & (lane == SLOTS + parity)
    amount = jnp.where(listed, weight, jnp.where(landing, 1, 0))
    place = dot(earlier_rows(items), exact(amount)).astype(jnp.int32)

    everyone = exact(jnp.where(crosses, weight, 0))
    row_item = lax.broadcasted_iota(jnp.int32, (1, items), 1)
    row_start, row_ways = ends_of(row_t, row_item & (prompts - 1), row_item >> 8)
    nodes = lax.broadcasted_iota(jnp.int32, (32, 1), 0)
    ways_done = sorted({sum(order[:p]) for order in ORDERS for p in range(4)})
    present = [jnp.where(nodes == (row_start ^ (row_ways & done)), 1, 0) for done in ways_done]
    held = dot(exact(jnp.concatenate(present, axis=0)), everyone)
    need = jnp.zeros((1, 64), jnp.float32)
    for k, done in enumerate(ways_done):
        most = jnp.max(held[32 * k : 32 * k + 32], axis=0, keepdims=True)
        need = jnp.where(routed == done, most, need)
    over = (need.astype(jnp.int32) > room) & ((lane < RECEIVED) | keeps)
    over = jnp.max(jnp.where(over, 1, 0), axis=1, keepdims=True)

    bases = [[place[:, HELD + q : HELD + q + 1] for q in range(4)]]
    for p in range(4):
        came = []
        for q in range(4):
            c = RECEIVED + 4 * p + q
            moved = (ways & ORDERS[q][p]) != 0
            came.append(jnp.where(moved, region(p, q) + place[:, c : c + 1], bases[p][q]))
        bases.append(came)

    slot = lax.broadcasted_iota(jnp.int32, (1, 128), 1)

    def sources(p, q):
        c = 4 * p + q
        first = jnp.where(listed[:, c : c + 1], place[:, c : c + 1], 1 << 20)
        offset = slot - first
        inside = (offset >= 0) & (offset < weight[:, c : c + 1])
        found = jnp.where(inside, offset + bases[p][q], 0)
        return jnp.minimum(jnp.sum(found, axis=0, keepdims=True), region(p, q) - 1)

    slots_ref[...] = jnp.concatenate(
        [jnp.zeros((4, 128), jnp.int32)] + [sources(p, q) for p in range(1, 4) for q in range(4)], axis=0
    )

    rank = jnp.where(parity == 0, place[:, SLOTS : SLOTS + 1], place[:, SLOTS + 1 : SLOTS + 2])
    rank = jnp.where(col_t == mine, rank, -1)
    lands = [rank[:prompts] == slot, rank[prompts:] == slot]

    def landed(value, j):
        return jnp.sum(jnp.where(lands[j], value[j * prompts : (j + 1) * prompts], 0), axis=0, keepdims=True)

    length = landed(col_l, 0)
    live = (length + (CHUNK - 1)) >> 5
    by = landed(turn, 0)
    k = lax.broadcasted_iota(jnp.int32, (PROMPT_CHUNKS, 1), 0)
    early, late = [], []
    for j in range(2):
        here = jnp.zeros((PROMPT_CHUNKS, 128), jnp.int32)
        last = jnp.zeros((PROMPT_CHUNKS, 128), jnp.int32)
        for q in range(4):
            c = RECEIVED + 12 + q
            moves = landed(jnp.where((ways & ORDERS[q][3]) != 0, 1, 0), j)
            held = landed(bases[3][q], j)
            comes = landed(place[:, c : c + 1], j)
            part = turned(jnp.full_like(by, SHARES[q]), by)
            rest = bits_set(part & below(k))
            dealt = (part >> k) & 1
            spot = begin_of(q, 3) + jnp.minimum(held + rest, region(3, q) - 1)
            here += dealt * jnp.where(moves != 0, begin_of(4, 3), spot)
            spot = LATE_BEGIN[q] + jnp.minimum(comes + rest, ROOM[3][q] - 1)
            last += dealt * jnp.where(moves != 0, spot, -1)
        early.append(jnp.where(k < live, here, begin_of(4, 3)))
        late.append(jnp.where(k < live, last, -1))
    rows = [length, jnp.broadcast_to(over, (1, 128)), jnp.zeros((6, 128), jnp.int32)]
    land_ref[...] = jnp.concatenate(early + late + rows, axis=0)


def plan_const():
    const = np.zeros((8, 64), np.int32)
    for p in range(4):
        for q, order in enumerate(ORDERS):
            for first, sender in ((SENT, 0), (RECEIVED, order[p])):
                const[:5, first + 4 * p + q] = (sum(order[:p]), order[p], sender, SHARES[q], ROOM[p][q])
    for q in range(4):
        const[3:5, HELD + q] = (SHARES[q], KEPT[q])
    return jnp.asarray(const)


def plan_call(kernel, name, rows, *operands):
    vmem = pl.BlockSpec(memory_space=pltpu.VMEM)
    return pl.pallas_call(
        kernel,
        out_shape=tuple(jax.ShapeDtypeStruct((r, 128), jnp.int32) for r in rows),
        in_specs=[pl.BlockSpec(memory_space=pltpu.SMEM), vmem, vmem, vmem],
        out_specs=(vmem,) * len(rows),
        compiler_params=pltpu.CompilerParams(vmem_limit_bytes=24 * MIB),
        cost_estimate=cost(SMALL),
        name=name,
    )(*operands)


def plan_operands(targets, prompt_lens, group, member):
    where = jnp.stack([node_of(group, member % 2), 2 * group + member % 2, group]).astype(jnp.int32)
    return where, targets.reshape(1, -1), prompt_lens.reshape(1, -1), plan_const()


def fetch(pairs, sems):
    copies = [
        pltpu.make_async_copy(source, target, sems.at[k]) for k, (source, target) in enumerate(pairs)
    ]
    for copy in copies:
        copy.start()
    return copies


def gather_chunks(table_ref, row, out_ref, pick):
    batch = 4

    def body(s, carry):
        first = s * batch
        held = [pick(table_ref[row, first + b]) for b in range(batch)]
        for b in range(batch):
            out_ref[first + b] = held[b]
        return carry

    lax.fori_loop(0, out_ref.shape[0] // batch, body, 0, unroll=2)


SMEM = pl.BlockSpec(memory_space=pltpu.SMEM)
ANY = pl.BlockSpec(memory_space=pl.ANY)
VMEM = pl.BlockSpec(memory_space=pltpu.VMEM)


def chunks_of(count):
    return jax.ShapeDtypeStruct((count, CHUNK, 256), jnp.bfloat16)


def cost(bytes_accessed, flops=0):
    return pl.CostEstimate(flops=flops, bytes_accessed=bytes_accessed, transcendentals=0)


def home_kernel(rows, table_ref, kv_ref, other_ref, *outs):
    def pick(i):
        row = i & (OWN_CHUNKS - 1)
        return jnp.where(i < OWN_CHUNKS, kv_ref[row], other_ref[row])

    for q in range(4):
        gather_chunks(table_ref, rows + q, outs[q], pick)


def home_lists(rows, rooms, table, kv, other):
    return pl.pallas_call(
        functools.partial(home_kernel, rows),
        out_shape=tuple(chunks_of(room) for room in rooms),
        in_specs=[SMEM, VMEM, VMEM],
        out_specs=(VMEM,) * 4,
        compiler_params=pltpu.CompilerParams(vmem_limit_bytes=24 * MIB),
        cost_estimate=cost(SMALL),
        name="home_lists",
    )(table, kv, other)


def part_pairs(part, boxes, space, begin=0):
    pairs = []
    for k, box in enumerate(boxes):
        at = begin + (region(k - 1, part) if k else 0)
        pairs.append((box, space.at[pl.ds(at, box.shape[0])]))
    return pairs


def next_kernel(phase, table_ref, *rest):
    each = phase + 1
    boxes, outs, space, sems = rest[: 4 * each], rest[4 * each : 4 * each + 4], rest[4 * each + 4], rest[4 * each + 5]
    copies = []
    for q in range(4):
        pairs = part_pairs(q, boxes[each * q : each * q + each], space, begin_of(q, phase))
        copies.append(fetch(pairs, sems.at[q]))
    for q in range(4):
        for copy in copies[q]:
            copy.wait()
        begin = begin_of(q, phase)
        gather_chunks(table_ref, 4 * phase + q, outs[q], lambda i: space[begin + i])


def next_lists(phase, table, boxes):
    flat = [box for part in boxes for box in part]
    return pl.pallas_call(
        functools.partial(next_kernel, phase),
        out_shape=tuple(chunks_of(room) for room in ROOM[phase]),
        in_specs=[SMEM] + [ANY] * len(flat),
        out_specs=(VMEM,) * 4,
        scratch_shapes=[
            pltpu.VMEM((begin_of(4, phase), CHUNK, 256), jnp.bfloat16),
            pltpu.SemaphoreType.DMA((4, phase + 1)),
        ],
        compiler_params=pltpu.CompilerParams(vmem_limit_bytes=28 * MIB),
        cost_estimate=cost(SMALL),
        name="next_lists",
    )(table, *flat)


def attend_row(query, first, second, own, length):
    scaling = 1.0 / math.sqrt(query.shape[1])
    upper = lax.broadcasted_iota(jnp.int32, query.shape, 0) < 8
    zero = jnp.zeros_like(query)
    wide = jnp.concatenate([jnp.where(upper, query, zero), jnp.where(upper, zero, query)], axis=1)
    keys = jnp.concatenate([first[:, :128], second[:, :128]], axis=1)
    values = jnp.concatenate([first[:, 128:], second[:, 128:]], axis=1)
    scores = (
        lax.dot_general(wide, keys, (((1,), (1,)), ((), ())), preferred_element_type=jnp.float32)
        * scaling
    )
    own = own.astype(jnp.float32)
    own_key = jnp.where(upper, own[0:1, :128], own[1:2, :128])
    own_value = jnp.where(upper, own[0:1, 128:], own[1:2, 128:])
    own_score = jnp.sum(query.astype(jnp.float32) * own_key, axis=1, keepdims=True) * scaling
    live = lax.broadcasted_iota(jnp.int32, scores.shape, 1) < length
    scores = jnp.where(live, scores, -jnp.inf)
    row_max = jnp.maximum(jnp.max(scores, axis=1, keepdims=True), own_score)
    weights = jnp.where(live, jnp.exp(scores - row_max), 0.0)
    own_weight = jnp.exp(own_score - row_max)
    denominator = jnp.sum(weights, axis=1, keepdims=True) + own_weight
    both = jnp.dot(weights.astype(jnp.bfloat16), values, preferred_element_type=jnp.float32)
    mixture = jnp.where(upper, both[:, :128], both[:, 128:])
    mixture += own_weight.astype(jnp.bfloat16).astype(jnp.float32) * own_value
    return mixture / denominator


def lay_rows(result, out_ref, first, rows):
    for row in range(0, rows, 16):
        for head in range(16):
            values = result[pl.ds(16 * row + head, 16, stride=16)]
            out_ref[first + row : first + row + 16, 128 * head : 128 * head + 128] = values.astype(jnp.bfloat16)


TOGETHER = 4
DEPTH = 4 * TOGETHER


def running_kernel(first, half_ref, pages_ref, lens_ref, query_ref, own_ref, pool_ref, out_ref, held, result, sems):
    rows = out_ref.shape[0]
    all_rows = lens_ref.shape[0] // 2
    max_pages = held.shape[1]
    start = half_ref[0] * all_rows + first

    def each_page(row, action):
        slot = row % DEPTH
        for c in range(max_pages):
            page = pages_ref[(start + row) * max_pages + c]
            action(pltpu.make_async_copy(pool_ref.at[page], held.at[slot, c], sems.at[slot, c]))

    def begin(group):
        for r in range(TOGETHER):
            each_page(group * TOGETHER + r, lambda copy: copy.start())

    ahead = DEPTH // TOGETHER - 1
    for group in range(ahead):
        begin(group)

    def body(group, carry):
        @pl.when(group + ahead < rows // TOGETHER)
        def _():
            begin(group + ahead)

        for r in range(TOGETHER):
            each_page(group * TOGETHER + r, lambda copy: copy.wait())
        results = []
        for r in range(TOGETHER):
            row = group * TOGETHER + r
            slot = row % DEPTH
            blocks = [held[slot, :, j].reshape(max_pages * 64, 256) for j in range(2)]
            results.append(
                attend_row(query_ref[first + row], *blocks, own_ref[first + row], lens_ref[start + row])
            )
        for r in range(TOGETHER):
            result[pl.ds((group * TOGETHER + r) * 16, 16)] = results[r]
        return carry

    lax.fori_loop(0, rows // TOGETHER, body, 0)
    lay_rows(result, out_ref, 0, rows)


def running_rows(first, count, half, pages, lens, queries, own, pool):
    max_pages = pages.shape[-1]
    return pl.pallas_call(
        functools.partial(running_kernel, first),
        out_shape=jax.ShapeDtypeStruct((count, 2048), jnp.bfloat16),
        in_specs=[SMEM, SMEM, SMEM, VMEM, VMEM, pl.BlockSpec(memory_space=pltpu.HBM)],
        out_specs=VMEM,
        scratch_shapes=[
            pltpu.VMEM((DEPTH, max_pages) + pool.shape[1:], jnp.bfloat16),
            pltpu.VMEM((count * 16, 128), jnp.float32),
            pltpu.SemaphoreType.DMA((DEPTH, max_pages)),
        ],
        compiler_params=pltpu.CompilerParams(vmem_limit_bytes=48 * MIB),
        cost_estimate=cost(SMALL),
        name="running_rows",
    )(half, pages.reshape(-1), lens.reshape(-1), queries, own, pool)


RING = 4


def early_kernel(land_ref, *rest):
    boxes, (landed_ref, block, sems, space, box_sems) = rest[:16], rest[16:]
    slots = landed_ref.shape[0]
    pairs = []
    for q in range(4):
        pairs += part_pairs(q, boxes[4 * q : 4 * q + 4], space, begin_of(q, 3))
    copies = fetch(pairs, box_sems)
    space[begin_of(4, 3)] = jnp.zeros((CHUNK, 256), jnp.bfloat16)
    for copy in copies:
        copy.wait()

    def write(slot):
        turn = slot % RING
        return pltpu.make_async_copy(block.at[turn], landed_ref.at[slot], sems.at[turn])

    def body(slot, carry):
        @pl.when(slot >= RING)
        def _():
            write(slot).wait()

        for j in range(2):
            for k in range(0, PROMPT_CHUNKS, 4):
                held = [space[land_ref[PROMPT_CHUNKS * j + k + b, slot]] for b in range(4)]
                for b in range(4):
                    block[slot % RING, j, k + b] = held[b]
        write(slot).start()
        return carry

    lax.fori_loop(0, slots, body, 0)
    for slot in range(slots - RING, slots):
        write(slot).wait()


def early_rows(slots, land, boxes):
    return pl.pallas_call(
        early_kernel,
        out_shape=jax.ShapeDtypeStruct((slots, 2, PROMPT_CHUNKS, CHUNK, 256), jnp.bfloat16),
        in_specs=[SMEM] + [ANY] * 16,
        out_specs=ANY,
        scratch_shapes=[
            pltpu.VMEM((RING, 2, PROMPT_CHUNKS, CHUNK, 256), jnp.bfloat16),
            pltpu.SemaphoreType.DMA((RING,)),
            pltpu.VMEM((begin_of(4, 3) + 1, CHUNK, 256), jnp.bfloat16),
            pltpu.SemaphoreType.DMA((16,)),
        ],
        compiler_params=pltpu.CompilerParams(vmem_limit_bytes=28 * MIB),
        cost_estimate=cost(SMALL),
        name="early_rows",
    )(land, *boxes)


LAND_RING = 8


def land_kernel(given, land_ref, query_ref, own_ref, early_ref, *rest):
    contexts, rest = rest[:given], rest[given:]
    boxes, (out_ref, landed_ref, block, result, in_sems, sems, space, box_sems) = rest[:4], rest[4:]
    slots = landed_ref.shape[0]
    first = out_ref.shape[0] - slots

    def read(slot):
        turn = slot % LAND_RING
        return pltpu.make_async_copy(early_ref.at[slot], block.at[turn], in_sems.at[turn])

    def write(slot):
        turn = slot % LAND_RING
        return pltpu.make_async_copy(block.at[turn], landed_ref.at[slot], sems.at[turn])

    copies = fetch([(box, space.at[pl.ds(LATE_BEGIN[q], box.shape[0])]) for q, box in enumerate(boxes)], box_sems)
    for slot in range(4):
        read(slot).start()
    done = 0
    for context in contexts:
        out_ref[done : done + context.shape[0]] = context[...]
        done += context.shape[0]
    for copy in copies:
        copy.wait()

    def complete(slot):
        turn = slot % LAND_RING
        length = land_ref[LENGTH, slot]
        for j in range(2):
            for k in range(0, PROMPT_CHUNKS, 2):
                held = []
                for b in range(2):
                    source = land_ref[LATE + PROMPT_CHUNKS * j + k + b, slot]
                    held.append(jnp.where(source >= 0, space[jnp.maximum(source, 0)], block[turn, j, k + b]))
                for b in range(2):
                    block[turn, j, k + b] = held[b]
        last = jnp.maximum(length - 1, 0) // CHUNK
        row = last * CHUNK + lax.broadcasted_iota(jnp.int32, (CHUNK, 256), 0)
        zero = jnp.zeros((CHUNK, 256), jnp.bfloat16)
        for j in range(2):
            block[turn, j, last] = jnp.where(row < length, block[turn, j, last], zero)

    def body(pair, carry):
        both = (2 * pair, 2 * pair + 1)

        @pl.when(2 * pair + 4 < slots)
        def _():
            for slot in both:

                @pl.when(slot + 4 >= LAND_RING)
                def _():
                    write(slot + 4).wait()

                read(slot + 4).start()

        for slot in both:
            read(slot).wait()
        for slot in both:
            complete(slot)
        for slot in both:
            write(slot).start()
        results = []
        for slot in both:
            blocks = [block[slot % LAND_RING, j].reshape(PROMPT_CHUNKS * CHUNK, 256) for j in range(2)]
            results.append(
                attend_row(query_ref[first + slot], *blocks, own_ref[first + slot], land_ref[LENGTH, slot])
            )
        for slot, value in zip(both, results):
            result[pl.ds(16 * slot, 16)] = value
        return carry

    lax.fori_loop(0, slots // 2, body, 0)
    lay_rows(result, out_ref, first, slots)
    for slot in range(slots - LAND_RING, slots):
        write(slot).wait()


def land_rows(land, queries, own, early, contexts, boxes):
    return pl.pallas_call(
        functools.partial(land_kernel, len(contexts)),
        out_shape=(
            jax.ShapeDtypeStruct((queries.shape[0], 2048), jnp.bfloat16),
            jax.ShapeDtypeStruct(early.shape, jnp.bfloat16),
        ),
        in_specs=[SMEM, VMEM, VMEM, ANY] + [VMEM] * len(contexts) + [ANY] * 4,
        out_specs=(VMEM, ANY),
        scratch_shapes=[
            pltpu.VMEM((LAND_RING,) + early.shape[1:], jnp.bfloat16),
            pltpu.VMEM((16 * early.shape[0], 128), jnp.float32),
            pltpu.SemaphoreType.DMA((LAND_RING,)),
            pltpu.SemaphoreType.DMA((LAND_RING,)),
            pltpu.VMEM((LATE_BEGIN[4], CHUNK, 256), jnp.bfloat16),
            pltpu.SemaphoreType.DMA((4,)),
        ],
        compiler_params=pltpu.CompilerParams(vmem_limit_bytes=24 * MIB),
        cost_estimate=cost(SMALL),
        name="land_rows",
    )(land, queries, own, early, *contexts, *boxes)


def routed(operands, kv, other, half, pages, lens, queries, own, pool):
    running = pages.shape[1]
    rows = queries.shape[0]
    (table,) = plan_call(first_plan_kernel, "first_plan", (8,), *operands)
    lists = home_lists(0, ROOM[0], table, kv, other)
    sent = [hop(value, order[0]) for value, order in zip(lists, ORDERS)]
    (where, table), _ = lax.optimization_barrier(((operands[0], table), lists))
    kept = home_lists(4, KEPT, table, kv, other)
    table, land = plan_call(plan_kernel, "plan", (16, 72), where, *operands[1:])
    boxes = [[k] for k in kept]
    contexts = []
    done = 0
    for phase, count in ((1, running // 4), (2, running // 2), (3, running // 4)):
        boxes = [part + [box] for part, box in zip(boxes, sent)]
        lists = next_lists(phase, table, boxes)
        sent = [hop(value, order[phase]) for value, order in zip(lists, ORDERS)]
        ready, _ = lax.optimization_barrier((half, lists))
        contexts.append(running_rows(done, count, ready, pages, lens, queries, own, pool))
        done += count
        if phase == 3:
            land, _ = lax.optimization_barrier((land, lists))
            early = early_rows(rows - running, land, [box for part in boxes for box in part])
            sent, _, early = lax.optimization_barrier((sent, contexts, early))
        else:
            table, _ = lax.optimization_barrier((table, contexts))
    context, landed = land_rows(land, queries, own, early, contexts, sent)
    return context, landed, land[OVER, 0]


def earlier_matches(labels, block_len, kind_count):
    onehot = (labels[:, None] == jnp.arange(kind_count, dtype=jnp.int32)[None, :]).astype(jnp.int32)
    blocks = onehot.reshape(labels.shape[0] // block_len, block_len, kind_count)
    before = jnp.cumsum(blocks, axis=1) - blocks
    return jnp.sum(before * blocks, axis=2).reshape(labels.shape[0])


def lookup(matches):
    prompt_ids = jnp.arange(matches.shape[1], dtype=jnp.int32)
    row_index = jnp.sum(jnp.where(matches, prompt_ids[None, :], 0), axis=1)
    return (row_index, jnp.any(matches, axis=1))


def pick_rows(table_rows, row_index, is_valid):
    picked = jnp.take(table_rows, row_index, axis=0)
    mask_shape = (is_valid.shape[0],) + (1,) * (picked.ndim - 1)
    return jnp.where(is_valid.reshape(mask_shape), picked, jnp.zeros_like(picked))


def any_fill(targets, prompt_lens, kv, queries, own):
    prompt_kv = kv.reshape(16, 1, 512, 256)
    groups = lax.axis_size("grp")
    group_id = lax.axis_index("grp")
    half_id = lax.axis_index("tp") % 2
    block_len = prompt_kv.shape[0]
    prompt_count = targets.shape[0]
    span_len = prompt_kv.shape[2]
    capacity = max(2, block_len // groups)
    source = jnp.arange(prompt_count, dtype=jnp.int32) // block_len
    arrival = earlier_matches(targets, prompt_count, 2 * groups)
    slot_ids = jnp.arange(block_len, dtype=jnp.int32)
    land_match = (targets[None, :] == 2 * group_id + half_id) & (
        arrival[None, :] == slot_ids[:, None]
    )
    land_len = jnp.sum(jnp.where(land_match, prompt_lens[None, :], 0), axis=1)
    land_live = jnp.arange(span_len, dtype=jnp.int32)[None, :] < land_len[:, None]
    land_index, land_valid = lookup(land_match)
    outgoing = source == group_id
    dest_ids = jnp.arange(groups, dtype=jnp.int32)
    cap_ids = jnp.arange(capacity, dtype=jnp.int32)
    partner = hop(prompt_kv, Z)
    pair_kv = jnp.where(
        half_id == 0,
        jnp.concatenate([prompt_kv, partner], axis=1),
        jnp.concatenate([partner, prompt_kv], axis=1),
    )
    within = earlier_matches(targets, block_len, 2 * groups)
    send_match = (
        outgoing[None, None, :]
        & (targets[None, None, :] == (2 * dest_ids + half_id)[:, None, None])
        & (within[None, None, :] == cap_ids[None, :, None])
    )
    send_index, send_valid = lookup(send_match.reshape(groups * capacity, prompt_count))
    send_index = jnp.where(send_valid, send_index - group_id * block_len, 0)
    outbox = pick_rows(pair_kv, send_index, send_valid)
    outbox = outbox.reshape((groups, capacity) + outbox.shape[1:])
    inbound = lax.all_to_all(outbox, "grp", split_axis=0, concat_axis=0, tiled=True)
    inbound = inbound.reshape((groups * capacity,) + inbound.shape[2:])
    entry_ids = source * capacity + within
    landed = pick_rows(inbound, jnp.take(entry_ids, land_index), land_valid)
    landed = jnp.where(land_live[:, None, :, None], landed, jnp.zeros_like(landed))
    handed = jnp.stack(
        [
            attend_row(queries[s], landed[s, 0], landed[s, 1], own[s], land_len[s])
            for s in range(block_len)
        ]
    )
    return handed, landed.reshape(block_len, 2, PROMPT_CHUNKS, CHUNK, 256)


def local(targets, prompt_lens, prompt_kv, cache_pool, block_table, cache_lens, queries, new_kv):
    group = lax.axis_index("grp")
    member = lax.axis_index("tp")
    kv = prompt_kv.reshape(OWN_CHUNKS, CHUNK, 256)
    other = hop(kv, CORE)
    operands = plan_operands(targets, prompt_lens, group, member)
    half = (member % 2).astype(jnp.int32).reshape(1)
    rows = queries.shape[2]
    running = block_table.shape[2]
    by_head = queries.reshape(rows, 16, 128)
    own = new_kv[0, 0]
    context, landed, over = routed(
        operands, kv, other, half, block_table[0], cache_lens[0], by_head, own, cache_pool[0, 0]
    )

    def again(carry):
        handed, landed = any_fill(targets, prompt_lens, kv, by_head[running:], own[running:])
        handed = handed.astype(jnp.bfloat16).reshape(rows - running, -1)
        return carry[0].at[running:].set(handed), landed, jnp.zeros((), jnp.int32)

    context, landed, _ = lax.while_loop(lambda carry: carry[2] > 0, again, (context, landed, over))
    return (
        context.reshape(1, 1, rows, queries.shape[3]),
        landed.reshape(1, 1, 16, 2, 512, 256),
    )


def solution(mesh):
    placed = (
        P(),
        P(),
        P("grp", "tp", None, None),
        P("grp", "tp", None, None, None, None),
        P("grp", None, None, None),
        P("grp", None, None),
        P("grp", "tp", None, None),
        P("grp", "tp", None, None, None),
    )
    return jax.shard_map(
        local,
        mesh=mesh,
        in_specs=placed,
        out_specs=(P("grp", "tp", None, None), P("grp", "tp", None, None, None, None)),
        check_vma=False,
    )
```

```python
import functools
import math

import jax
import jax.numpy as jnp
import numpy as np
from jax import lax
from jax.experimental import pallas as pl
from jax.experimental.pallas import tpu as pltpu
from jax.sharding import PartitionSpec as P

CHUNK = 32
PROMPT_CHUNKS = 16
OWN_CHUNKS = 256
HOME = 512
X, YA, YB, Z, CORE = 1, 2, 4, 8, 16
ORDERS = ((X, Z, YB, YA), (YA, YB, Z, X), (YB, YA, X, Z), (Z, X, YA, YB))
DEAL = (2, 0, 1, 3, 2, 0, 1, 2, 3, 0, 1, 2, 0, 1, 3, 2)
SHARES = tuple(sum(1 << k for k, part in enumerate(DEAL) if part == q) for q in range(4))
ROOM = ((40, 40, 48, 36), (48, 44, 48, 48), (64, 52, 48, 52), (72, 72, 68, 60))
MIB = 1024 * 1024
SMALL = 4096


KEPT = (52, 52, 64, 40)


def region(phase, part):
    return KEPT[part] + sum(rooms[part] for rooms in ROOM[:phase])


def begin_of(part, phase):
    return sum(region(phase, q) for q in range(part))


LATE_BEGIN = tuple(sum(ROOM[3][:q]) for q in range(5))


def flipped(group, mask):
    x, core, y = (group >> 1) & 1, group & 1, group >> 2
    if mask & X:
        x ^= 1
    if mask & YA:
        y ^= 1
    if mask & YB:
        y = 3 - y
    if mask & CORE:
        core ^= 1
    return (y << 2) | (x << 1) | core


def hop(value, axis):
    if axis == Z:
        return lax.ppermute(value, "tp", [(t, t ^ 1) for t in range(lax.axis_size("tp"))])
    return lax.ppermute(value, "grp", [(g, flipped(g, axis)) for g in range(lax.axis_size("grp"))])


def node_of(group, parity):
    y = group >> 2
    return (
        ((group >> 1) & 1)
        | (((y ^ (y >> 1)) & 1) << 1)
        | (((y >> 1) & 1) << 2)
        | (parity << 3)
        | ((group & 1) << 4)
    )


def bits_set(word):
    word = word - ((word >> 1) & 0x5555)
    word = (word & 0x3333) + ((word >> 2) & 0x3333)
    word = (word + (word >> 4)) & 0x0F0F
    return (word + (word >> 8)) & 0x1F


def turned(share, by):
    return ((share | (share << 16)) >> by) & 0xFFFF


def below(k):
    return (1 << k) - 1


def exact(values):
    return values.astype(jnp.float32).astype(jnp.bfloat16)


def dot(left, right):
    return jnp.dot(left, right, preferred_element_type=jnp.float32)


def standing(row):
    size = row.shape[1]
    down = lax.broadcasted_iota(jnp.int32, (size, size), 0)
    along = lax.broadcasted_iota(jnp.int32, (size, size), 1)
    return jnp.sum(jnp.where(down == along, row, 0), axis=1, keepdims=True)


def ends_of(targets, prompt, parity):
    start = node_of(prompt >> 4, parity)
    end = node_of(targets >> 1, targets & 1)
    start = (start & 15) | (end & CORE)
    return start, start ^ end


def earlier_rows(size):
    down = lax.broadcasted_iota(jnp.int32, (size, size), 0)
    along = lax.broadcasted_iota(jnp.int32, (size, size), 1)
    return exact(jnp.where(along < down, 1, 0))


SENT, RECEIVED, SLOTS, HELD = 0, 16, 32, 36


def first_plan_kernel(where_ref, targets_ref, lens_ref, const_ref, table_ref):
    me, group = where_ref[0], where_ref[2]
    local = lax.broadcasted_iota(jnp.int32, (32, 1), 0)
    prompt = 16 * (group & ~1) + local
    match = lax.broadcasted_iota(jnp.int32, (32, targets_ref.shape[1]), 1) == prompt
    targets = jnp.sum(jnp.where(match, targets_ref[...], 0), axis=1, keepdims=True)
    lens = jnp.sum(jnp.where(match, lens_ref[...], 0), axis=1, keepdims=True)
    start, ways = ends_of(targets, prompt, (me >> 3) & 1)
    bit, share = const_ref[1:2, :], const_ref[3:4, :]
    lane = lax.broadcasted_iota(jnp.int32, (1, 64), 1)
    word = turned(share, (prompt * 5) & 15) & below((lens + (CHUNK - 1)) >> 5)
    goes = (lane < 4) & ((ways & bit) != 0) | (lane >= HELD) & (lane < HELD + 4)
    goes = goes & (start == me)
    place = dot(earlier_rows(32), exact(jnp.where(goes, bits_set(word), 0))).astype(jnp.int32)
    place = jnp.where(goes, place, -256)

    def each_chunk(values):
        wide = jnp.broadcast_to(values[:, None, :], (32, PROMPT_CHUNKS, values.shape[1]))
        return wide.reshape(32 * PROMPT_CHUNKS, values.shape[1])

    unit = lax.broadcasted_iota(jnp.int32, (HOME, 1), 0)
    k = unit & 15
    home = jnp.where(((unit >> 8) & 1) == (group & 1), 0, OWN_CHUNKS) + (unit & (OWN_CHUNKS - 1))
    words = each_chunk(word)
    spot = jnp.where(((words >> k) & 1) != 0, each_chunk(place) + bits_set(words & below(k)), -1)
    slot = lax.broadcasted_iota(jnp.int32, (1, 128), 1)
    rows = []
    for c in (0, 1, 2, 3, HELD, HELD + 1, HELD + 2, HELD + 3):
        rows.append(jnp.sum(jnp.where(spot[:, c : c + 1] == slot, home, 0), axis=0, keepdims=True))
    table_ref[...] = jnp.concatenate(rows, axis=0)


LATE, LENGTH, OVER = 32, 64, 65


def plan_kernel(where_ref, targets_ref, lens_ref, const_ref, slots_ref, land_ref):
    me, mine = where_ref[0], where_ref[1]
    row_t = jnp.concatenate([targets_ref[...], targets_ref[...]], axis=1)
    items = row_t.shape[1]
    prompts = items // 2
    col_t, col_l = standing(targets_ref[...]), standing(lens_ref[...])
    col_t, col_l = (jnp.concatenate([c, c], axis=0) for c in (col_t, col_l))
    item = lax.broadcasted_iota(jnp.int32, (items, 1), 0)
    prompt, parity = item & (prompts - 1), item >> 8
    start, ways = ends_of(col_t, prompt, parity)
    turn = (prompt * 5) & 15
    routed, bit, sender, share, room = (const_ref[k : k + 1, :] for k in range(5))
    lane = lax.broadcasted_iota(jnp.int32, (1, 64), 1)
    keeps = (lane >= HELD) & (lane < HELD + 4)
    weight = bits_set(turned(share, turn) & below((col_l + (CHUNK - 1)) >> 5))
    crosses = ((ways & bit) != 0) & (lane < SLOTS) | keeps
    listed = crosses & ((start ^ (ways & routed)) == (me ^ sender))
    landing = (col_t == mine) & (lane == SLOTS + parity)
    amount = jnp.where(listed, weight, jnp.where(landing, 1, 0))
    place = dot(earlier_rows(items), exact(amount)).astype(jnp.int32)

    everyone = exact(jnp.where(crosses, weight, 0))
    row_item = lax.broadcasted_iota(jnp.int32, (1, items), 1)
    row_start, row_ways = ends_of(row_t, row_item & (prompts - 1), row_item >> 8)
    nodes = lax.broadcasted_iota(jnp.int32, (32, 1), 0)
    ways_done = sorted({sum(order[:p]) for order in ORDERS for p in range(4)})
    present = [jnp.where(nodes == (row_start ^ (row_ways & done)), 1, 0) for done in ways_done]
    held = dot(exact(jnp.concatenate(present, axis=0)), everyone)
    need = jnp.zeros((1, 64), jnp.float32)
    for k, done in enumerate(ways_done):
        most = jnp.max(held[32 * k : 32 * k + 32], axis=0, keepdims=True)
        need = jnp.where(routed == done, most, need)
    over = (need.astype(jnp.int32) > room) & ((lane < RECEIVED) | keeps)
    over = jnp.max(jnp.where(over, 1, 0), axis=1, keepdims=True)

    bases = [[place[:, HELD + q : HELD + q + 1] for q in range(4)]]
    for p in range(4):
        came = []
        for q in range(4):
            c = RECEIVED + 4 * p + q
            moved = (ways & ORDERS[q][p]) != 0
            came.append(jnp.where(moved, region(p, q) + place[:, c : c + 1], bases[p][q]))
        bases.append(came)

    slot = lax.broadcasted_iota(jnp.int32, (1, 128), 1)

    def sources(p, q):
        c = 4 * p + q
        first = jnp.where(listed[:, c : c + 1], place[:, c : c + 1], 1 << 20)
        offset = slot - first
        inside = (offset >= 0) & (offset < weight[:, c : c + 1])
        found = jnp.where(inside, offset + bases[p][q], 0)
        return jnp.minimum(jnp.sum(found, axis=0, keepdims=True), region(p, q) - 1)

    slots_ref[...] = jnp.concatenate(
        [jnp.zeros((4, 128), jnp.int32)] + [sources(p, q) for p in range(1, 4) for q in range(4)], axis=0
    )

    rank = jnp.where(parity == 0, place[:, SLOTS : SLOTS + 1], place[:, SLOTS + 1 : SLOTS + 2])
    rank = jnp.where(col_t == mine, rank, -1)
    lands = [rank[:prompts] == slot, rank[prompts:] == slot]

    def landed(value, j):
        return jnp.sum(jnp.where(lands[j], value[j * prompts : (j + 1) * prompts], 0), axis=0, keepdims=True)

    length = landed(col_l, 0)
    live = (length + (CHUNK - 1)) >> 5
    by = landed(turn, 0)
    k = lax.broadcasted_iota(jnp.int32, (PROMPT_CHUNKS, 1), 0)
    early, late = [], []
    for j in range(2):
        here = jnp.zeros((PROMPT_CHUNKS, 128), jnp.int32)
        last = jnp.zeros((PROMPT_CHUNKS, 128), jnp.int32)
        for q in range(4):
            c = RECEIVED + 12 + q
            moves = landed(jnp.where((ways & ORDERS[q][3]) != 0, 1, 0), j)
            held = landed(bases[3][q], j)
            comes = landed(place[:, c : c + 1], j)
            part = turned(jnp.full_like(by, SHARES[q]), by)
            rest = bits_set(part & below(k))
            dealt = (part >> k) & 1
            spot = begin_of(q, 3) + jnp.minimum(held + rest, region(3, q) - 1)
            here += dealt * jnp.where(moves != 0, begin_of(4, 3), spot)
            spot = LATE_BEGIN[q] + jnp.minimum(comes + rest, ROOM[3][q] - 1)
            last += dealt * jnp.where(moves != 0, spot, -1)
        early.append(jnp.where(k < live, here, begin_of(4, 3)))
        late.append(jnp.where(k < live, last, -1))
    rows = [length, jnp.broadcast_to(over, (1, 128)), jnp.zeros((6, 128), jnp.int32)]
    land_ref[...] = jnp.concatenate(early + late + rows, axis=0)


def plan_const():
    const = np.zeros((8, 64), np.int32)
    for p in range(4):
        for q, order in enumerate(ORDERS):
            for first, sender in ((SENT, 0), (RECEIVED, order[p])):
                const[:5, first + 4 * p + q] = (sum(order[:p]), order[p], sender, SHARES[q], ROOM[p][q])
    for q in range(4):
        const[3:5, HELD + q] = (SHARES[q], KEPT[q])
    return jnp.asarray(const)


def plan_call(kernel, name, rows, *operands):
    vmem = pl.BlockSpec(memory_space=pltpu.VMEM)
    return pl.pallas_call(
        kernel,
        out_shape=tuple(jax.ShapeDtypeStruct((r, 128), jnp.int32) for r in rows),
        in_specs=[pl.BlockSpec(memory_space=pltpu.SMEM), vmem, vmem, vmem],
        out_specs=(vmem,) * len(rows),
        compiler_params=pltpu.CompilerParams(vmem_limit_bytes=24 * MIB),
        cost_estimate=cost(SMALL),
        name=name,
    )(*operands)


def plan_operands(targets, prompt_lens, group, member):
    where = jnp.stack([node_of(group, member % 2), 2 * group + member % 2, group]).astype(jnp.int32)
    return where, targets.reshape(1, -1), prompt_lens.reshape(1, -1), plan_const()


def fetch(pairs, sems):
    copies = [
        pltpu.make_async_copy(source, target, sems.at[k]) for k, (source, target) in enumerate(pairs)
    ]
    for copy in copies:
        copy.start()
    return copies


def gather_chunks(table_ref, row, out_ref, pick):
    def some(first, batch):
        held = [pick(table_ref[row, first + b], first + b) for b in range(batch)]
        for b in range(batch):
            out_ref[first + b] = held[b]

    def body(s, carry):
        some(8 * s, 8)
        return carry

    count = out_ref.shape[0]
    lax.fori_loop(0, count // 8, body, 0)
    if count % 8:
        some(count // 8 * 8, count % 8)


SMEM = pl.BlockSpec(memory_space=pltpu.SMEM)
ANY = pl.BlockSpec(memory_space=pl.ANY)
VMEM = pl.BlockSpec(memory_space=pltpu.VMEM)


def chunks_of(count):
    return jax.ShapeDtypeStruct((count, CHUNK, 256), jnp.bfloat16)


def cost(bytes_accessed, flops=0):
    return pl.CostEstimate(flops=flops, bytes_accessed=bytes_accessed, transcendentals=0)


def home_kernel(rows, table_ref, kv_ref, other_ref, *outs):
    def pick(i, s):
        row = i & (OWN_CHUNKS - 1)
        return jnp.where(i < OWN_CHUNKS, kv_ref[row], other_ref[row])

    for q in range(4):
        gather_chunks(table_ref, rows + q, outs[q], pick)


def own_kernel(table_ref, kv_ref, *outs):
    for q in range(4):
        gather_chunks(table_ref, q, outs[q], lambda i, s: kv_ref[i & (OWN_CHUNKS - 1)])


def other_kernel(table_ref, other_ref, *rest):
    befores, outs = rest[:4], rest[4:]
    for q in range(4):

        def pick(i, s):
            return jnp.where(i < OWN_CHUNKS, befores[q][s], other_ref[i & (OWN_CHUNKS - 1)])

        gather_chunks(table_ref, q, outs[q], pick)


def lists_call(kernel, name, rooms, table, *operands):
    return pl.pallas_call(
        kernel,
        out_shape=tuple(chunks_of(room) for room in rooms),
        in_specs=[SMEM] + [VMEM] * len(operands),
        out_specs=(VMEM,) * 4,
        compiler_params=pltpu.CompilerParams(vmem_limit_bytes=28 * MIB),
        cost_estimate=cost(SMALL),
        name=name,
    )(table, *operands)


def part_pairs(part, boxes, space, begin=0):
    pairs = []
    for k, box in enumerate(boxes):
        at = begin + (region(k - 1, part) if k else 0)
        pairs.append((box, space.at[pl.ds(at, box.shape[0])]))
    return pairs


def before_kernel(phase, table_ref, *rest):
    boxes, outs, space, sems = rest[: 4 * phase], rest[4 * phase : 4 * phase + 4], rest[4 * phase + 4], rest[4 * phase + 5]
    copies = []
    for q in range(4):
        pairs = part_pairs(q, boxes[phase * q : phase * q + phase], space, begin_of(q, phase - 1))
        copies.append(fetch(pairs, sems.at[q]))
    for q in range(4):
        for copy in copies[q]:
            copy.wait()
        begin, end = begin_of(q, phase - 1), region(phase - 1, q) - 1
        gather_chunks(table_ref, 4 * phase + q, outs[q], lambda i, s: space[begin + jnp.minimum(i, end)])


def before_lists(phase, table, boxes):
    flat = [box for part in boxes for box in part]
    return pl.pallas_call(
        functools.partial(before_kernel, phase),
        out_shape=tuple(chunks_of(room) for room in ROOM[phase]),
        in_specs=[SMEM] + [ANY] * len(flat),
        out_specs=(VMEM,) * 4,
        scratch_shapes=[
            pltpu.VMEM((begin_of(4, phase - 1), CHUNK, 256), jnp.bfloat16),
            pltpu.SemaphoreType.DMA((4, phase)),
        ],
        compiler_params=pltpu.CompilerParams(vmem_limit_bytes=28 * MIB),
        cost_estimate=cost(SMALL),
        name="before_lists",
    )(table, *flat)


def after_kernel(phase, table_ref, *rest):
    befores, boxes, outs = rest[:4], rest[4:8], rest[8:]
    for q in range(4):
        begin = region(phase - 1, q)

        def pick(i, s):
            return jnp.where(i < begin, befores[q][s], boxes[q][jnp.maximum(i - begin, 0)])

        gather_chunks(table_ref, 4 * phase + q, outs[q], pick)


def attend_row(query, first, second, own, length):
    scaling = 1.0 / math.sqrt(query.shape[1])
    upper = lax.broadcasted_iota(jnp.int32, query.shape, 0) < 8
    zero = jnp.zeros_like(query)
    wide = jnp.concatenate([jnp.where(upper, query, zero), jnp.where(upper, zero, query)], axis=1)
    keys = jnp.concatenate([first[:, :128], second[:, :128]], axis=1)
    values = jnp.concatenate([first[:, 128:], second[:, 128:]], axis=1)
    scores = (
        lax.dot_general(wide, keys, (((1,), (1,)), ((), ())), preferred_element_type=jnp.float32)
        * scaling
    )
    own = own.astype(jnp.float32)
    own_key = jnp.where(upper, own[0:1, :128], own[1:2, :128])
    own_value = jnp.where(upper, own[0:1, 128:], own[1:2, 128:])
    own_score = jnp.sum(query.astype(jnp.float32) * own_key, axis=1, keepdims=True) * scaling
    live = lax.broadcasted_iota(jnp.int32, scores.shape, 1) < length
    scores = jnp.where(live, scores, -jnp.inf)
    row_max = jnp.maximum(jnp.max(scores, axis=1, keepdims=True), own_score)
    weights = jnp.where(live, jnp.exp(scores - row_max), 0.0)
    own_weight = jnp.exp(own_score - row_max)
    denominator = jnp.sum(weights, axis=1, keepdims=True) + own_weight
    both = jnp.dot(weights.astype(jnp.bfloat16), values, preferred_element_type=jnp.float32)
    mixture = jnp.where(upper, both[:, :128], both[:, 128:])
    mixture += own_weight.astype(jnp.bfloat16).astype(jnp.float32) * own_value
    return mixture / denominator


def lay_rows(result, out_ref, first, rows):
    for row in range(0, rows, 16):
        for head in range(16):
            values = result[pl.ds(16 * row + head, 16, stride=16)]
            out_ref[first + row : first + row + 16, 128 * head : 128 * head + 128] = values.astype(jnp.bfloat16)


TOGETHER = 4
DEPTH = 4 * TOGETHER


def running_kernel(first, half_ref, pages_ref, lens_ref, query_ref, own_ref, pool_ref, out_ref, held, result, sems):
    rows = out_ref.shape[0]
    all_rows = lens_ref.shape[0] // 2
    max_pages = held.shape[1]
    start = half_ref[0] * all_rows + first

    def each_page(row, action):
        slot = row % DEPTH
        for c in range(max_pages):
            page = pages_ref[(start + row) * max_pages + c]
            action(pltpu.make_async_copy(pool_ref.at[page], held.at[slot, c], sems.at[slot, c]))

    def begin(group):
        for r in range(TOGETHER):
            each_page(group * TOGETHER + r, lambda copy: copy.start())

    ahead = DEPTH // TOGETHER - 1
    for group in range(ahead):
        begin(group)

    def body(group, carry):
        @pl.when(group + ahead < rows // TOGETHER)
        def _():
            begin(group + ahead)

        for r in range(TOGETHER):
            each_page(group * TOGETHER + r, lambda copy: copy.wait())
        results = []
        for r in range(TOGETHER):
            row = group * TOGETHER + r
            slot = row % DEPTH
            blocks = [held[slot, :, j].reshape(max_pages * 64, 256) for j in range(2)]
            results.append(
                attend_row(query_ref[first + row], *blocks, own_ref[first + row], lens_ref[start + row])
            )
        for r in range(TOGETHER):
            result[pl.ds((group * TOGETHER + r) * 16, 16)] = results[r]
        return carry

    lax.fori_loop(0, rows // TOGETHER, body, 0)
    lay_rows(result, out_ref, 0, rows)


def running_rows(first, count, half, pages, lens, queries, own, pool):
    max_pages = pages.shape[0] // lens.shape[0]
    return pl.pallas_call(
        functools.partial(running_kernel, first),
        out_shape=jax.ShapeDtypeStruct((count, 2048), jnp.bfloat16),
        in_specs=[SMEM, SMEM, SMEM, VMEM, VMEM, pl.BlockSpec(memory_space=pltpu.HBM)],
        out_specs=VMEM,
        scratch_shapes=[
            pltpu.VMEM((DEPTH, max_pages) + pool.shape[1:], jnp.bfloat16),
            pltpu.VMEM((count * 16, 128), jnp.float32),
            pltpu.SemaphoreType.DMA((DEPTH, max_pages)),
        ],
        compiler_params=pltpu.CompilerParams(vmem_limit_bytes=40 * MIB),
        cost_estimate=cost(SMALL),
        name="running_rows",
    )(half, pages, lens, queries, own, pool)


RING = 4


def early_kernel(land_ref, *rest):
    boxes, (landed_ref, block, sems, space, box_sems) = rest[:16], rest[16:]
    slots = landed_ref.shape[0]
    pairs = []
    for q in range(4):
        pairs += part_pairs(q, boxes[4 * q : 4 * q + 4], space, begin_of(q, 3))
    copies = fetch(pairs, box_sems)
    space[begin_of(4, 3)] = jnp.zeros((CHUNK, 256), jnp.bfloat16)
    for copy in copies:
        copy.wait()

    def write(slot):
        turn = slot % RING
        return pltpu.make_async_copy(block.at[turn], landed_ref.at[slot], sems.at[turn])

    def body(slot, carry):
        @pl.when(slot >= RING)
        def _():
            write(slot).wait()

        for j in range(2):
            for k in range(0, PROMPT_CHUNKS, 8):
                held = [space[land_ref[PROMPT_CHUNKS * j + k + b, slot]] for b in range(8)]
                for b in range(8):
                    block[slot % RING, j, k + b] = held[b]
        write(slot).start()
        return carry

    lax.fori_loop(0, slots, body, 0)
    for slot in range(slots - RING, slots):
        write(slot).wait()


def early_rows(slots, land, boxes):
    return pl.pallas_call(
        early_kernel,
        out_shape=jax.ShapeDtypeStruct((slots, 2, PROMPT_CHUNKS, CHUNK, 256), jnp.bfloat16),
        in_specs=[SMEM] + [ANY] * 16,
        out_specs=ANY,
        scratch_shapes=[
            pltpu.VMEM((RING, 2, PROMPT_CHUNKS, CHUNK, 256), jnp.bfloat16),
            pltpu.SemaphoreType.DMA((RING,)),
            pltpu.VMEM((begin_of(4, 3) + 1, CHUNK, 256), jnp.bfloat16),
            pltpu.SemaphoreType.DMA((16,)),
        ],
        compiler_params=pltpu.CompilerParams(vmem_limit_bytes=28 * MIB),
        cost_estimate=cost(SMALL),
        name="early_rows",
    )(land, *boxes)


LAND_RING = 8


def land_kernel(given, land_ref, query_ref, own_ref, early_ref, *rest):
    contexts, rest = rest[:given], rest[given:]
    boxes, rest = rest[:4], rest[4:]
    out_ref, landed_ref, block, result, handed, in_sems, sems, space, box_sems, out_sems = rest
    slots = landed_ref.shape[0]
    first = out_ref.shape[0] - slots

    def read(slot):
        turn = slot % LAND_RING
        return pltpu.make_async_copy(early_ref.at[slot], block.at[turn], in_sems.at[turn])

    def write(slot):
        turn = slot % LAND_RING
        return pltpu.make_async_copy(block.at[turn], landed_ref.at[slot], sems.at[turn])

    copies = fetch([(box, space.at[pl.ds(LATE_BEGIN[q], box.shape[0])]) for q, box in enumerate(boxes)], box_sems)
    for slot in range(4):
        read(slot).start()
    done = 0
    pairs = []
    for context in contexts:
        pairs.append((context, out_ref.at[pl.ds(done, context.shape[0])]))
        done += context.shape[0]
    decoded = fetch(pairs, out_sems)
    for copy in copies:
        copy.wait()

    def complete(slot):
        turn = slot % LAND_RING
        length = land_ref[LENGTH, slot]
        for j in range(2):
            for k in range(0, PROMPT_CHUNKS, 8):
                held = []
                for b in range(8):
                    source = land_ref[LATE + PROMPT_CHUNKS * j + k + b, slot]
                    held.append(jnp.where(source >= 0, space[jnp.maximum(source, 0)], block[turn, j, k + b]))
                for b in range(8):
                    block[turn, j, k + b] = held[b]
        last = jnp.maximum(length - 1, 0) // CHUNK
        row = last * CHUNK + lax.broadcasted_iota(jnp.int32, (CHUNK, 256), 0)
        zero = jnp.zeros((CHUNK, 256), jnp.bfloat16)
        for j in range(2):
            block[turn, j, last] = jnp.where(row < length, block[turn, j, last], zero)

    def body(pair, carry):
        both = (2 * pair, 2 * pair + 1)

        @pl.when(2 * pair + 4 < slots)
        def _():
            for slot in both:

                @pl.when(slot + 4 >= LAND_RING)
                def _():
                    write(slot + 4).wait()

                read(slot + 4).start()

        for slot in both:
            read(slot).wait()
        for slot in both:
            complete(slot)
        for slot in both:
            write(slot).start()
        results = []
        for slot in both:
            blocks = [block[slot % LAND_RING, j].reshape(PROMPT_CHUNKS * CHUNK, 256) for j in range(2)]
            results.append(
                attend_row(query_ref[first + slot], *blocks, own_ref[first + slot], land_ref[LENGTH, slot])
            )
        for slot, value in zip(both, results):
            result[pl.ds(16 * slot, 16)] = value
        return carry

    lax.fori_loop(0, slots // 2, body, 0)
    lay_rows(result, handed, 0, slots)
    last = pltpu.make_async_copy(handed, out_ref.at[pl.ds(first, slots)], out_sems.at[len(contexts)])
    last.start()
    for slot in range(slots - LAND_RING, slots):
        write(slot).wait()
    for copy in decoded + [last]:
        copy.wait()


def land_rows(land, queries, own, early, contexts, boxes):
    return pl.pallas_call(
        functools.partial(land_kernel, len(contexts)),
        out_shape=(
            jax.ShapeDtypeStruct((queries.shape[0], 2048), jnp.bfloat16),
            jax.ShapeDtypeStruct(early.shape, jnp.bfloat16),
        ),
        in_specs=[SMEM, VMEM, VMEM, ANY] + [VMEM] * len(contexts) + [ANY] * 4,
        out_specs=(ANY, ANY),
        scratch_shapes=[
            pltpu.VMEM((LAND_RING,) + early.shape[1:], jnp.bfloat16),
            pltpu.VMEM((16 * early.shape[0], 128), jnp.float32),
            pltpu.VMEM((early.shape[0], 2048), jnp.bfloat16),
            pltpu.SemaphoreType.DMA((LAND_RING,)),
            pltpu.SemaphoreType.DMA((LAND_RING,)),
            pltpu.VMEM((LATE_BEGIN[4], CHUNK, 256), jnp.bfloat16),
            pltpu.SemaphoreType.DMA((4,)),
            pltpu.SemaphoreType.DMA((len(contexts) + 1,)),
        ],
        compiler_params=pltpu.CompilerParams(vmem_limit_bytes=24 * MIB),
        cost_estimate=cost(SMALL),
        name="land_rows",
    )(land, queries, own, early, *contexts, *boxes)


def routed(operands, kv, half, pages, lens, queries, own, pool):
    running = pages.shape[1]
    rows = queries.shape[0]
    pages, lens = pages.reshape(-1), lens.reshape(-1)
    other = hop(kv, CORE)
    (table,) = plan_call(first_plan_kernel, "first_plan", (8,), *operands)
    lists = lists_call(own_kernel, "own_lists", ROOM[0], table, kv)
    queries = queries.reshape(rows, 16, 128)
    lists, other, queries, pages, lens = lax.optimization_barrier((lists, other, queries, pages, lens))
    lists = lists_call(other_kernel, "first_lists", ROOM[0], table, other, *lists)
    sent = [hop(value, order[0]) for value, order in zip(lists, ORDERS)]
    (where, table), _ = lax.optimization_barrier(((operands[0], table), lists))
    kept = lists_call(functools.partial(home_kernel, 4), "kept_lists", KEPT, table, kv, other)
    table, land = plan_call(plan_kernel, "plan", (16, 72), where, *operands[1:])
    boxes = [[k] for k in kept]
    befores = before_lists(1, table, boxes)
    contexts = []
    done = 0
    for phase, count in ((1, running // 4), (2, running // 2), (3, running // 4)):
        table, sent, befores = lax.optimization_barrier((table, sent, befores))
        lists = lists_call(functools.partial(after_kernel, phase), "after_lists", ROOM[phase], table, *befores, *sent)
        boxes = [part + [box] for part, box in zip(boxes, sent)]
        sent = [hop(value, order[phase]) for value, order in zip(lists, ORDERS)]
        (ready, table, land), _ = lax.optimization_barrier(((half, table, land), lists))
        contexts.append(running_rows(done, count, ready, pages, lens, queries, own, pool))
        done += count
        if phase < 3:
            befores = before_lists(phase + 1, table, boxes)
            table, _ = lax.optimization_barrier((table, contexts))
        else:
            early = early_rows(rows - running, land, [box for part in boxes for box in part])
            sent, _, early = lax.optimization_barrier((sent, contexts, early))
    context, landed = land_rows(land, queries, own, early, contexts, sent)
    return context, landed, land[OVER, 0]


def earlier_matches(labels, block_len, kind_count):
    onehot = (labels[:, None] == jnp.arange(kind_count, dtype=jnp.int32)[None, :]).astype(jnp.int32)
    blocks = onehot.reshape(labels.shape[0] // block_len, block_len, kind_count)
    before = jnp.cumsum(blocks, axis=1) - blocks
    return jnp.sum(before * blocks, axis=2).reshape(labels.shape[0])


def lookup(matches):
    prompt_ids = jnp.arange(matches.shape[1], dtype=jnp.int32)
    row_index = jnp.sum(jnp.where(matches, prompt_ids[None, :], 0), axis=1)
    return (row_index, jnp.any(matches, axis=1))


def pick_rows(table_rows, row_index, is_valid):
    picked = jnp.take(table_rows, row_index, axis=0)
    mask_shape = (is_valid.shape[0],) + (1,) * (picked.ndim - 1)
    return jnp.where(is_valid.reshape(mask_shape), picked, jnp.zeros_like(picked))


def any_fill(targets, prompt_lens, kv, queries, own):
    prompt_kv = kv.reshape(16, 1, 512, 256)
    groups = lax.axis_size("grp")
    group_id = lax.axis_index("grp")
    half_id = lax.axis_index("tp") % 2
    block_len = prompt_kv.shape[0]
    prompt_count = targets.shape[0]
    span_len = prompt_kv.shape[2]
    capacity = max(2, block_len // groups)
    source = jnp.arange(prompt_count, dtype=jnp.int32) // block_len
    arrival = earlier_matches(targets, prompt_count, 2 * groups)
    slot_ids = jnp.arange(block_len, dtype=jnp.int32)
    land_match = (targets[None, :] == 2 * group_id + half_id) & (
        arrival[None, :] == slot_ids[:, None]
    )
    land_len = jnp.sum(jnp.where(land_match, prompt_lens[None, :], 0), axis=1)
    land_live = jnp.arange(span_len, dtype=jnp.int32)[None, :] < land_len[:, None]
    land_index, land_valid = lookup(land_match)
    outgoing = source == group_id
    dest_ids = jnp.arange(groups, dtype=jnp.int32)
    cap_ids = jnp.arange(capacity, dtype=jnp.int32)
    partner = hop(prompt_kv, Z)
    pair_kv = jnp.where(
        half_id == 0,
        jnp.concatenate([prompt_kv, partner], axis=1),
        jnp.concatenate([partner, prompt_kv], axis=1),
    )
    within = earlier_matches(targets, block_len, 2 * groups)
    send_match = (
        outgoing[None, None, :]
        & (targets[None, None, :] == (2 * dest_ids + half_id)[:, None, None])
        & (within[None, None, :] == cap_ids[None, :, None])
    )
    send_index, send_valid = lookup(send_match.reshape(groups * capacity, prompt_count))
    send_index = jnp.where(send_valid, send_index - group_id * block_len, 0)
    outbox = pick_rows(pair_kv, send_index, send_valid)
    outbox = outbox.reshape((groups, capacity) + outbox.shape[1:])
    inbound = lax.all_to_all(outbox, "grp", split_axis=0, concat_axis=0, tiled=True)
    inbound = inbound.reshape((groups * capacity,) + inbound.shape[2:])
    entry_ids = source * capacity + within
    landed = pick_rows(inbound, jnp.take(entry_ids, land_index), land_valid)
    landed = jnp.where(land_live[:, None, :, None], landed, jnp.zeros_like(landed))
    handed = jnp.stack(
        [
            attend_row(queries[s], landed[s, 0], landed[s, 1], own[s], land_len[s])
            for s in range(block_len)
        ]
    )
    return handed, landed.reshape(block_len, 2, PROMPT_CHUNKS, CHUNK, 256)


def local(targets, prompt_lens, prompt_kv, cache_pool, block_table, cache_lens, queries, new_kv):
    group = lax.axis_index("grp")
    member = lax.axis_index("tp")
    kv = prompt_kv.reshape(OWN_CHUNKS, CHUNK, 256)
    operands = plan_operands(targets, prompt_lens, group, member)
    half = (member % 2).astype(jnp.int32).reshape(1)
    rows = queries.shape[2]
    running = block_table.shape[2]
    own = new_kv[0, 0]
    queries = queries[0, 0]
    context, landed, over = routed(
        operands, kv, half, block_table[0], cache_lens[0], queries, own, cache_pool[0, 0]
    )

    def again(carry):
        handed, landed = any_fill(targets, prompt_lens, kv, queries[running:].reshape(-1, 16, 128), own[running:])
        handed = handed.astype(jnp.bfloat16).reshape(rows - running, -1)
        return carry[0].at[running:].set(handed), landed, jnp.zeros((), jnp.int32)

    context, landed, _ = lax.while_loop(lambda carry: carry[2] > 0, again, (context, landed, over))
    return (
        context.reshape(1, 1, rows, -1),
        landed.reshape(1, 1, 16, 2, 512, 256),
    )


def solution(mesh):
    placed = (
        P(),
        P(),
        P("grp", "tp", None, None),
        P("grp", "tp", None, None, None, None),
        P("grp", None, None, None),
        P("grp", None, None),
        P("grp", "tp", None, None),
        P("grp", "tp", None, None, None),
    )
    return jax.shard_map(
        local,
        mesh=mesh,
        in_specs=placed,
        out_specs=(P("grp", "tp", None, None), P("grp", "tp", None, None, None, None)),
        check_vma=False,
    )
```

```python
import functools
import math

import jax
import jax.numpy as jnp
import numpy as np
from jax import lax
from jax.experimental import pallas as pl
from jax.experimental.pallas import tpu as pltpu
from jax.sharding import PartitionSpec as P

CHUNK = 32
PROMPT_CHUNKS = 16
OWN_CHUNKS = 256
HOME = 512
X, YA, YB, Z, CORE = 1, 2, 4, 8, 16
ORDERS = ((X, Z, YB, YA), (YA, YB, Z, X), (YB, YA, X, Z), (Z, X, YA, YB))
DEAL = (2, 0, 1, 3, 2, 0, 1, 2, 3, 0, 1, 2, 0, 1, 3, 2)
SHARES = tuple(sum(1 << k for k, part in enumerate(DEAL) if part == q) for q in range(4))
ROOM = ((40, 40, 48, 36), (48, 44, 48, 48), (64, 52, 48, 52), (72, 72, 68, 60))
MIB = 1024 * 1024
SMALL = 4096


KEPT = (52, 52, 64, 40)


def region(phase, part):
    return KEPT[part] + sum(rooms[part] for rooms in ROOM[:phase])


def begin_of(part, phase):
    return sum(region(phase, q) for q in range(part))


LATE_BEGIN = tuple(sum(ROOM[3][:q]) for q in range(5))


def flipped(group, mask):
    x, core, y = (group >> 1) & 1, group & 1, group >> 2
    if mask & X:
        x ^= 1
    if mask & YA:
        y ^= 1
    if mask & YB:
        y = 3 - y
    if mask & CORE:
        core ^= 1
    return (y << 2) | (x << 1) | core


def hop(value, axis):
    if axis == Z:
        return lax.ppermute(value, "tp", [(t, t ^ 1) for t in range(lax.axis_size("tp"))])
    return lax.ppermute(value, "grp", [(g, flipped(g, axis)) for g in range(lax.axis_size("grp"))])


def node_of(group, parity):
    y = group >> 2
    return (
        ((group >> 1) & 1)
        | (((y ^ (y >> 1)) & 1) << 1)
        | (((y >> 1) & 1) << 2)
        | (parity << 3)
        | ((group & 1) << 4)
    )


def bits_set(word):
    word = word - ((word >> 1) & 0x5555)
    word = (word & 0x3333) + ((word >> 2) & 0x3333)
    word = (word + (word >> 4)) & 0x0F0F
    return (word + (word >> 8)) & 0x1F


def turned(share, by):
    return ((share | (share << 16)) >> by) & 0xFFFF


def below(k):
    return (1 << k) - 1


def exact(values):
    return values.astype(jnp.float32).astype(jnp.bfloat16)


def dot(left, right):
    return jnp.dot(left, right, preferred_element_type=jnp.float32)


def standing(row):
    size = row.shape[1]
    down = lax.broadcasted_iota(jnp.int32, (size, size), 0)
    along = lax.broadcasted_iota(jnp.int32, (size, size), 1)
    return jnp.sum(jnp.where(down == along, row, 0), axis=1, keepdims=True)


def ends_of(targets, prompt, parity):
    start = node_of(prompt >> 4, parity)
    end = node_of(targets >> 1, targets & 1)
    start = (start & 15) | (end & CORE)
    return start, start ^ end


def earlier_rows(size):
    down = lax.broadcasted_iota(jnp.int32, (size, size), 0)
    along = lax.broadcasted_iota(jnp.int32, (size, size), 1)
    return exact(jnp.where(along < down, 1, 0))


SENT, RECEIVED, SLOTS, HELD = 0, 16, 32, 36


def first_plan_kernel(where_ref, targets_ref, lens_ref, const_ref, table_ref):
    me, group = where_ref[0], where_ref[2]
    local = lax.broadcasted_iota(jnp.int32, (32, 1), 0)
    prompt = 16 * (group & ~1) + local
    match = lax.broadcasted_iota(jnp.int32, (32, targets_ref.shape[1]), 1) == prompt
    targets = jnp.sum(jnp.where(match, targets_ref[...], 0), axis=1, keepdims=True)
    lens = jnp.sum(jnp.where(match, lens_ref[...], 0), axis=1, keepdims=True)
    start, ways = ends_of(targets, prompt, (me >> 3) & 1)
    bit, share = const_ref[1:2, :], const_ref[3:4, :]
    lane = lax.broadcasted_iota(jnp.int32, (1, 64), 1)
    word = turned(share, (prompt * 5) & 15) & below((lens + (CHUNK - 1)) >> 5)
    goes = (lane < 4) & ((ways & bit) != 0) | (lane >= HELD) & (lane < HELD + 4)
    goes = goes & (start == me)
    place = dot(earlier_rows(32), exact(jnp.where(goes, bits_set(word), 0))).astype(jnp.int32)
    place = jnp.where(goes, place, -256)

    def each_chunk(values):
        wide = jnp.broadcast_to(values[:, None, :], (32, PROMPT_CHUNKS, values.shape[1]))
        return wide.reshape(32 * PROMPT_CHUNKS, values.shape[1])

    unit = lax.broadcasted_iota(jnp.int32, (HOME, 1), 0)
    k = unit & 15
    home = jnp.where(((unit >> 8) & 1) == (group & 1), 0, OWN_CHUNKS) + (unit & (OWN_CHUNKS - 1))
    words = each_chunk(word)
    spot = jnp.where(((words >> k) & 1) != 0, each_chunk(place) + bits_set(words & below(k)), -1)
    slot = lax.broadcasted_iota(jnp.int32, (1, 128), 1)
    rows = []
    for c in (0, 1, 2, 3, HELD, HELD + 1, HELD + 2, HELD + 3):
        rows.append(jnp.sum(jnp.where(spot[:, c : c + 1] == slot, home, 0), axis=0, keepdims=True))
    table_ref[...] = jnp.concatenate(rows, axis=0)


LATE, LENGTH, OVER = 32, 64, 65


def plan_kernel(where_ref, targets_ref, lens_ref, const_ref, slots_ref, land_ref):
    me, mine = where_ref[0], where_ref[1]
    row_t = jnp.concatenate([targets_ref[...], targets_ref[...]], axis=1)
    items = row_t.shape[1]
    prompts = items // 2
    col_t, col_l = standing(targets_ref[...]), standing(lens_ref[...])
    col_t, col_l = (jnp.concatenate([c, c], axis=0) for c in (col_t, col_l))
    item = lax.broadcasted_iota(jnp.int32, (items, 1), 0)
    prompt, parity = item & (prompts - 1), item >> 8
    start, ways = ends_of(col_t, prompt, parity)
    turn = (prompt * 5) & 15
    routed, bit, sender, share, room = (const_ref[k : k + 1, :] for k in range(5))
    lane = lax.broadcasted_iota(jnp.int32, (1, 64), 1)
    keeps = (lane >= HELD) & (lane < HELD + 4)
    weight = bits_set(turned(share, turn) & below((col_l + (CHUNK - 1)) >> 5))
    crosses = ((ways & bit) != 0) & (lane < SLOTS) | keeps
    listed = crosses & ((start ^ (ways & routed)) == (me ^ sender))
    landing = (col_t == mine) & (lane == SLOTS + parity)
    amount = jnp.where(listed, weight, jnp.where(landing, 1, 0))
    place = dot(earlier_rows(items), exact(amount)).astype(jnp.int32)

    everyone = exact(jnp.where(crosses, weight, 0))
    row_item = lax.broadcasted_iota(jnp.int32, (1, items), 1)
    row_start, row_ways = ends_of(row_t, row_item & (prompts - 1), row_item >> 8)
    nodes = lax.broadcasted_iota(jnp.int32, (32, 1), 0)
    ways_done = sorted({sum(order[:p]) for order in ORDERS for p in range(4)})
    present = [jnp.where(nodes == (row_start ^ (row_ways & done)), 1, 0) for done in ways_done]
    held = dot(exact(jnp.concatenate(present, axis=0)), everyone)
    need = jnp.zeros((1, 64), jnp.float32)
    for k, done in enumerate(ways_done):
        most = jnp.max(held[32 * k : 32 * k + 32], axis=0, keepdims=True)
        need = jnp.where(routed == done, most, need)
    over = (need.astype(jnp.int32) > room) & ((lane < RECEIVED) | keeps)
    over = jnp.max(jnp.where(over, 1, 0), axis=1, keepdims=True)

    bases = [[place[:, HELD + q : HELD + q + 1] for q in range(4)]]
    for p in range(4):
        came = []
        for q in range(4):
            c = RECEIVED + 4 * p + q
            moved = (ways & ORDERS[q][p]) != 0
            came.append(jnp.where(moved, region(p, q) + place[:, c : c + 1], bases[p][q]))
        bases.append(came)

    slot = lax.broadcasted_iota(jnp.int32, (1, 128), 1)

    def sources(p, q):
        c = 4 * p + q
        first = jnp.where(listed[:, c : c + 1], place[:, c : c + 1], 1 << 20)
        offset = slot - first
        inside = (offset >= 0) & (offset < weight[:, c : c + 1])
        found = jnp.where(inside, offset + bases[p][q], 0)
        return jnp.minimum(jnp.sum(found, axis=0, keepdims=True), region(p, q) - 1)

    slots_ref[...] = jnp.concatenate(
        [jnp.zeros((4, 128), jnp.int32)] + [sources(p, q) for p in range(1, 4) for q in range(4)], axis=0
    )

    rank = jnp.where(parity == 0, place[:, SLOTS : SLOTS + 1], place[:, SLOTS + 1 : SLOTS + 2])
    rank = jnp.where(col_t == mine, rank, -1)
    lands = [rank[:prompts] == slot, rank[prompts:] == slot]

    def landed(value, j):
        return jnp.sum(jnp.where(lands[j], value[j * prompts : (j + 1) * prompts], 0), axis=0, keepdims=True)

    length = landed(col_l, 0)
    live = (length + (CHUNK - 1)) >> 5
    by = landed(turn, 0)
    k = lax.broadcasted_iota(jnp.int32, (PROMPT_CHUNKS, 1), 0)
    early, late = [], []
    for j in range(2):
        here = jnp.zeros((PROMPT_CHUNKS, 128), jnp.int32)
        last = jnp.zeros((PROMPT_CHUNKS, 128), jnp.int32)
        for q in range(4):
            c = RECEIVED + 12 + q
            moves = landed(jnp.where((ways & ORDERS[q][3]) != 0, 1, 0), j)
            held = landed(bases[3][q], j)
            comes = landed(place[:, c : c + 1], j)
            part = turned(jnp.full_like(by, SHARES[q]), by)
            rest = bits_set(part & below(k))
            dealt = (part >> k) & 1
            spot = begin_of(q, 3) + jnp.minimum(held + rest, region(3, q) - 1)
            here += dealt * jnp.where(moves != 0, begin_of(4, 3), spot)
            spot = LATE_BEGIN[q] + jnp.minimum(comes + rest, ROOM[3][q] - 1)
            last += dealt * jnp.where(moves != 0, spot, -1)
        early.append(jnp.where(k < live, here, begin_of(4, 3)))
        late.append(jnp.where(k < live, last, -1))
    rows = [length, jnp.broadcast_to(over, (1, 128)), jnp.zeros((6, 128), jnp.int32)]
    land_ref[...] = jnp.concatenate(early + late + rows, axis=0)


def plan_const():
    const = np.zeros((8, 64), np.int32)
    for p in range(4):
        for q, order in enumerate(ORDERS):
            for first, sender in ((SENT, 0), (RECEIVED, order[p])):
                const[:5, first + 4 * p + q] = (sum(order[:p]), order[p], sender, SHARES[q], ROOM[p][q])
    for q in range(4):
        const[3:5, HELD + q] = (SHARES[q], KEPT[q])
    return jnp.asarray(const)


def plan_call(kernel, name, rows, *operands):
    vmem = pl.BlockSpec(memory_space=pltpu.VMEM)
    return pl.pallas_call(
        kernel,
        out_shape=tuple(jax.ShapeDtypeStruct((r, 128), jnp.int32) for r in rows),
        in_specs=[pl.BlockSpec(memory_space=pltpu.SMEM), vmem, vmem, vmem],
        out_specs=(vmem,) * len(rows),
        compiler_params=pltpu.CompilerParams(vmem_limit_bytes=24 * MIB),
        cost_estimate=cost(SMALL),
        name=name,
    )(*operands)


def plan_operands(targets, prompt_lens, group, member):
    where = jnp.stack([node_of(group, member % 2), 2 * group + member % 2, group]).astype(jnp.int32)
    return where, targets.reshape(1, -1), prompt_lens.reshape(1, -1), plan_const()


def fetch(pairs, sems):
    copies = [
        pltpu.make_async_copy(source, target, sems.at[k]) for k, (source, target) in enumerate(pairs)
    ]
    for copy in copies:
        copy.start()
    return copies


def gather_chunks(table_ref, row, out_ref, pick):
    def some(first, batch):
        held = [pick(table_ref[row, first + b], first + b) for b in range(batch)]
        for b in range(batch):
            out_ref[first + b] = held[b]

    def body(s, carry):
        some(8 * s, 8)
        return carry

    count = out_ref.shape[0]
    lax.fori_loop(0, count // 8, body, 0)
    if count % 8:
        some(count // 8 * 8, count % 8)


SMEM = pl.BlockSpec(memory_space=pltpu.SMEM)
ANY = pl.BlockSpec(memory_space=pl.ANY)
VMEM = pl.BlockSpec(memory_space=pltpu.VMEM)


def chunks_of(count):
    return jax.ShapeDtypeStruct((count, CHUNK, 256), jnp.bfloat16)


def cost(bytes_accessed, flops=0):
    return pl.CostEstimate(flops=flops, bytes_accessed=bytes_accessed, transcendentals=0)


def home_kernel(rows, table_ref, kv_ref, other_ref, *outs):
    def pick(i, s):
        row = i & (OWN_CHUNKS - 1)
        return jnp.where(i < OWN_CHUNKS, kv_ref[row], other_ref[row])

    for q in range(4):
        gather_chunks(table_ref, rows + q, outs[q], pick)


def own_kernel(table_ref, kv_ref, *outs):
    for q in range(4):
        gather_chunks(table_ref, q, outs[q], lambda i, s: kv_ref[i & (OWN_CHUNKS - 1)])


def other_kernel(table_ref, other_ref, *rest):
    befores, outs = rest[:4], rest[4:]
    for q in range(4):

        def pick(i, s):
            return jnp.where(i < OWN_CHUNKS, befores[q][s], other_ref[i & (OWN_CHUNKS - 1)])

        gather_chunks(table_ref, q, outs[q], pick)


def lists_call(kernel, name, rooms, table, *operands):
    return pl.pallas_call(
        kernel,
        out_shape=tuple(chunks_of(room) for room in rooms),
        in_specs=[SMEM] + [VMEM] * len(operands),
        out_specs=(VMEM,) * 4,
        compiler_params=pltpu.CompilerParams(vmem_limit_bytes=28 * MIB),
        cost_estimate=cost(SMALL),
        name=name,
    )(table, *operands)


def part_pairs(part, boxes, space, begin=0):
    pairs = []
    for k, box in enumerate(boxes):
        at = begin + (region(k - 1, part) if k else 0)
        pairs.append((box, space.at[pl.ds(at, box.shape[0])]))
    return pairs


def before_kernel(phase, table_ref, *rest):
    boxes, outs, space, sems = rest[: 4 * phase], rest[4 * phase : 4 * phase + 4], rest[4 * phase + 4], rest[4 * phase + 5]
    copies = []
    for q in range(4):
        pairs = part_pairs(q, boxes[phase * q : phase * q + phase], space, begin_of(q, phase - 1))
        copies.append(fetch(pairs, sems.at[q]))
    for q in range(4):
        for copy in copies[q]:
            copy.wait()
        begin, end = begin_of(q, phase - 1), region(phase - 1, q) - 1
        gather_chunks(table_ref, 4 * phase + q, outs[q], lambda i, s: space[begin + jnp.minimum(i, end)])


def before_lists(phase, table, boxes):
    flat = [box for part in boxes for box in part]
    return pl.pallas_call(
        functools.partial(before_kernel, phase),
        out_shape=tuple(chunks_of(room) for room in ROOM[phase]),
        in_specs=[SMEM] + [ANY] * len(flat),
        out_specs=(VMEM,) * 4,
        scratch_shapes=[
            pltpu.VMEM((begin_of(4, phase - 1), CHUNK, 256), jnp.bfloat16),
            pltpu.SemaphoreType.DMA((4, phase)),
        ],
        compiler_params=pltpu.CompilerParams(vmem_limit_bytes=28 * MIB),
        cost_estimate=cost(SMALL),
        name="before_lists",
    )(table, *flat)


def after_kernel(phase, table_ref, *rest):
    befores, boxes, outs = rest[:4], rest[4:8], rest[8:]
    for q in range(4):
        begin = region(phase - 1, q)

        def pick(i, s):
            return jnp.where(i < begin, befores[q][s], boxes[q][jnp.maximum(i - begin, 0)])

        gather_chunks(table_ref, 4 * phase + q, outs[q], pick)


def attend_row(query, first, second, own, length):
    scaling = 1.0 / math.sqrt(query.shape[1])
    upper = lax.broadcasted_iota(jnp.int32, query.shape, 0) < 8
    zero = jnp.zeros_like(query)
    wide = jnp.concatenate([jnp.where(upper, query, zero), jnp.where(upper, zero, query)], axis=1)
    keys = jnp.concatenate([first[:, :128], second[:, :128]], axis=1)
    values = jnp.concatenate([first[:, 128:], second[:, 128:]], axis=1)
    scores = (
        lax.dot_general(wide, keys, (((1,), (1,)), ((), ())), preferred_element_type=jnp.float32)
        * scaling
    )
    own = own.astype(jnp.float32)
    own_key = jnp.where(upper, own[0:1, :128], own[1:2, :128])
    own_value = jnp.where(upper, own[0:1, 128:], own[1:2, 128:])
    own_score = jnp.sum(query.astype(jnp.float32) * own_key, axis=1, keepdims=True) * scaling
    live = lax.broadcasted_iota(jnp.int32, scores.shape, 1) < length
    scores = jnp.where(live, scores, -jnp.inf)
    row_max = jnp.maximum(jnp.max(scores, axis=1, keepdims=True), own_score)
    weights = jnp.where(live, jnp.exp(scores - row_max), 0.0)
    own_weight = jnp.exp(own_score - row_max)
    denominator = jnp.sum(weights, axis=1, keepdims=True) + own_weight
    both = jnp.dot(weights.astype(jnp.bfloat16), values, preferred_element_type=jnp.float32)
    mixture = jnp.where(upper, both[:, :128], both[:, 128:])
    mixture += own_weight.astype(jnp.bfloat16).astype(jnp.float32) * own_value
    return mixture / denominator


def lay_rows(result, out_ref, first, rows):
    for row in range(0, rows, 16):
        for head in range(16):
            values = result[pl.ds(16 * row + head, 16, stride=16)]
            out_ref[first + row : first + row + 16, 128 * head : 128 * head + 128] = values.astype(jnp.bfloat16)


TOGETHER = 4
DEPTH = 4 * TOGETHER


def running_kernel(first, half_ref, pages_ref, lens_ref, query_ref, own_ref, pool_ref, out_ref, held, result, sems):
    rows = out_ref.shape[0]
    all_rows = lens_ref.shape[0] // 2
    max_pages = held.shape[1]
    start = half_ref[0] * all_rows + first

    def each_page(row, action):
        slot = row % DEPTH
        for c in range(max_pages):
            page = pages_ref[(start + row) * max_pages + c]
            action(pltpu.make_async_copy(pool_ref.at[page], held.at[slot, c], sems.at[slot, c]))

    def begin(group):
        for r in range(TOGETHER):
            each_page(group * TOGETHER + r, lambda copy: copy.start())

    ahead = DEPTH // TOGETHER - 1
    for group in range(ahead):
        begin(group)

    def body(group, carry):
        @pl.when(group + ahead < rows // TOGETHER)
        def _():
            begin(group + ahead)

        for r in range(TOGETHER):
            each_page(group * TOGETHER + r, lambda copy: copy.wait())
        results = []
        for r in range(TOGETHER):
            row = group * TOGETHER + r
            slot = row % DEPTH
            blocks = [held[slot, :, j].reshape(max_pages * 64, 256) for j in range(2)]
            results.append(
                attend_row(query_ref[first + row], *blocks, own_ref[first + row], lens_ref[start + row])
            )
        for r in range(TOGETHER):
            result[pl.ds((group * TOGETHER + r) * 16, 16)] = results[r]
        return carry

    lax.fori_loop(0, rows // TOGETHER, body, 0)
    lay_rows(result, out_ref, 0, rows)


def running_rows(first, count, half, pages, lens, queries, own, pool):
    max_pages = pages.shape[0] // lens.shape[0]
    return pl.pallas_call(
        functools.partial(running_kernel, first),
        out_shape=jax.ShapeDtypeStruct((count, 2048), jnp.bfloat16),
        in_specs=[SMEM, SMEM, SMEM, VMEM, VMEM, pl.BlockSpec(memory_space=pltpu.HBM)],
        out_specs=VMEM,
        scratch_shapes=[
            pltpu.VMEM((DEPTH, max_pages) + pool.shape[1:], jnp.bfloat16),
            pltpu.VMEM((count * 16, 128), jnp.float32),
            pltpu.SemaphoreType.DMA((DEPTH, max_pages)),
        ],
        compiler_params=pltpu.CompilerParams(vmem_limit_bytes=40 * MIB),
        cost_estimate=cost(SMALL),
        name="running_rows",
    )(half, pages, lens, queries, own, pool)


RING = 4


def early_kernel(land_ref, *rest):
    boxes, (landed_ref, block, sems, space, box_sems) = rest[:16], rest[16:]
    slots = landed_ref.shape[0]
    pairs = []
    for q in range(4):
        pairs += part_pairs(q, boxes[4 * q : 4 * q + 4], space, begin_of(q, 3))
    copies = fetch(pairs, box_sems)
    space[begin_of(4, 3)] = jnp.zeros((CHUNK, 256), jnp.bfloat16)
    for copy in copies:
        copy.wait()

    def write(slot):
        turn = slot % RING
        return pltpu.make_async_copy(block.at[turn], landed_ref.at[slot], sems.at[turn])

    def body(slot, carry):
        @pl.when(slot >= RING)
        def _():
            write(slot).wait()

        for j in range(2):
            for k in range(0, PROMPT_CHUNKS, 8):
                held = [space[land_ref[PROMPT_CHUNKS * j + k + b, slot]] for b in range(8)]
                for b in range(8):
                    block[slot % RING, j, k + b] = held[b]
        write(slot).start()
        return carry

    lax.fori_loop(0, slots, body, 0)
    for slot in range(slots - RING, slots):
        write(slot).wait()


def early_rows(slots, land, boxes):
    return pl.pallas_call(
        early_kernel,
        out_shape=jax.ShapeDtypeStruct((slots, 2, PROMPT_CHUNKS, CHUNK, 256), jnp.bfloat16),
        in_specs=[SMEM] + [ANY] * 16,
        out_specs=ANY,
        scratch_shapes=[
            pltpu.VMEM((RING, 2, PROMPT_CHUNKS, CHUNK, 256), jnp.bfloat16),
            pltpu.SemaphoreType.DMA((RING,)),
            pltpu.VMEM((begin_of(4, 3) + 1, CHUNK, 256), jnp.bfloat16),
            pltpu.SemaphoreType.DMA((16,)),
        ],
        compiler_params=pltpu.CompilerParams(vmem_limit_bytes=28 * MIB),
        cost_estimate=cost(SMALL),
        name="early_rows",
    )(land, *boxes)


def land_kernel(given, land_ref, query_ref, own_ref, early_ref, *rest):
    contexts, rest = rest[:given], rest[given:]
    boxes, rest = rest[:4], rest[4:]
    out_ref, landed_ref, even, odd, result, handed, sems, space, box_sems, out_sems = rest
    slots = landed_ref.shape[0]
    first = out_ref.shape[0] - slots
    copies = fetch([(box, space.at[pl.ds(LATE_BEGIN[q], box.shape[0])]) for q, box in enumerate(boxes)], box_sems)
    done = 0
    pairs = []
    for context in contexts:
        pairs.append((context, out_ref.at[pl.ds(done, context.shape[0])]))
        done += context.shape[0]
    decoded = fetch(pairs, out_sems)
    for copy in copies:
        copy.wait()

    def write(pair, block, turn):
        return pltpu.make_async_copy(block, landed_ref.at[pl.ds(2 * pair, 2)], sems.at[turn])

    def complete(pair, block):
        for r in range(2):
            slot = 2 * pair + r
            length = land_ref[LENGTH, slot]
            for j in range(2):
                for k in range(0, PROMPT_CHUNKS, 8):
                    held = []
                    for b in range(8):
                        source = land_ref[LATE + PROMPT_CHUNKS * j + k + b, slot]
                        before = early_ref[slot, j, k + b]
                        held.append(jnp.where(source >= 0, space[jnp.maximum(source, 0)], before))
                    for b in range(8):
                        block[r, j, k + b] = held[b]
            last = jnp.maximum(length - 1, 0) // CHUNK
            row = last * CHUNK + lax.broadcasted_iota(jnp.int32, (CHUNK, 256), 0)
            zero = jnp.zeros((CHUNK, 256), jnp.bfloat16)
            for j in range(2):
                block[r, j, last] = jnp.where(row < length, block[r, j, last], zero)

    def attend(pair, block):
        values = []
        for r in range(2):
            slot = 2 * pair + r
            blocks = [block[r, j].reshape(PROMPT_CHUNKS * CHUNK, 256) for j in range(2)]
            values.append(
                attend_row(query_ref[first + slot], *blocks, own_ref[first + slot], land_ref[LENGTH, slot])
            )
        for r in range(2):
            result[pl.ds(16 * (2 * pair + r), 16)] = values[r]

    last = slots // 2 - 1
    complete(0, even)
    write(0, even, 0).start()

    def body(step, carry):
        pair = 2 * step

        @pl.when(step > 0)
        def _():
            write(pair - 1, odd, 1).wait()

        attend(pair, even)
        complete(pair + 1, odd)
        write(pair + 1, odd, 1).start()
        write(pair, even, 0).wait()
        attend(pair + 1, odd)
        complete(pair + 2, even)
        write(pair + 2, even, 0).start()
        return carry

    lax.fori_loop(0, last // 2, body, 0)
    write(last - 2, odd, 1).wait()
    attend(last - 1, even)
    complete(last, odd)
    write(last, odd, 1).start()
    attend(last, odd)
    lay_rows(result, handed, 0, slots)
    final = pltpu.make_async_copy(handed, out_ref.at[pl.ds(first, slots)], out_sems.at[len(contexts)])
    final.start()
    write(last - 1, even, 0).wait()
    write(last, odd, 1).wait()
    for copy in decoded + [final]:
        copy.wait()


def land_rows(land, queries, own, early, contexts, boxes):
    return pl.pallas_call(
        functools.partial(land_kernel, len(contexts)),
        out_shape=(
            jax.ShapeDtypeStruct((queries.shape[0], 2048), jnp.bfloat16),
            jax.ShapeDtypeStruct(early.shape, jnp.bfloat16),
        ),
        in_specs=[SMEM, VMEM, VMEM, VMEM] + [VMEM] * len(contexts) + [ANY] * 4,
        out_specs=(pl.BlockSpec(memory_space=pltpu.HBM),) * 2,
        scratch_shapes=[
            pltpu.VMEM((2,) + early.shape[1:], jnp.bfloat16),
            pltpu.VMEM((2,) + early.shape[1:], jnp.bfloat16),
            pltpu.VMEM((16 * early.shape[0], 128), jnp.float32),
            pltpu.VMEM((early.shape[0], 2048), jnp.bfloat16),
            pltpu.SemaphoreType.DMA((2,)),
            pltpu.VMEM((LATE_BEGIN[4], CHUNK, 256), jnp.bfloat16),
            pltpu.SemaphoreType.DMA((4,)),
            pltpu.SemaphoreType.DMA((len(contexts) + 1,)),
        ],
        compiler_params=pltpu.CompilerParams(vmem_limit_bytes=24 * MIB),
        cost_estimate=cost(SMALL),
        name="land_rows",
    )(land, queries, own, early, *contexts, *boxes)


def routed(operands, kv, half, pages, lens, queries, own, pool):
    running = pages.shape[1]
    rows = queries.shape[0]
    pages, lens = pages.reshape(-1), lens.reshape(-1)
    other = hop(kv, CORE)
    (table,) = plan_call(first_plan_kernel, "first_plan", (8,), *operands)
    lists = lists_call(own_kernel, "own_lists", ROOM[0], table, kv)
    queries = queries.reshape(rows, 16, 128)
    lists, other, queries, pages, lens = lax.optimization_barrier((lists, other, queries, pages, lens))
    lists = lists_call(other_kernel, "first_lists", ROOM[0], table, other, *lists)
    sent = [hop(value, order[0]) for value, order in zip(lists, ORDERS)]
    (where, table), _ = lax.optimization_barrier(((operands[0], table), lists))
    kept = lists_call(functools.partial(home_kernel, 4), "kept_lists", KEPT, table, kv, other)
    table, land = plan_call(plan_kernel, "plan", (16, 72), where, *operands[1:])
    boxes = [[k] for k in kept]
    befores = before_lists(1, table, boxes)
    contexts = []
    done = 0
    for phase, count in ((1, running // 2), (2, running // 2), (3, 0)):
        table, sent, befores = lax.optimization_barrier((table, sent, befores))
        lists = lists_call(functools.partial(after_kernel, phase), "after_lists", ROOM[phase], table, *befores, *sent)
        boxes = [part + [box] for part, box in zip(boxes, sent)]
        sent = [hop(value, order[phase]) for value, order in zip(lists, ORDERS)]
        (ready, table, land), _ = lax.optimization_barrier(((half, table, land), lists))
        if count:
            contexts.append(running_rows(done, count, ready, pages, lens, queries, own, pool))
            done += count
        if phase < 3:
            befores = before_lists(phase + 1, table, boxes)
            table, _ = lax.optimization_barrier((table, contexts))
        else:
            early = early_rows(rows - running, land, [box for part in boxes for box in part])
            sent, _, early = lax.optimization_barrier((sent, contexts, early))
    context, landed = land_rows(land, queries, own, early, contexts, sent)
    return context, landed, land[OVER, 0]


def earlier_matches(labels, block_len, kind_count):
    onehot = (labels[:, None] == jnp.arange(kind_count, dtype=jnp.int32)[None, :]).astype(jnp.int32)
    blocks = onehot.reshape(labels.shape[0] // block_len, block_len, kind_count)
    before = jnp.cumsum(blocks, axis=1) - blocks
    return jnp.sum(before * blocks, axis=2).reshape(labels.shape[0])


def lookup(matches):
    prompt_ids = jnp.arange(matches.shape[1], dtype=jnp.int32)
    row_index = jnp.sum(jnp.where(matches, prompt_ids[None, :], 0), axis=1)
    return (row_index, jnp.any(matches, axis=1))


def pick_rows(table_rows, row_index, is_valid):
    picked = jnp.take(table_rows, row_index, axis=0)
    mask_shape = (is_valid.shape[0],) + (1,) * (picked.ndim - 1)
    return jnp.where(is_valid.reshape(mask_shape), picked, jnp.zeros_like(picked))


def any_fill(targets, prompt_lens, kv, queries, own):
    prompt_kv = kv.reshape(16, 1, 512, 256)
    groups = lax.axis_size("grp")
    group_id = lax.axis_index("grp")
    half_id = lax.axis_index("tp") % 2
    block_len = prompt_kv.shape[0]
    prompt_count = targets.shape[0]
    span_len = prompt_kv.shape[2]
    capacity = max(2, block_len // groups)
    source = jnp.arange(prompt_count, dtype=jnp.int32) // block_len
    arrival = earlier_matches(targets, prompt_count, 2 * groups)
    slot_ids = jnp.arange(block_len, dtype=jnp.int32)
    land_match = (targets[None, :] == 2 * group_id + half_id) & (
        arrival[None, :] == slot_ids[:, None]
    )
    land_len = jnp.sum(jnp.where(land_match, prompt_lens[None, :], 0), axis=1)
    land_live = jnp.arange(span_len, dtype=jnp.int32)[None, :] < land_len[:, None]
    land_index, land_valid = lookup(land_match)
    outgoing = source == group_id
    dest_ids = jnp.arange(groups, dtype=jnp.int32)
    cap_ids = jnp.arange(capacity, dtype=jnp.int32)
    partner = hop(prompt_kv, Z)
    pair_kv = jnp.where(
        half_id == 0,
        jnp.concatenate([prompt_kv, partner], axis=1),
        jnp.concatenate([partner, prompt_kv], axis=1),
    )
    within = earlier_matches(targets, block_len, 2 * groups)
    send_match = (
        outgoing[None, None, :]
        & (targets[None, None, :] == (2 * dest_ids + half_id)[:, None, None])
        & (within[None, None, :] == cap_ids[None, :, None])
    )
    send_index, send_valid = lookup(send_match.reshape(groups * capacity, prompt_count))
    send_index = jnp.where(send_valid, send_index - group_id * block_len, 0)
    outbox = pick_rows(pair_kv, send_index, send_valid)
    outbox = outbox.reshape((groups, capacity) + outbox.shape[1:])
    inbound = lax.all_to_all(outbox, "grp", split_axis=0, concat_axis=0, tiled=True)
    inbound = inbound.reshape((groups * capacity,) + inbound.shape[2:])
    entry_ids = source * capacity + within
    landed = pick_rows(inbound, jnp.take(entry_ids, land_index), land_valid)
    landed = jnp.where(land_live[:, None, :, None], landed, jnp.zeros_like(landed))
    handed = jnp.stack(
        [
            attend_row(queries[s], landed[s, 0], landed[s, 1], own[s], land_len[s])
            for s in range(block_len)
        ]
    )
    return handed, landed.reshape(block_len, 2, PROMPT_CHUNKS, CHUNK, 256)


def local(targets, prompt_lens, prompt_kv, cache_pool, block_table, cache_lens, queries, new_kv):
    group = lax.axis_index("grp")
    member = lax.axis_index("tp")
    kv = prompt_kv.reshape(OWN_CHUNKS, CHUNK, 256)
    operands = plan_operands(targets, prompt_lens, group, member)
    half = (member % 2).astype(jnp.int32).reshape(1)
    rows = queries.shape[2]
    running = block_table.shape[2]
    own = new_kv[0, 0]
    queries = queries[0, 0]
    context, landed, over = routed(
        operands, kv, half, block_table[0], cache_lens[0], queries, own, cache_pool[0, 0]
    )

    def again(carry):
        handed, landed = any_fill(targets, prompt_lens, kv, queries[running:].reshape(-1, 16, 128), own[running:])
        handed = handed.astype(jnp.bfloat16).reshape(rows - running, -1)
        return carry[0].at[running:].set(handed), landed, jnp.zeros((), jnp.int32)

    context, landed, _ = lax.while_loop(lambda carry: carry[2] > 0, again, (context, landed, over))
    return (
        context.reshape(1, 1, rows, -1),
        landed.reshape(1, 1, 16, 2, 512, 256),
    )


def solution(mesh):
    placed = (
        P(),
        P(),
        P("grp", "tp", None, None),
        P("grp", "tp", None, None, None, None),
        P("grp", None, None, None),
        P("grp", None, None),
        P("grp", "tp", None, None),
        P("grp", "tp", None, None, None),
    )
    return jax.shard_map(
        local,
        mesh=mesh,
        in_specs=placed,
        out_specs=(P("grp", "tp", None, None), P("grp", "tp", None, None, None, None)),
        check_vma=False,
    )
```

```python
import functools
import math

import jax
import jax.numpy as jnp
import numpy as np
from jax import lax
from jax.experimental import pallas as pl
from jax.experimental.pallas import tpu as pltpu
from jax.sharding import PartitionSpec as P

CHUNK = 32
PROMPT_CHUNKS = 16
OWN_CHUNKS = 256
HOME = 512
X, YA, YB, Z, CORE = 1, 2, 4, 8, 16
ORDERS = ((X, Z, YB, YA), (YA, YB, Z, X), (YB, YA, X, Z), (Z, X, YA, YB))
DEAL = (2, 0, 1, 3, 2, 0, 1, 2, 3, 0, 1, 2, 0, 1, 3, 2)
SHARES = tuple(sum(1 << k for k, part in enumerate(DEAL) if part == q) for q in range(4))
ROOM = ((38, 41, 47, 36), (44, 36, 50, 48), (64, 52, 47, 53), (72, 68, 63, 56))
MIB = 1024 * 1024
SMALL = 4096


KEPT = (52, 52, 64, 40)


def region(phase, part):
    return KEPT[part] + sum(rooms[part] for rooms in ROOM[:phase])


def begin_of(part, phase):
    return sum(region(phase, q) for q in range(part))


LATE_BEGIN = tuple(sum(ROOM[3][:q]) for q in range(5))


def flipped(group, mask):
    x, core, y = (group >> 1) & 1, group & 1, group >> 2
    if mask & X:
        x ^= 1
    if mask & YA:
        y ^= 1
    if mask & YB:
        y = 3 - y
    if mask & CORE:
        core ^= 1
    return (y << 2) | (x << 1) | core


def hop(value, axis):
    if axis == Z:
        return lax.ppermute(value, "tp", [(t, t ^ 1) for t in range(lax.axis_size("tp"))])
    return lax.ppermute(value, "grp", [(g, flipped(g, axis)) for g in range(lax.axis_size("grp"))])


def node_of(group, parity):
    y = group >> 2
    return (
        ((group >> 1) & 1)
        | (((y ^ (y >> 1)) & 1) << 1)
        | (((y >> 1) & 1) << 2)
        | (parity << 3)
        | ((group & 1) << 4)
    )


def bits_set(word):
    word = word - ((word >> 1) & 0x5555)
    word = (word & 0x3333) + ((word >> 2) & 0x3333)
    word = (word + (word >> 4)) & 0x0F0F
    return (word + (word >> 8)) & 0x1F


def turned(share, by):
    return ((share | (share << 16)) >> by) & 0xFFFF


def below(k):
    return (1 << k) - 1


def exact(values):
    return values.astype(jnp.float32).astype(jnp.bfloat16)


def dot(left, right):
    return jnp.dot(left, right, preferred_element_type=jnp.float32)


def standing(row):
    size = row.shape[1]
    down = lax.broadcasted_iota(jnp.int32, (size, size), 0)
    along = lax.broadcasted_iota(jnp.int32, (size, size), 1)
    return jnp.sum(jnp.where(down == along, row, 0), axis=1, keepdims=True)


def ends_of(targets, prompt, parity):
    start = node_of(prompt >> 4, parity)
    end = node_of(targets >> 1, targets & 1)
    start = (start & 15) | (end & CORE)
    return start, start ^ end


def earlier_rows(size):
    down = lax.broadcasted_iota(jnp.int32, (size, size), 0)
    along = lax.broadcasted_iota(jnp.int32, (size, size), 1)
    return exact(jnp.where(along < down, 1, 0))


SENT, RECEIVED, SLOTS, HELD = 0, 16, 32, 36


def first_plan_kernel(where_ref, targets_ref, lens_ref, table_ref):
    me, group = where_ref[0], where_ref[2]
    local = lax.broadcasted_iota(jnp.int32, (32, 1), 0)
    prompt = 16 * (group & ~1) + local
    match = lax.broadcasted_iota(jnp.int32, (32, targets_ref.shape[1]), 1) == prompt
    targets = jnp.sum(jnp.where(match, targets_ref[...], 0), axis=1, keepdims=True)
    lens = jnp.sum(jnp.where(match, lens_ref[...], 0), axis=1, keepdims=True)
    start, ways = ends_of(targets, prompt, (me >> 3) & 1)
    lane = lax.broadcasted_iota(jnp.int32, (1, 64), 1)
    bit = sum(jnp.where(lane == q, ORDERS[q][0], 0) for q in range(4))
    share = sum(jnp.where((lane == q) | (lane == HELD + q), SHARES[q], 0) for q in range(4))
    word = turned(share, (prompt * 5) & 15) & below((lens + (CHUNK - 1)) >> 5)
    goes = (lane < 4) & ((ways & bit) != 0) | (lane >= HELD) & (lane < HELD + 4)
    goes = goes & (start == me)
    place = dot(earlier_rows(32), exact(jnp.where(goes, bits_set(word), 0))).astype(jnp.int32)
    place = jnp.where(goes, place, -256)

    def each_chunk(values):
        wide = jnp.broadcast_to(values[:, None, :], (32, PROMPT_CHUNKS, values.shape[1]))
        return wide.reshape(32 * PROMPT_CHUNKS, values.shape[1])

    unit = lax.broadcasted_iota(jnp.int32, (HOME, 1), 0)
    k = unit & 15
    home = jnp.where(((unit >> 8) & 1) == (group & 1), 0, OWN_CHUNKS) + (unit & (OWN_CHUNKS - 1))
    words = each_chunk(word)
    spot = jnp.where(((words >> k) & 1) != 0, each_chunk(place) + bits_set(words & below(k)), -1)
    slot = lax.broadcasted_iota(jnp.int32, (1, 128), 1)
    rows = []
    for c in (0, 1, 2, 3, HELD, HELD + 1, HELD + 2, HELD + 3):
        rows.append(jnp.sum(jnp.where(spot[:, c : c + 1] == slot, home, 0), axis=0, keepdims=True))
    table_ref[...] = jnp.concatenate(rows, axis=0)


LATE, LENGTH, OVER = 32, 64, 65


def plan_kernel(where_ref, targets_ref, lens_ref, const_ref, slots_ref, land_ref):
    me, mine = where_ref[0], where_ref[1]
    row_t = jnp.concatenate([targets_ref[...], targets_ref[...]], axis=1)
    items = row_t.shape[1]
    prompts = items // 2
    col_t, col_l = standing(targets_ref[...]), standing(lens_ref[...])
    col_t, col_l = (jnp.concatenate([c, c], axis=0) for c in (col_t, col_l))
    item = lax.broadcasted_iota(jnp.int32, (items, 1), 0)
    prompt, parity = item & (prompts - 1), item >> 8
    start, ways = ends_of(col_t, prompt, parity)
    turn = (prompt * 5) & 15
    routed, bit, sender, share, room = (const_ref[k : k + 1, :] for k in range(5))
    lane = lax.broadcasted_iota(jnp.int32, (1, 64), 1)
    keeps = (lane >= HELD) & (lane < HELD + 4)
    weight = bits_set(turned(share, turn) & below((col_l + (CHUNK - 1)) >> 5))
    crosses = ((ways & bit) != 0) & (lane < SLOTS) | keeps
    listed = crosses & ((start ^ (ways & routed)) == (me ^ sender))
    landing = (col_t == mine) & (lane == SLOTS + parity)
    amount = jnp.where(listed, weight, jnp.where(landing, 1, 0))
    place = dot(earlier_rows(items), exact(amount)).astype(jnp.int32)

    everyone = exact(jnp.where(crosses, weight, 0))
    row_item = lax.broadcasted_iota(jnp.int32, (1, items), 1)
    row_start, row_ways = ends_of(row_t, row_item & (prompts - 1), row_item >> 8)
    nodes = lax.broadcasted_iota(jnp.int32, (32, 1), 0)
    ways_done = sorted({sum(order[:p]) for order in ORDERS for p in range(4)})
    present = [jnp.where(nodes == (row_start ^ (row_ways & done)), 1, 0) for done in ways_done]
    held = dot(exact(jnp.concatenate(present, axis=0)), everyone)
    need = jnp.zeros((1, 64), jnp.float32)
    for k, done in enumerate(ways_done):
        most = jnp.max(held[32 * k : 32 * k + 32], axis=0, keepdims=True)
        need = jnp.where(routed == done, most, need)
    over = (need.astype(jnp.int32) > room) & ((lane < RECEIVED) | keeps)
    over = jnp.max(jnp.where(over, 1, 0), axis=1, keepdims=True)

    bases = [[place[:, HELD + q : HELD + q + 1] for q in range(4)]]
    for p in range(4):
        came = []
        for q in range(4):
            c = RECEIVED + 4 * p + q
            moved = (ways & ORDERS[q][p]) != 0
            came.append(jnp.where(moved, region(p, q) + place[:, c : c + 1], bases[p][q]))
        bases.append(came)

    slot = lax.broadcasted_iota(jnp.int32, (1, 128), 1)

    def sources(p, q):
        c = 4 * p + q
        first = jnp.where(listed[:, c : c + 1], place[:, c : c + 1], 1 << 20)
        offset = slot - first
        inside = (offset >= 0) & (offset < weight[:, c : c + 1])
        found = jnp.where(inside, offset + bases[p][q], 0)
        return jnp.minimum(jnp.sum(found, axis=0, keepdims=True), region(p, q) - 1)

    slots_ref[...] = jnp.concatenate(
        [jnp.zeros((4, 128), jnp.int32)] + [sources(p, q) for p in range(1, 4) for q in range(4)], axis=0
    )

    rank = jnp.where(parity == 0, place[:, SLOTS : SLOTS + 1], place[:, SLOTS + 1 : SLOTS + 2])
    rank = jnp.where(col_t == mine, rank, -1)
    lands = [rank[:prompts] == slot, rank[prompts:] == slot]

    def landed(value, j):
        return jnp.sum(jnp.where(lands[j], value[j * prompts : (j + 1) * prompts], 0), axis=0, keepdims=True)

    length = landed(col_l, 0)
    live = (length + (CHUNK - 1)) >> 5
    by = landed(turn, 0)
    k = lax.broadcasted_iota(jnp.int32, (PROMPT_CHUNKS, 1), 0)
    early, late = [], []
    for j in range(2):
        here = jnp.zeros((PROMPT_CHUNKS, 128), jnp.int32)
        last = jnp.zeros((PROMPT_CHUNKS, 128), jnp.int32)
        for q in range(4):
            c = RECEIVED + 12 + q
            moves = landed(jnp.where((ways & ORDERS[q][3]) != 0, 1, 0), j)
            held = landed(bases[3][q], j)
            comes = landed(place[:, c : c + 1], j)
            part = turned(jnp.full_like(by, SHARES[q]), by)
            rest = bits_set(part & below(k))
            dealt = (part >> k) & 1
            spot = begin_of(q, 3) + jnp.minimum(held + rest, region(3, q) - 1)
            here += dealt * jnp.where(moves != 0, begin_of(4, 3), spot)
            spot = LATE_BEGIN[q] + jnp.minimum(comes + rest, ROOM[3][q] - 1)
            last += dealt * jnp.where(moves != 0, spot, -1)
        early.append(jnp.where(k < live, here, begin_of(4, 3)))
        late.append(jnp.where(k < live, last, -1))
    rows = [length, jnp.broadcast_to(over, (1, 128)), jnp.zeros((6, 128), jnp.int32)]
    land_ref[...] = jnp.concatenate(early + late + rows, axis=0)


def plan_const():
    const = np.zeros((8, 64), np.int32)
    for p in range(4):
        for q, order in enumerate(ORDERS):
            for first, sender in ((SENT, 0), (RECEIVED, order[p])):
                const[:5, first + 4 * p + q] = (sum(order[:p]), order[p], sender, SHARES[q], ROOM[p][q])
    for q in range(4):
        const[3:5, HELD + q] = (SHARES[q], KEPT[q])
    return jnp.asarray(const)


def plan_call(kernel, name, rows, *operands):
    vmem = pl.BlockSpec(memory_space=pltpu.VMEM)
    return pl.pallas_call(
        kernel,
        out_shape=tuple(jax.ShapeDtypeStruct((r, 128), jnp.int32) for r in rows),
        in_specs=[pl.BlockSpec(memory_space=pltpu.SMEM)] + [vmem] * (len(operands) - 1),
        out_specs=(vmem,) * len(rows),
        compiler_params=pltpu.CompilerParams(vmem_limit_bytes=12 * MIB),
        cost_estimate=cost(SMALL),
        name=name,
    )(*operands)


def plan_operands(targets, prompt_lens, group, member):
    where = jnp.stack([node_of(group, member % 2), 2 * group + member % 2, group]).astype(jnp.int32)
    return where, targets.reshape(1, -1), prompt_lens.reshape(1, -1), plan_const()


def fetch(pairs, sems):
    copies = [
        pltpu.make_async_copy(source, target, sems.at[k]) for k, (source, target) in enumerate(pairs)
    ]
    for copy in copies:
        copy.start()
    return copies


def gather_chunks(table_ref, row, out_ref, pick):
    def some(first, batch):
        held = [pick(table_ref[row, first + b], first + b) for b in range(batch)]
        for b in range(batch):
            out_ref[first + b] = held[b]

    def body(s, carry):
        some(8 * s, 8)
        return carry

    count = out_ref.shape[0]
    lax.fori_loop(0, count // 8, body, 0)
    if count % 8:
        some(count // 8 * 8, count % 8)


SMEM = pl.BlockSpec(memory_space=pltpu.SMEM)
ANY = pl.BlockSpec(memory_space=pl.ANY)
VMEM = pl.BlockSpec(memory_space=pltpu.VMEM)


def chunks_of(count):
    return jax.ShapeDtypeStruct((count, CHUNK, 256), jnp.bfloat16)


def cost(bytes_accessed, flops=0):
    return pl.CostEstimate(flops=flops, bytes_accessed=bytes_accessed, transcendentals=0)


def home_kernel(rows, table_ref, kv_ref, other_ref, *outs):
    def pick(i, s):
        row = i & (OWN_CHUNKS - 1)
        return jnp.where(i < OWN_CHUNKS, kv_ref[row], other_ref[row])

    for q in range(4):
        gather_chunks(table_ref, rows + q, outs[q], pick)


def own_kernel(table_ref, kv_ref, *outs):
    for q in range(4):
        gather_chunks(table_ref, q, outs[q], lambda i, s: kv_ref[i & (OWN_CHUNKS - 1)])


def other_kernel(table_ref, other_ref, *rest):
    befores, outs = rest[:4], rest[4:]
    for q in range(4):

        def pick(i, s):
            return jnp.where(i < OWN_CHUNKS, befores[q][s], other_ref[i & (OWN_CHUNKS - 1)])

        gather_chunks(table_ref, q, outs[q], pick)


def lists_call(kernel, name, rooms, table, *operands):
    return pl.pallas_call(
        kernel,
        out_shape=tuple(chunks_of(room) for room in rooms),
        in_specs=[SMEM] + [VMEM] * len(operands),
        out_specs=(VMEM,) * 4,
        compiler_params=pltpu.CompilerParams(vmem_limit_bytes=18 * MIB),
        cost_estimate=cost(SMALL),
        name=name,
    )(table, *operands)


def part_pairs(part, boxes, space, begin=0):
    pairs = []
    for k, box in enumerate(boxes):
        at = begin + (region(k - 1, part) if k else 0)
        pairs.append((box, space.at[pl.ds(at, box.shape[0])]))
    return pairs


def before_kernel(phase, table_ref, *rest):
    boxes, outs, space, sems = rest[: 4 * phase], rest[4 * phase : 4 * phase + 4], rest[4 * phase + 4], rest[4 * phase + 5]
    copies = []
    for q in range(4):
        pairs = part_pairs(q, boxes[phase * q : phase * q + phase], space, begin_of(q, phase - 1))
        copies.append(fetch(pairs, sems.at[q]))
    for q in range(4):
        for copy in copies[q]:
            copy.wait()
        begin, end = begin_of(q, phase - 1), region(phase - 1, q) - 1
        gather_chunks(table_ref, 4 * phase + q, outs[q], lambda i, s: space[begin + jnp.minimum(i, end)])


def before_lists(phase, table, boxes):
    flat = [box for part in boxes for box in part]
    return pl.pallas_call(
        functools.partial(before_kernel, phase),
        out_shape=tuple(chunks_of(room) for room in ROOM[phase]),
        in_specs=[SMEM] + [ANY] * len(flat),
        out_specs=(VMEM,) * 4,
        scratch_shapes=[
            pltpu.VMEM((begin_of(4, phase - 1), CHUNK, 256), jnp.bfloat16),
            pltpu.SemaphoreType.DMA((4, phase)),
        ],
        compiler_params=pltpu.CompilerParams(vmem_limit_bytes=28 * MIB),
        cost_estimate=cost(SMALL),
        name="before_lists",
    )(table, *flat)


def after_kernel(phase, table_ref, *rest):
    befores, boxes, outs = rest[:4], rest[4:8], rest[8:]
    for q in range(4):
        begin = region(phase - 1, q)

        def pick(i, s):
            return jnp.where(i < begin, befores[q][s], boxes[q][jnp.maximum(i - begin, 0)])

        gather_chunks(table_ref, 4 * phase + q, outs[q], pick)


def attend_row(query, first, second, own, length):
    scaling = 1.0 / math.sqrt(query.shape[1])
    upper = lax.broadcasted_iota(jnp.int32, query.shape, 0) < 8
    zero = jnp.zeros_like(query)
    wide = jnp.concatenate([jnp.where(upper, query, zero), jnp.where(upper, zero, query)], axis=1)
    keys = jnp.concatenate([first[:, :128], second[:, :128]], axis=1)
    values = jnp.concatenate([first[:, 128:], second[:, 128:]], axis=1)
    scores = (
        lax.dot_general(wide, keys, (((1,), (1,)), ((), ())), preferred_element_type=jnp.float32)
        * scaling
    )
    own = own.astype(jnp.float32)
    own_key = jnp.where(upper, own[0:1, :128], own[1:2, :128])
    own_value = jnp.where(upper, own[0:1, 128:], own[1:2, 128:])
    own_score = jnp.sum(query.astype(jnp.float32) * own_key, axis=1, keepdims=True) * scaling
    live = lax.broadcasted_iota(jnp.int32, scores.shape, 1) < length
    scores = jnp.where(live, scores, -jnp.inf)
    row_max = jnp.maximum(jnp.max(scores, axis=1, keepdims=True), own_score)
    weights = jnp.where(live, jnp.exp(scores - row_max), 0.0)
    own_weight = jnp.exp(own_score - row_max)
    denominator = jnp.sum(weights, axis=1, keepdims=True) + own_weight
    both = jnp.dot(weights.astype(jnp.bfloat16), values, preferred_element_type=jnp.float32)
    mixture = jnp.where(upper, both[:, :128], both[:, 128:])
    mixture += own_weight.astype(jnp.bfloat16).astype(jnp.float32) * own_value
    return mixture / denominator


def lay_rows(result, out_ref, first, rows):
    for row in range(0, rows, 16):
        for head in range(16):
            values = result[pl.ds(16 * row + head, 16, stride=16)]
            out_ref[first + row : first + row + 16, 128 * head : 128 * head + 128] = values.astype(jnp.bfloat16)


TOGETHER = 4
DEPTH = 4 * TOGETHER


def running_kernel(first, rows, given, half_ref, pages_ref, lens_ref, query_ref, own_ref, pool_ref, *rest):
    befores, outs, (held, result, sems) = rest[:given], rest[given:-3], rest[-3:]
    begin_row = 0
    for before in befores:
        result[0 : before.shape[0]] = before[...]
        begin_row = before.shape[0] // 16
    all_rows = lens_ref.shape[0] // 2
    max_pages = held.shape[1]
    start = half_ref[0] * all_rows + first

    def each_page(row, action):
        slot = row % DEPTH
        for c in range(max_pages):
            page = pages_ref[(start + row) * max_pages + c]
            action(pltpu.make_async_copy(pool_ref.at[page], held.at[slot, c], sems.at[slot, c]))

    def begin(group):
        for r in range(TOGETHER):
            each_page(group * TOGETHER + r, lambda copy: copy.start())

    ahead = DEPTH // TOGETHER - 1
    for group in range(ahead):
        begin(group)

    def body(group, carry):
        @pl.when(group + ahead < rows // TOGETHER)
        def _():
            begin(group + ahead)

        for r in range(TOGETHER):
            each_page(group * TOGETHER + r, lambda copy: copy.wait())
        results = []
        for r in range(TOGETHER):
            row = group * TOGETHER + r
            slot = row % DEPTH
            blocks = [held[slot, :, j].reshape(max_pages * 64, 256) for j in range(2)]
            results.append(
                attend_row(query_ref[first + row], *blocks, own_ref[first + row], lens_ref[start + row])
            )
        for r in range(TOGETHER):
            result[pl.ds((begin_row + group * TOGETHER + r) * 16, 16)] = results[r]
        return carry

    lax.fori_loop(0, rows // TOGETHER, body, 0)
    laid = outs[0].shape[0]
    lay_rows(result, outs[0], 0, laid)
    for rest_ref in outs[1:]:
        rest_ref[...] = result[16 * laid :]


def running_rows(first, count, befores, half, pages, lens, queries, own, pool):
    total = count + sum(b.shape[0] for b in befores) // 16
    left = total % 16
    shapes = [jax.ShapeDtypeStruct((total - left, 2048), jnp.bfloat16)]
    if left:
        shapes.append(jax.ShapeDtypeStruct((16 * left, 128), jnp.float32))
    max_pages = pages.shape[0] // lens.shape[0]
    return pl.pallas_call(
        functools.partial(running_kernel, first, count, len(befores)),
        out_shape=tuple(shapes),
        in_specs=[SMEM, SMEM, SMEM, VMEM, VMEM, ANY] + [VMEM] * len(befores),
        out_specs=(VMEM,) * len(shapes),
        scratch_shapes=[
            pltpu.VMEM((DEPTH, max_pages) + pool.shape[1:], jnp.bfloat16),
            pltpu.VMEM((total * 16, 128), jnp.float32),
            pltpu.SemaphoreType.DMA((DEPTH, max_pages)),
        ],
        compiler_params=pltpu.CompilerParams(vmem_limit_bytes=40 * MIB),
        cost_estimate=cost(SMALL),
        name="running_rows",
    )(half, pages, lens, queries, own, pool, *befores)


RING = 4


def early_kernel(land_ref, *rest):
    boxes, (landed_ref, block, sems, space, box_sems) = rest[:16], rest[16:]
    slots = landed_ref.shape[0]
    pairs = []
    for q in range(4):
        pairs += part_pairs(q, boxes[4 * q : 4 * q + 4], space, begin_of(q, 3))
    copies = fetch(pairs, box_sems)
    space[begin_of(4, 3)] = jnp.zeros((CHUNK, 256), jnp.bfloat16)
    for copy in copies:
        copy.wait()

    def write(slot):
        turn = slot % RING
        return pltpu.make_async_copy(block.at[turn], landed_ref.at[slot], sems.at[turn])

    def body(slot, carry):
        @pl.when(slot >= RING)
        def _():
            write(slot).wait()

        for j in range(2):
            for k in range(0, PROMPT_CHUNKS, 8):
                held = [space[land_ref[PROMPT_CHUNKS * j + k + b, slot]] for b in range(8)]
                for b in range(8):
                    block[slot % RING, j, k + b] = held[b]
        write(slot).start()
        return carry

    lax.fori_loop(0, slots, body, 0)
    for slot in range(slots - RING, slots):
        write(slot).wait()


def early_rows(slots, land, boxes):
    return pl.pallas_call(
        early_kernel,
        out_shape=jax.ShapeDtypeStruct((slots, 2, PROMPT_CHUNKS, CHUNK, 256), jnp.bfloat16),
        in_specs=[SMEM] + [ANY] * 16,
        out_specs=ANY,
        scratch_shapes=[
            pltpu.VMEM((RING, 2, PROMPT_CHUNKS, CHUNK, 256), jnp.bfloat16),
            pltpu.SemaphoreType.DMA((RING,)),
            pltpu.VMEM((begin_of(4, 3) + 1, CHUNK, 256), jnp.bfloat16),
            pltpu.SemaphoreType.DMA((16,)),
        ],
        compiler_params=pltpu.CompilerParams(vmem_limit_bytes=28 * MIB),
        cost_estimate=cost(SMALL),
        name="early_rows",
    )(land, *boxes)


def land_kernel(given, land_ref, query_ref, own_ref, early_ref, *rest):
    contexts, rest = rest[:given], rest[given:]
    boxes, rest = rest[:4], rest[4:]
    out_ref, landed_ref, even, odd, result, handed, sems, space, box_sems, out_sems = rest
    slots = landed_ref.shape[0]
    first = out_ref.shape[0] - slots
    copies = fetch([(box, space.at[pl.ds(LATE_BEGIN[q], box.shape[0])]) for q, box in enumerate(boxes)], box_sems)
    done = 0
    pairs = []
    for context in contexts:
        pairs.append((context, out_ref.at[pl.ds(done, context.shape[0])]))
        done += context.shape[0]
    decoded = fetch(pairs, out_sems)
    for copy in copies:
        copy.wait()

    def write(pair, block, turn):
        return pltpu.make_async_copy(block, landed_ref.at[pl.ds(2 * pair, 2)], sems.at[turn])

    def complete(pair, block):
        for r in range(2):
            slot = 2 * pair + r
            length = land_ref[LENGTH, slot]
            for j in range(2):
                for k in range(0, PROMPT_CHUNKS, 8):
                    held = []
                    for b in range(8):
                        source = land_ref[LATE + PROMPT_CHUNKS * j + k + b, slot]
                        before = early_ref[slot, j, k + b]
                        held.append(jnp.where(source >= 0, space[jnp.maximum(source, 0)], before))
                    for b in range(8):
                        block[r, j, k + b] = held[b]
            last = jnp.maximum(length - 1, 0) // CHUNK
            row = last * CHUNK + lax.broadcasted_iota(jnp.int32, (CHUNK, 256), 0)
            zero = jnp.zeros((CHUNK, 256), jnp.bfloat16)
            for j in range(2):
                block[r, j, last] = jnp.where(row < length, block[r, j, last], zero)

    def attend(pair, block):
        values = []
        for r in range(2):
            slot = 2 * pair + r
            blocks = [block[r, j].reshape(PROMPT_CHUNKS * CHUNK, 256) for j in range(2)]
            values.append(
                attend_row(query_ref[first + slot], *blocks, own_ref[first + slot], land_ref[LENGTH, slot])
            )
        for r in range(2):
            result[pl.ds(16 * (2 * pair + r), 16)] = values[r]

    last = slots // 2 - 1
    complete(0, even)
    write(0, even, 0).start()

    def body(step, carry):
        pair = 2 * step

        @pl.when(step > 0)
        def _():
            write(pair - 1, odd, 1).wait()

        attend(pair, even)
        complete(pair + 1, odd)
        write(pair + 1, odd, 1).start()
        write(pair, even, 0).wait()
        attend(pair + 1, odd)
        complete(pair + 2, even)
        write(pair + 2, even, 0).start()
        return carry

    lax.fori_loop(0, last // 2, body, 0)
    write(last - 2, odd, 1).wait()
    attend(last - 1, even)
    complete(last, odd)
    write(last, odd, 1).start()
    attend(last, odd)
    lay_rows(result, handed, 0, slots)
    final = pltpu.make_async_copy(handed, out_ref.at[pl.ds(first, slots)], out_sems.at[len(contexts)])
    final.start()
    write(last - 1, even, 0).wait()
    write(last, odd, 1).wait()
    for copy in decoded + [final]:
        copy.wait()


def land_rows(land, queries, own, early, contexts, boxes):
    return pl.pallas_call(
        functools.partial(land_kernel, len(contexts)),
        out_shape=(
            jax.ShapeDtypeStruct((queries.shape[0], 2048), jnp.bfloat16),
            jax.ShapeDtypeStruct(early.shape, jnp.bfloat16),
        ),
        in_specs=[SMEM, VMEM, VMEM, VMEM] + [VMEM] * len(contexts) + [ANY] * 4,
        out_specs=(pl.BlockSpec(memory_space=pltpu.HBM),) * 2,
        scratch_shapes=[
            pltpu.VMEM((2,) + early.shape[1:], jnp.bfloat16),
            pltpu.VMEM((2,) + early.shape[1:], jnp.bfloat16),
            pltpu.VMEM((16 * early.shape[0], 128), jnp.float32),
            pltpu.VMEM((early.shape[0], 2048), jnp.bfloat16),
            pltpu.SemaphoreType.DMA((2,)),
            pltpu.VMEM((LATE_BEGIN[4], CHUNK, 256), jnp.bfloat16),
            pltpu.SemaphoreType.DMA((4,)),
            pltpu.SemaphoreType.DMA((len(contexts) + 1,)),
        ],
        compiler_params=pltpu.CompilerParams(vmem_limit_bytes=24 * MIB),
        cost_estimate=cost(SMALL),
        name="land_rows",
    )(land, queries, own, early, *contexts, *boxes)


def routed(operands, kv, half, pages, lens, queries, own, pool):
    running = pages.shape[1]
    rows = queries.shape[0]
    pages, lens = pages.reshape(-1), lens.reshape(-1)
    other = hop(kv, CORE)
    (table,) = plan_call(first_plan_kernel, "first_plan", (8,), *operands[:3])
    lists = lists_call(own_kernel, "own_lists", ROOM[0], table, kv)
    queries = queries.reshape(rows, 16, 128)
    lists, other, queries, pages, lens = lax.optimization_barrier((lists, other, queries, pages, lens))
    lists = lists_call(other_kernel, "first_lists", ROOM[0], table, other, *lists)
    sent = [hop(value, order[0]) for value, order in zip(lists, ORDERS)]
    (where, table), _ = lax.optimization_barrier(((operands[0], table), lists))
    kept = lists_call(functools.partial(home_kernel, 4), "kept_lists", KEPT, table, kv, other)
    table, land = plan_call(plan_kernel, "plan", (16, 72), where, *operands[1:])
    boxes = [[k] for k in kept]
    befores = before_lists(1, table, boxes)
    contexts, left = [], []
    done = 0
    for phase, count in ((1, running * 3 // 8), (2, running * 5 // 8), (3, 0)):
        table, sent, befores = lax.optimization_barrier((table, sent, befores))
        lists = lists_call(functools.partial(after_kernel, phase), "after_lists", ROOM[phase], table, *befores, *sent)
        boxes = [part + [box] for part, box in zip(boxes, sent)]
        sent = [hop(value, order[phase]) for value, order in zip(lists, ORDERS)]
        (ready, table, land), _ = lax.optimization_barrier(((half, table, land), lists))
        if count:
            context, *left = running_rows(done, count, left, ready, pages, lens, queries, own, pool)
            contexts.append(context)
            done += count
        if phase < 3:
            befores = before_lists(phase + 1, table, boxes)
            table, _ = lax.optimization_barrier((table, contexts))
        else:
            early = early_rows(rows - running, land, [box for part in boxes for box in part])
            sent, _, early = lax.optimization_barrier((sent, contexts, early))
    context, landed = land_rows(land, queries, own, early, contexts, sent)
    return context, landed, land[OVER, 0]


def earlier_matches(labels, block_len, kind_count):
    onehot = (labels[:, None] == jnp.arange(kind_count, dtype=jnp.int32)[None, :]).astype(jnp.int32)
    blocks = onehot.reshape(labels.shape[0] // block_len, block_len, kind_count)
    before = jnp.cumsum(blocks, axis=1) - blocks
    return jnp.sum(before * blocks, axis=2).reshape(labels.shape[0])


def lookup(matches):
    prompt_ids = jnp.arange(matches.shape[1], dtype=jnp.int32)
    row_index = jnp.sum(jnp.where(matches, prompt_ids[None, :], 0), axis=1)
    return (row_index, jnp.any(matches, axis=1))


def pick_rows(table_rows, row_index, is_valid):
    picked = jnp.take(table_rows, row_index, axis=0)
    mask_shape = (is_valid.shape[0],) + (1,) * (picked.ndim - 1)
    return jnp.where(is_valid.reshape(mask_shape), picked, jnp.zeros_like(picked))


def any_fill(targets, prompt_lens, kv, queries, own):
    prompt_kv = kv.reshape(16, 1, 512, 256)
    groups = lax.axis_size("grp")
    group_id = lax.axis_index("grp")
    half_id = lax.axis_index("tp") % 2
    block_len = prompt_kv.shape[0]
    prompt_count = targets.shape[0]
    span_len = prompt_kv.shape[2]
    capacity = max(2, block_len // groups)
    source = jnp.arange(prompt_count, dtype=jnp.int32) // block_len
    arrival = earlier_matches(targets, prompt_count, 2 * groups)
    slot_ids = jnp.arange(block_len, dtype=jnp.int32)
    land_match = (targets[None, :] == 2 * group_id + half_id) & (
        arrival[None, :] == slot_ids[:, None]
    )
    land_len = jnp.sum(jnp.where(land_match, prompt_lens[None, :], 0), axis=1)
    land_live = jnp.arange(span_len, dtype=jnp.int32)[None, :] < land_len[:, None]
    land_index, land_valid = lookup(land_match)
    outgoing = source == group_id
    dest_ids = jnp.arange(groups, dtype=jnp.int32)
    cap_ids = jnp.arange(capacity, dtype=jnp.int32)
    partner = hop(prompt_kv, Z)
    pair_kv = jnp.where(
        half_id == 0,
        jnp.concatenate([prompt_kv, partner], axis=1),
        jnp.concatenate([partner, prompt_kv], axis=1),
    )
    within = earlier_matches(targets, block_len, 2 * groups)
    send_match = (
        outgoing[None, None, :]
        & (targets[None, None, :] == (2 * dest_ids + half_id)[:, None, None])
        & (within[None, None, :] == cap_ids[None, :, None])
    )
    send_index, send_valid = lookup(send_match.reshape(groups * capacity, prompt_count))
    send_index = jnp.where(send_valid, send_index - group_id * block_len, 0)
    outbox = pick_rows(pair_kv, send_index, send_valid)
    outbox = outbox.reshape((groups, capacity) + outbox.shape[1:])
    inbound = lax.all_to_all(outbox, "grp", split_axis=0, concat_axis=0, tiled=True)
    inbound = inbound.reshape((groups * capacity,) + inbound.shape[2:])
    entry_ids = source * capacity + within
    landed = pick_rows(inbound, jnp.take(entry_ids, land_index), land_valid)
    landed = jnp.where(land_live[:, None, :, None], landed, jnp.zeros_like(landed))
    handed = jnp.stack(
        [
            attend_row(queries[s], landed[s, 0], landed[s, 1], own[s], land_len[s])
            for s in range(block_len)
        ]
    )
    return handed, landed.reshape(block_len, 2, PROMPT_CHUNKS, CHUNK, 256)


def local(targets, prompt_lens, prompt_kv, cache_pool, block_table, cache_lens, queries, new_kv):
    group = lax.axis_index("grp")
    member = lax.axis_index("tp")
    kv = prompt_kv.reshape(OWN_CHUNKS, CHUNK, 256)
    operands = plan_operands(targets, prompt_lens, group, member)
    half = (member % 2).astype(jnp.int32).reshape(1)
    rows = queries.shape[2]
    running = block_table.shape[2]
    own = new_kv[0, 0]
    queries = queries[0, 0]
    context, landed, over = routed(
        operands, kv, half, block_table[0], cache_lens[0], queries, own, cache_pool[0, 0]
    )

    def again(carry):
        handed, landed = any_fill(targets, prompt_lens, kv, queries[running:].reshape(-1, 16, 128), own[running:])
        handed = handed.astype(jnp.bfloat16).reshape(rows - running, -1)
        return carry[0].at[running:].set(handed), landed, jnp.zeros((), jnp.int32)

    context, landed, _ = lax.while_loop(lambda carry: carry[2] > 0, again, (context, landed, over))
    return (
        context.reshape(1, 1, rows, -1),
        landed.reshape(1, 1, 16, 2, 512, 256),
    )


def solution(mesh):
    placed = (
        P(),
        P(),
        P("grp", "tp", None, None),
        P("grp", "tp", None, None, None, None),
        P("grp", None, None, None),
        P("grp", None, None),
        P("grp", "tp", None, None),
        P("grp", "tp", None, None, None),
    )
    return jax.shard_map(
        local,
        mesh=mesh,
        in_specs=placed,
        out_specs=(P("grp", "tp", None, None), P("grp", "tp", None, None, None, None)),
        check_vma=False,
    )
```
